32 devices in a mesh: slot: 4 (over y, x), mp: 4 (over z), dp: 2 (over core).
Axes of the slice: x: 2, y: 2, z: 4, core: 2. Of those that a mesh axis runs over, the one named last changes fastest.
Arguments:
- byte_ids: int32 [2, 4096, 8], P(None, 'dp'), may hold values from 0 to 255
- item_ids: int32 [2, 2, 2048], P(None, 'dp'), may hold values from 0 to 4, never falling along the last dimension, each value on 1 to 1024 neighbouring positions
- loss_mask: int32 [2, 4096, 8], P(None, 'dp'), may hold values from 0 to 1, as said below
- attend_in: float32 [1024, 3, 1024], P(('slot', 'dp'), None, 'mp'), may hold values from -0.1875 to 0.1875
- expand_in: float32 [1024, 4096], P(('slot', 'dp'), 'mp'), may hold values from -0.1875 to 0.1875
- attend_out: float32 [1024, 1024], P('mp', ('slot', 'dp')), may hold values from -0.75 to 0.75
- expand_out: float32 [4096, 1024], P('mp', ('slot', 'dp')), may hold values from -0.09375 to 0.09375
- slot_table: float32 [8, 256, 128], P('slot'), may hold values from -6 to 6
- local_pack: float32 [3475456], P(('slot', 'mp', 'dp')), as said below
- moment_attend_in: float32 [1024, 3, 1024], P(('slot', 'dp'), None, 'mp'), may hold values from -3.8146973e-05 to 3.8146973e-05
- moment_expand_in: float32 [1024, 4096], P(('slot', 'dp'), 'mp'), may hold values from -3.8146973e-05 to 3.8146973e-05
- moment_attend_out: float32 [1024, 1024], P('mp', ('slot', 'dp')), may hold values from -3.8146973e-05 to 3.8146973e-05
- moment_expand_out: float32 [4096, 1024], P('mp', ('slot', 'dp')), may hold values from -3.8146973e-05 to 3.8146973e-05
- moment_slot_table: float32 [8, 256, 128], P('slot'), may hold values from -3.8146973e-05 to 3.8146973e-05
- moment_local_pack: float32 [3475456], P(('slot', 'mp', 'dp')), may hold values from -3.8146973e-05 to 3.8146973e-05
- average_attend_in: float32 [1024, 3, 1024], P(('slot', 'dp'), None, 'mp'), may hold values from -0.1875 to 0.1875
- average_expand_in: float32 [1024, 4096], P(('slot', 'dp'), 'mp'), may hold values from -0.1875 to 0.1875
- average_attend_out: float32 [1024, 1024], P('mp', ('slot', 'dp')), may hold values from -0.75 to 0.75
- average_expand_out: float32 [4096, 1024], P('mp', ('slot', 'dp')), may hold values from -0.09375 to 0.09375
- average_slot_table: float32 [8, 256, 128], P('slot'), may hold values from -6 to 6
- average_local_pack: float32 [3475456], P(('slot', 'mp', 'dp')), as said below
Outputs:
- loss_sum: float32 [], replicated
- mask_count: float32 [], replicated
- clip_norm: float32 [], replicated
- next_attend_in: float32 [1024, 3, 1024], P(('slot', 'dp'), None, 'mp')
- next_moment_attend_in: float32 [1024, 3, 1024], P(('slot', 'dp'), None, 'mp')
- next_average_attend_in: float32 [1024, 3, 1024], P(('slot', 'dp'), None, 'mp')
- next_expand_in: float32 [1024, 4096], P(('slot', 'dp'), 'mp')
- next_moment_expand_in: float32 [1024, 4096], P(('slot', 'dp'), 'mp')
- next_average_expand_in: float32 [1024, 4096], P(('slot', 'dp'), 'mp')
- next_attend_out: float32 [1024, 1024], P('mp', ('slot', 'dp'))
- next_moment_attend_out: float32 [1024, 1024], P('mp', ('slot', 'dp'))
- next_average_attend_out: float32 [1024, 1024], P('mp', ('slot', 'dp'))
- next_expand_out: float32 [4096, 1024], P('mp', ('slot', 'dp'))
- next_moment_expand_out: float32 [4096, 1024], P('mp', ('slot', 'dp'))
- next_average_expand_out: float32 [4096, 1024], P('mp', ('slot', 'dp'))
- next_slot_table: float32 [8, 256, 128], P('slot')
- next_moment_slot_table: float32 [8, 256, 128], P('slot')
- next_average_slot_table: float32 [8, 256, 128], P('slot')
- next_local_pack: float32 [3475456], P(('slot', 'mp', 'dp'))
- next_moment_local_pack: float32 [3475456], P(('slot', 'mp', 'dp'))
- next_average_local_pack: float32 [3475456], P(('slot', 'mp', 'dp'))
The draws below stay inside these ranges and needn't reach their ends.
Inputs may be any that keep to these rules, and one draw needn't show every extreme that they name: local_pack holds the byte layer weights of fan-in scale and gains near 1, laid end to end as the steps list them. average_local_pack is laid out as local_pack. loss_mask holds 0 and 1 only.
All inputs are finite; a program needn't handle non-finite values.
Results may differ from the reference program's by a relative error of at most 0.012.
Values may be sent and summed in bfloat16 or wider, within the bound.
A program may use at most 256 MiB of HBM per device.

```python
import math
import jax
import jax.numpy as jnp
import numpy as np
from jax import lax

D = 1024
H = 16
FF = 4096
LD = 512
LH = 8
LFF = 2048
VOCAB = 256
SLOTS = 8
SEQ = 2048
MICRO = 2
ITEMS = 5
HEADDIM = 64
LHEADDIM = 64
GSLOT = 128
GROUPS = 2
PATCHES = 4096
LPARAMS = 3475456
PARAMS = 16320512


def local_pieces(base_key):
    layouts = ((LD * 3 * LD, LD ** (-0.5)), (LD * LFF, LD ** (-0.5)), (LD * LD, (LD // 4) ** (-0.5)), (LFF * LD, LFF ** (-0.5)), (LD * VOCAB, LD ** (-0.5)), (VOCAB * LD, 0.2), (GSLOT * LD, GSLOT ** (-0.5)))
    pieces = []
    for number, (length, spread) in enumerate(layouts):
        pieces.append(spread * jax.random.normal(jax.random.fold_in(base_key, number), (length,), jnp.float32))
    gains = 1.0 + 0.1 * jax.random.uniform(jax.random.fold_in(base_key, 50), (D + 2 * LD,), jnp.float32, -1.0, 1.0)
    return jnp.concatenate(pieces + [gains])


def draw_local_pack(key, part):
    return local_pieces(jax.random.fold_in(key, 1))


def draw_average_local_pack(key, part):
    return local_pieces(jax.random.fold_in(key, 2))


def draw_loss_mask(key, part):
    pack_index = jnp.arange(PATCHES, dtype=jnp.int32) // SEQ
    limit = 3 + 6 * pack_index // max(GROUPS - 1, 1)
    drawn = jax.random.randint(jax.random.fold_in(key, 3), (MICRO, PATCHES, SLOTS), 0, 10, jnp.int32)
    return (drawn < limit[None, :, None]).astype(jnp.int32)


def plant(entries, own_key, least, largest):
    longest = entries.shape.index(max(entries.shape))
    spots = []
    for shift in (0, 1):
        where = [jax.random.randint(jax.random.fold_in(own_key, axis), (), 0, length) for axis, length in enumerate(entries.shape)]
        where[longest] = (where[longest] + shift) % entries.shape[longest]
        spots.append(tuple(where))
    return entries.at[spots[0]].set(least).at[spots[1]].set(largest)


def steps_of(key, dims, split, least, high):
    level = 1.0
    for dim, shards_of in split:
        draws = jax.random.uniform(jax.random.fold_in(jax.random.fold_in(key, 6), dim), (shards_of,), jnp.float32, least / len(split), high / len(split))
        level = level * jnp.repeat(jnp.exp(draws), dims[dim] // shards_of).reshape((-1,) + (1,) * (len(dims) - 1 - dim))
    return level


def split_up(count, total, most, slope):
    loads = [(1 << 20) // math.isqrt(rank ** slope) + 1 for rank in range(2, count + 1)]
    rest, given = total - most - (count - 1), [1] * (count - 1)
    while rest > 0:
        free = [i for i in range(count - 1) if given[i] < most]
        pool, budget = sum([loads[i] for i in free]), rest
        for i in free:
            addition = min(most - given[i], max(1, budget * loads[i] // pool), rest)
            given[i] = given[i] + addition
            rest = rest - addition
    return np.array([most] + given)


def ragged_sizes(stream_key, amount, total, most, skew):
    if amount == 2:
        one = jax.random.randint(stream_key, (), max(1, total - most), min(most, total - 1) + 1)
        return jnp.stack([one, total - one])
    lengths = jnp.asarray(split_up(amount, total, most, skew), jnp.int32)
    pairs = (amount - 1) // 2
    giver, taker = lengths[1:1 + 2 * pairs:2], lengths[2:2 + 2 * pairs:2]
    room = jnp.minimum(giver - 1, most - taker)
    passed = jax.random.randint(jax.random.fold_in(stream_key, 1), (pairs,), 0, 1 << 20) % (room + 1)
    lengths = lengths.at[1:1 + 2 * pairs:2].set(giver - passed).at[2:2 + 2 * pairs:2].set(taker + passed)
    return lengths[jax.random.permutation(jax.random.fold_in(stream_key, 2), amount)]


def noise(key, shape, scale, bound, shards=(), kind=jnp.bfloat16):
    array = jax.random.normal(key, shape, jnp.float32) * scale
    if len(shards) > 0:
        array = steps_of(key, shape, shards, -0.22, 0.18) * array
    return jnp.clip(array, min=-bound, max=bound).astype(kind)


def setup_inputs(seed: int = 0) -> dict:
    keys = jax.random.split(jax.random.key(seed), 22)
    byte_ids = plant(jax.random.randint(keys[0], (MICRO, PATCHES, SLOTS), 0, VOCAB), jax.random.fold_in(keys[0], 1), 0, VOCAB - 1).astype(jnp.int32)
    item_ids = jax.vmap(lambda own: jnp.searchsorted(jnp.cumsum(ragged_sizes(own, ITEMS, SEQ, SEQ // 2, 2)), jnp.arange(SEQ), side="right"))(jax.random.split(keys[1], MICRO * GROUPS)).reshape((MICRO, GROUPS, SEQ)).astype(jnp.int32)
    loss_mask = draw_loss_mask(jax.random.fold_in(keys[21], 71), 0)
    attend_in = noise(keys[3], (D, 3, D), D ** -0.5, 0.1875, ((0, 8), (2, 4)), jnp.float32)
    expand_in = noise(keys[4], (D, FF), D ** -0.5, 0.1875, ((0, 8), (1, 4)), jnp.float32)
    attend_out = noise(keys[5], (D, D), (D // 16) ** -0.5, 0.75, ((0, 4), (1, 8)), jnp.float32)
    expand_out = noise(keys[6], (FF, D), FF ** -0.5, 0.09375, ((0, 4), (1, 8)), jnp.float32)
    slot_table = noise(keys[7], (SLOTS, VOCAB, GSLOT), 1.0, 6.0, ((0, 4),), jnp.float32)
    local_pack = draw_local_pack(jax.random.fold_in(keys[21], 71), 0)
    moment_attend_in = noise(keys[9], (D, 3, D), (0.01 * PARAMS ** -0.5), 3.814697265625e-05, ((0, 8), (2, 4)), jnp.float32)
    moment_expand_in = noise(keys[10], (D, FF), (0.01 * PARAMS ** -0.5), 3.814697265625e-05, ((0, 8), (1, 4)), jnp.float32)
    moment_attend_out = noise(keys[11], (D, D), (0.01 * PARAMS ** -0.5), 3.814697265625e-05, ((0, 4), (1, 8)), jnp.float32)
    moment_expand_out = noise(keys[12], (FF, D), (0.01 * PARAMS ** -0.5), 3.814697265625e-05, ((0, 4), (1, 8)), jnp.float32)
    moment_slot_table = noise(keys[13], (SLOTS, VOCAB, GSLOT), (0.01 * PARAMS ** -0.5), 3.814697265625e-05, ((0, 4),), jnp.float32)
    moment_local_pack = noise(keys[14], (LPARAMS,), (0.01 * PARAMS ** -0.5), 3.814697265625e-05, ((0, 32),), jnp.float32)
    average_attend_in = noise(keys[15], (D, 3, D), D ** -0.5, 0.1875, ((0, 8), (2, 4)), jnp.float32)
    average_expand_in = noise(keys[16], (D, FF), D ** -0.5, 0.1875, ((0, 8), (1, 4)), jnp.float32)
    average_attend_out = noise(keys[17], (D, D), (D // 16) ** -0.5, 0.75, ((0, 4), (1, 8)), jnp.float32)
    average_expand_out = noise(keys[18], (FF, D), FF ** -0.5, 0.09375, ((0, 4), (1, 8)), jnp.float32)
    average_slot_table = noise(keys[19], (SLOTS, VOCAB, GSLOT), 1.0, 6.0, ((0, 4),), jnp.float32)
    average_local_pack = draw_average_local_pack(jax.random.fold_in(keys[21], 71), 0)
    return {"byte_ids": byte_ids, "item_ids": item_ids, "loss_mask": loss_mask, "attend_in": attend_in, "expand_in": expand_in, "attend_out": attend_out, "expand_out": expand_out, "slot_table": slot_table, "local_pack": local_pack, "moment_attend_in": moment_attend_in, "moment_expand_in": moment_expand_in, "moment_attend_out": moment_attend_out, "moment_expand_out": moment_expand_out, "moment_slot_table": moment_slot_table, "moment_local_pack": moment_local_pack, "average_attend_in": average_attend_in, "average_expand_in": average_expand_in, "average_attend_out": average_attend_out, "average_expand_out": average_expand_out, "average_slot_table": average_slot_table, "average_local_pack": average_local_pack}


@jax.custom_vjp
def low(v):
    return lax.optimization_barrier(v.astype(jnp.bfloat16)).astype(jnp.float32)

@jax.custom_vjp
def low_back(v):
    return v

def low_keep(v):
    return (low(v), None)

def low_pass(kept, grad):
    return (grad,)

def back_keep(v):
    return (v, None)

def back_low(kept, grad):
    return (low(grad),)
low.defvjp(low_keep, low_pass)
low_back.defvjp(back_keep, back_low)
epsilon = 1e-06
clip_max = 0.01
momentum_keep = 0.9
average_keep = 0.9
rate_dense = 3000.0
rate_table = 60000.0
rate_project = 15000.0
masked_score = -1e+30
highest = lax.Precision.HIGHEST

def product_high(left, right):
    return jnp.dot(left, right, precision=highest, preferred_element_type=jnp.float32)

def rms_norm(values, gain):
    return values * lax.rsqrt(lax.optimization_barrier(jnp.mean(values * values, axis=-1, keepdims=True)) + epsilon) * gain

def gelu_tanh(values):
    return jax.nn.gelu(values, approximate=True)

def split_pack(packed):
    layouts = ((LD, 3 * LD), (LD, LFF), (LD, LD), (LFF, LD), (LD, VOCAB), (VOCAB, LD), (GSLOT, LD), (D + 2 * LD,))
    pieces = []
    offset = 0
    for layout in layouts:
        length = math.prod(layout)
        pieces.append(packed[offset:offset + length].reshape(layout))
        offset = offset + length
    return pieces

def global_attention(block):
    query, key_rows, value_rows, items = block
    scores = low_back(jnp.einsum('qhd,khd->hqk', query, key_rows, precision=highest) * HEADDIM ** (-0.5))
    positions = jnp.arange(SEQ)
    allowed = (items[:, None] == items[None, :]) & (positions[None, :] <= positions[:, None])
    scores = jnp.where(allowed[None], scores, masked_score)
    probs = low(jax.nn.softmax(scores, axis=-1))
    return jnp.einsum('hqk,khd->qhd', probs, value_rows, precision=highest)

def micro_loss(params, group_ids, group_items, group_mask, mask_count):
    attend_in, expand_in, attend_out, expand_out, slot_table, local_pack = [low(weight) for weight in params]
    local_in, local_up, local_out, local_down, head, embed, bridge, gains = split_pack(local_pack)
    gain_global = gains[:D]
    gain_local = gains[D:D + LD]
    gain_final = gains[D + LD:]
    previous = jnp.concatenate([jnp.zeros((1, SLOTS), jnp.int32), group_ids[:-1]], axis=0)
    flat_items = group_items.reshape(PATCHES)
    positions = jnp.arange(PATCHES) % SEQ
    earlier = jnp.concatenate([flat_items[:1], flat_items[:-1]])
    keep_rows = ((positions > 0) & (flat_items == earlier)).astype(jnp.float32)
    start_rows = slot_table[jnp.arange(SLOTS)[None, :], previous].reshape(PATCHES, D) * keep_rows[:, None]
    start_rows = low_back(start_rows)
    hidden = low(rms_norm(start_rows, gain_global))
    projected = low_back(low(product_high(hidden, attend_in.reshape(D, 3 * D))))

    def heads_of(block):
        return block.reshape(GROUPS, SEQ, H, HEADDIM)
    attended = lax.map(jax.checkpoint(global_attention), (heads_of(projected[:, :D]), heads_of(projected[:, D:2 * D]), heads_of(projected[:, 2 * D:]), group_items))
    attended = low_back(low(attended.reshape(PATCHES, D)))
    expanded = low_back(product_high(hidden, expand_in))
    active = low(gelu_tanh(expanded))
    middle = start_rows + low_back(product_high(attended, attend_out) + product_high(active, expand_out))
    inputs = low(middle).reshape(PATCHES * SLOTS, GSLOT)
    prev_byte = jnp.concatenate([jnp.zeros((PATCHES, 1), jnp.int32), group_ids[:, :-1]], axis=1).reshape(-1)
    leading = jnp.tile(jnp.arange(SLOTS) > 0, PATCHES).astype(jnp.float32)
    start_sum = low_back(product_high(inputs, bridge) + embed[prev_byte] * leading[:, None])
    hidden_local = low(rms_norm(start_sum, gain_local))
    lqkv = low_back(low(product_high(hidden_local, local_in)))

    def local_heads(block):
        return block.reshape(PATCHES, SLOTS, LH, LHEADDIM)
    lquery = local_heads(lqkv[:, :LD])
    lkey = local_heads(lqkv[:, LD:2 * LD])
    lvalue = local_heads(lqkv[:, 2 * LD:])
    lscores = low_back(jnp.einsum('pqhd,pkhd->phqk', lquery, lkey, precision=highest) * LHEADDIM ** (-0.5))
    causal = jnp.arange(SLOTS)[:, None] >= jnp.arange(SLOTS)[None, :]
    lscores = jnp.where(causal, lscores, masked_score)
    lprobs = low(jax.nn.softmax(lscores, axis=-1))
    lattended = low_back(low(jnp.einsum('phqk,pkhd->pqhd', lprobs, lvalue, precision=highest).reshape(-1, LD)))
    lexpanded = low_back(product_high(hidden_local, local_up))
    lactive = low(gelu_tanh(lexpanded))
    after = start_sum + low_back(product_high(lattended, local_out) + product_high(lactive, local_down))
    final = low(rms_norm(after, gain_final))
    logits = low_back(product_high(final, head))
    log_total = jax.nn.logsumexp(logits, axis=-1)
    picked = jnp.take_along_axis(logits, group_ids.reshape(-1, 1), axis=-1)[:, 0]
    return jnp.sum(group_mask.reshape(-1).astype(jnp.float32) * (log_total - picked)) / mask_count

def update(weight, moment, average, gradient, factor, rate):
    step_grad = factor * gradient
    moment_next = momentum_keep * moment + step_grad
    weight_next = weight - rate * (step_grad + momentum_keep * moment_next)
    average_next = average_keep * average + (1.0 - average_keep) * weight_next
    return (weight_next, moment_next, average_next)

def reference(byte_ids, item_ids, loss_mask, attend_in, expand_in, attend_out, expand_out, slot_table, local_pack, moment_attend_in, moment_expand_in, moment_attend_out, moment_expand_out, moment_slot_table, moment_local_pack, average_attend_in, average_expand_in, average_attend_out, average_expand_out, average_slot_table, average_local_pack):
    weights = (attend_in, expand_in, attend_out, expand_out, slot_table, local_pack)
    mask_count = jnp.sum(loss_mask.astype(jnp.float32))

    def total(params):
        loss = 0.0
        for micro_index in range(MICRO):
            loss = loss + micro_loss(params, byte_ids[micro_index], item_ids[micro_index], loss_mask[micro_index], mask_count)
        return loss
    loss_value, pull = jax.vjp(total, weights)
    grads = pull(jnp.ones_like(loss_value))[0]
    squares = 0.0
    for gradient in grads:
        squares = squares + jnp.sum(gradient * gradient)
    clip_norm = jnp.sqrt(squares)
    factor = clip_max / jnp.maximum(clip_norm, clip_max)
    in_next = update(attend_in, moment_attend_in, average_attend_in, grads[0], factor, rate_dense)
    up_next = update(expand_in, moment_expand_in, average_expand_in, grads[1], factor, rate_dense)
    out_next = update(attend_out, moment_attend_out, average_attend_out, grads[2], factor, rate_project)
    down_next = update(expand_out, moment_expand_out, average_expand_out, grads[3], factor, rate_dense)
    table_next = update(slot_table, moment_slot_table, average_slot_table, grads[4], factor, rate_table)
    pack_next = update(local_pack, moment_local_pack, average_local_pack, grads[5], factor, rate_dense)
    return (loss_value * mask_count, mask_count, clip_norm, in_next[0], in_next[1], in_next[2], up_next[0], up_next[1], up_next[2], out_next[0], out_next[1], out_next[2], down_next[0], down_next[1], down_next[2], table_next[0], table_next[1], table_next[2], pack_next[0], pack_next[1], pack_next[2])
```

```python
import functools

import jax
import jax.numpy as jnp
from jax import lax
from jax.experimental import pallas as pl
from jax.experimental.pallas import tpu as pltpu
from jax.sharding import PartitionSpec as P

D = 1024
LD = 512
LH = 8
LFF = 2048
VOCAB = 256
SLOTS = 8
HEADDIM = 64
LHEADDIM = 64
GSLOT = 128
BLK = 256
F32 = jnp.float32
BF16 = jnp.bfloat16
MESH = pl.DeviceIdType.MESH

longest_item = 1024


epsilon = 1e-06
clip_max = 0.01
momentum_keep = 0.9
average_keep = 0.9
rate_dense = 3000.0
rate_table = 60000.0
rate_project = 15000.0
masked_score = -1e30


def product(left, right):
    return jnp.dot(left, right, preferred_element_type=jnp.float32)


def gram_product(left, right):
    return lax.dot_general(
        left, right, (((0,), (0,)), ((), ())), preferred_element_type=jnp.float32
    )


def back_product(left, right):
    return lax.dot_general(
        left, right, (((1,), (1,)), ((), ())), preferred_element_type=jnp.float32
    )


def gelu_tanh(values):
    return jax.nn.gelu(values, approximate=True)


def gelu_back(values, gradient):
    return jax.vjp(gelu_tanh, values)[1](gradient)[0]


def norm_forward(values, gain):
    factor = lax.rsqrt(jnp.mean(values * values, axis=-1, keepdims=True) + epsilon)
    scaled = values * factor
    return (scaled * gain, scaled, factor)


def norm_backward(scaled, factor, gain, gradient):
    inner = gradient * gain
    return factor * (inner - scaled * jnp.mean(inner * scaled, axis=-1, keepdims=True))


def split_pack(packed):
    layouts = (
        (LD, 3 * LD),
        (LD, LFF),
        (LD, LD),
        (LFF, LD),
        (LD, VOCAB),
        (VOCAB, LD),
        (GSLOT, LD),
        (D + 2 * LD,),
    )
    pieces = []
    offset = 0
    for layout in layouts:
        length = 1
        for extent in layout:
            length = length * extent
        pieces.append(packed[offset : offset + length].reshape(layout))
        offset = offset + length
    return pieces


def mm(a, b):
    return lax.dot_general(a, b, (((1,), (0,)), ((), ())), preferred_element_type=F32)


def mm_tn(a, b):
    return lax.dot_general(a, b, (((0,), (0,)), ((), ())), preferred_element_type=F32)


def mm_nt(a, b):
    return lax.dot_general(a, b, (((1,), (1,)), ((), ())), preferred_element_type=F32)


def stack_heads(x):
    lane = lax.broadcasted_iota(jnp.int32, x.shape, 1)
    zero = jnp.zeros_like(x)
    return jnp.concatenate([jnp.where(lane < 64, x, zero), jnp.where(lane < 64, zero, x)], axis=0)


def window_fill(rows, width, own_ref, earlier, keys, values_t, values, keys_t):
    for place, ref in enumerate(earlier):
        at = (len(earlier) - 1 - place) * rows
        if keys is not None:
            keys[at : at + rows, :] = ref[:, :width]
        if values is not None:
            values[at : at + rows, :] = ref[:, width:]
        if values_t is not None:
            values_t[:, at : at + rows] = jnp.transpose(ref[:, width:])
        if keys_t is not None:
            keys_t[:, at : at + rows] = jnp.transpose(ref[:, :width])
    at = len(earlier) * rows
    if keys is not None:
        keys[at : at + rows, :] = own_ref[:, width : 2 * width]
    if values is not None:
        values[at : at + rows, :] = own_ref[:, 2 * width :]
    if values_t is not None:
        values_t[:, at : at + rows] = jnp.transpose(own_ref[:, 2 * width :])
    if keys_t is not None:
        keys_t[:, at : at + rows] = jnp.transpose(own_ref[:, width : 2 * width])


def fwd_kernel(rows, width, count, low_ref, start_ref, own_ref, *rest):
    earlier, (att_ref, lse_ref, keys, values_t) = rest[:count], rest[count:]
    window_fill(rows, width, own_ref, earlier, keys, values_t, None, None)
    base = count * rows
    key_iota = lax.broadcasted_iota(jnp.int32, (BLK, 2 * BLK), 0)
    q_iota = lax.broadcasted_iota(jnp.int32, (1, 2 * BLK), 1) % BLK
    pairs = width // 128
    for qt in range(rows // BLK):
        q_pos = q_iota + (base + qt * BLK)
        start = start_ref[qt]
        start = jnp.concatenate([start, start], axis=1)
        for pair in range(pairs):
            cs = slice(pair * 128, pair * 128 + 128)
            qs = stack_heads(own_ref[qt * BLK : (qt + 1) * BLK, cs] * jnp.asarray(0.125, BF16))

            def block(i, carry):
                top, total, acc = carry
                kb = base // BLK + qt - i
                at = pl.ds(pl.multiple_of(kb * BLK, BLK), BLK)
                s = mm_nt(keys[at, cs], qs)
                pos = key_iota + kb * BLK
                s = jnp.where((pos >= start) & (pos <= q_pos), s, masked_score)
                new = jnp.maximum(top, jnp.max(s, axis=0, keepdims=True))
                p = jnp.exp(s - new)
                alpha = jnp.exp(top - new)
                total = total * alpha + jnp.sum(p, axis=0, keepdims=True)
                acc = acc * alpha + mm(values_t[cs, at], p.astype(BF16))
                return new, total, acc

            init = (
                jnp.full((1, 2 * BLK), masked_score, F32),
                jnp.zeros((1, 2 * BLK), F32),
                jnp.zeros((128, 2 * BLK), F32),
            )
            top, total, acc = lax.fori_loop(0, base // BLK + qt + 1 - low_ref[qt], block, init)
            acc = acc * (1.0 / total)
            sub = lax.broadcasted_iota(jnp.int32, (128, BLK), 0)
            both = jnp.where(sub < 64, acc[:, :BLK], acc[:, BLK:])
            att_ref[qt * BLK : (qt + 1) * BLK, cs] = jnp.transpose(both).astype(BF16)
            lse_ref[qt * pairs + pair] = top + jnp.log(total)


def bwd_kernel(rows, width, count, low_ref, start_ref, own_ref, *rest):
    earlier = rest[:count]
    att_ref, attg_ref, lse_ref = rest[count : count + 3]
    dq_ref, dkv_refs = rest[count + 3], rest[count + 4 : 2 * count + 5]
    keys, values, keys_t, dkeys, dvalues = rest[2 * count + 5 :]
    window_fill(rows, width, own_ref, earlier, keys, None, values, keys_t)
    base = count * rows
    dkeys[...] = jnp.zeros_like(dkeys)
    dvalues[...] = jnp.zeros_like(dvalues)
    key_iota = lax.broadcasted_iota(jnp.int32, (BLK, 2 * BLK), 0)
    q_iota = lax.broadcasted_iota(jnp.int32, (1, 2 * BLK), 1) % BLK
    pairs = width // 128
    for qt in range(rows // BLK):
        q_pos = q_iota + (base + qt * BLK)
        start = start_ref[qt]
        start = jnp.concatenate([start, start], axis=1)
        rq = slice(qt * BLK, (qt + 1) * BLK)
        for pair in range(pairs):
            cs = slice(pair * 128, pair * 128 + 128)
            qs = stack_heads(own_ref[rq, cs] * jnp.asarray(0.125, BF16))
            das = stack_heads(attg_ref[rq, cs])
            att = att_ref[rq, cs]
            both = jnp.concatenate([att, att], axis=0).astype(F32) * das.astype(F32)
            delta = jnp.sum(jnp.transpose(both), axis=0, keepdims=True)
            lse = lse_ref[qt * pairs + pair]

            def block(i, acc):
                kb = base // BLK + qt - i
                at = pl.ds(pl.multiple_of(kb * BLK, BLK), BLK)
                s = mm_nt(keys[at, cs], qs)
                pos = key_iota + kb * BLK
                p = jnp.where((pos >= start) & (pos <= q_pos), jnp.exp(s - lse), 0.0)
                dp = mm_nt(values[at, cs], das)
                ds = (p * (dp - delta)).astype(BF16)
                dkeys[at, cs] += mm(ds, qs)
                dvalues[at, cs] += mm(p.astype(BF16), das)
                return acc + mm(keys_t[cs, at], ds)

            acc = lax.fori_loop(
                0, base // BLK + qt + 1 - low_ref[qt], block, jnp.zeros((128, 2 * BLK), F32)
            )
            sub = lax.broadcasted_iota(jnp.int32, (128, BLK), 0)
            both = jnp.where(sub < 64, acc[:, :BLK], acc[:, BLK:]) * 0.125
            dq_ref[rq, cs] = jnp.transpose(both).astype(BF16)
    for place in range(count + 1):
        at = (count - place) * rows
        dkv_refs[place][:, :width] = dkeys[at : at + rows, :].astype(BF16)
        dkv_refs[place][:, width:] = dvalues[at : at + rows, :].astype(BF16)


def specs(n):
    return [pl.BlockSpec(memory_space=pltpu.SMEM)] + [pl.BlockSpec(memory_space=pltpu.VMEM)] * n


def attention_fwd(low, start, own, earlier):
    rows, width = own.shape[0], own.shape[1] // 3
    count = len(earlier)
    span = (count + 1) * rows
    units = rows // BLK * (width // 128)
    return pl.pallas_call(
        functools.partial(fwd_kernel, rows, width, count),
        out_shape=[
            jax.ShapeDtypeStruct((rows, width), BF16),
            jax.ShapeDtypeStruct((units, 1, 2 * BLK), F32),
        ],
        in_specs=specs(2 + count),
        out_specs=[pl.BlockSpec(memory_space=pltpu.VMEM)] * 2,
        scratch_shapes=[pltpu.VMEM((span, width), BF16), pltpu.VMEM((width, span), BF16)],
        compiler_params=pltpu.CompilerParams(vmem_limit_bytes=32 * 2**20),
        name="patch_attention",
    )(low, start, own, *earlier)


def attention_bwd(low, start, own, earlier, attended, attended_grad, lse):
    rows, width = own.shape[0], own.shape[1] // 3
    count = len(earlier)
    span = (count + 1) * rows
    out = pl.pallas_call(
        functools.partial(bwd_kernel, rows, width, count),
        out_shape=[jax.ShapeDtypeStruct((rows, width), BF16)]
        + [jax.ShapeDtypeStruct((rows, 2 * width), BF16)] * (count + 1),
        in_specs=specs(5 + count),
        out_specs=[pl.BlockSpec(memory_space=pltpu.VMEM)] * (count + 2),
        scratch_shapes=[
            pltpu.VMEM((span, width), BF16),
            pltpu.VMEM((span, width), BF16),
            pltpu.VMEM((width, span), BF16),
            pltpu.VMEM((span, width), F32),
            pltpu.VMEM((span, width), F32),
        ],
        compiler_params=pltpu.CompilerParams(vmem_limit_bytes=32 * 2**20),
        name="patch_attention_back",
    )(low, start, own, *earlier, attended, attended_grad, lse)
    return out[0], out[1:]


def gelu_pair(x):
    c = 0.7978845608028654
    x2 = x * x
    t = jnp.tanh(c * (x + 0.044715 * (x2 * x)))
    half = 0.5 * (1.0 + t)
    slope = half + (0.5 * c) * x * (1.0 - t * t) * (1.0 + (3 * 0.044715) * x2)
    return x * half, slope


def byte_kernel(
    rows, tile, with_base,
    inputs_ref, ids_ref, weight_ref, w_in, w_up, w_out, w_down, w_head, w_embed, w_bridge, gains_ref,
    *rest,
):
    if with_base:
        base, rest = rest[:9], rest[9:]
    else:
        base = None
    (g_in, g_up, g_out, g_down, g_head, g_embed, g_bridge, g_gain, loss_ref, inputg_ref,
     hid, proj, probs, att, act, slope, fin, lgrad, bgrad, egrad, attg, projg, sgrad, startv) = rest
    steps = rows // tile
    blocks = tile // 128
    g_gain_local = gains_ref[0:1, :]
    g_gain_final = gains_ref[1:2, :]
    lane = lax.broadcasted_iota(jnp.int32, (128, 128), 1)
    first = (lane < 64)
    r_i = lax.broadcasted_iota(jnp.int32, (256, 128), 0) % 128
    c_i = lax.broadcasted_iota(jnp.int32, (256, 128), 1)
    allowed = (r_i // SLOTS == c_i // SLOTS) & (c_i <= r_i)
    vocab_ids = lax.broadcasted_iota(jnp.int32, (tile, VOCAB), 1)
    zero_low = jnp.zeros((128, 128), BF16)

    def stack(x):
        return jnp.concatenate([jnp.where(first, x, zero_low), jnp.where(first, zero_low, x)], axis=0)

    def norm(v):
        factor = lax.rsqrt(jnp.mean(v * v, axis=-1, keepdims=True) + epsilon)
        return v * factor, factor

    def step(t, carry):
        loss, gl, gf = carry
        at = pl.ds(pl.multiple_of(t * tile, tile), tile)
        inputs = inputs_ref[at, :]
        prev = ids_ref[at, 0:1]
        own = ids_ref[at, 1:2]
        weighting = weight_ref[at, :]
        lookup = jnp.where(prev == vocab_ids, 1.0, 0.0).astype(BF16)
        start = mm(inputs, w_bridge[...]) + mm(lookup, w_embed[...])
        startv[...] = start
        scaled, factor = norm(start)
        hidden = (scaled * g_gain_local).astype(BF16)
        hid[at, :] = hidden
        for c in range(3):
            proj[:, c * LD : (c + 1) * LD] = mm(hidden, w_in[:, c * LD : (c + 1) * LD]).astype(BF16)

        def attend(b, _):
            ra = pl.ds(pl.multiple_of(b * 128, 128), 128)
            for pair in range(4):
                cs = slice(pair * 128, pair * 128 + 128)
                qs = stack(proj[ra, cs] * jnp.asarray(0.125, BF16))
                kp = proj[ra, LD + pair * 128 : LD + pair * 128 + 128]
                vp = proj[ra, 2 * LD + pair * 128 : 2 * LD + pair * 128 + 128]
                s = jnp.where(allowed, mm_nt(qs, kp), masked_score)
                e = jnp.exp(s - jnp.max(s, axis=-1, keepdims=True))
                p = e * (1.0 / jnp.sum(e, axis=-1, keepdims=True))
                probs[b * 4 + pair] = p
                pl_ = p.astype(BF16)
                wide = jnp.concatenate([pl_[:128], pl_[128:]], axis=1)
                att[pl.ds(pl.multiple_of(t * tile + b * 128, 128), 128), cs] = mm(wide, stack(vp)).astype(BF16)
            return 0

        lax.fori_loop(0, blocks, attend, 0)
        attended = att[at, :]
        after = start + mm(attended, w_out[...])
        for c in range(4):
            cs = slice(c * 512, c * 512 + 512)
            a, s = gelu_pair(mm(hidden, w_up[:, cs]))
            a = a.astype(BF16)
            act[at, cs] = a
            slope[:, cs] = s
            after = after + mm(a, w_down[cs, :])
        scaled_f, factor_f = norm(after)
        final = (scaled_f * g_gain_final).astype(BF16)
        fin[at, :] = final
        logits = mm(final, w_head[...])
        hot = jnp.where(own == vocab_ids, 1.0, 0.0)
        top = jnp.max(logits, axis=-1, keepdims=True)
        log_total = top + jnp.log(jnp.sum(jnp.exp(logits - top), axis=-1, keepdims=True))
        loss = loss + jnp.sum(
            weighting * (log_total - jnp.sum(logits * hot, axis=-1, keepdims=True)), axis=0, keepdims=True
        )
        lg = ((jnp.exp(logits - log_total) - hot) * weighting).astype(BF16)
        lgrad[at, :] = lg
        fg = mm_nt(lg, w_head[...])
        gf = gf + jnp.sum(fg * scaled_f, axis=0, keepdims=True)
        inner = fg * g_gain_final
        after_grad = factor_f * (inner - scaled_f * jnp.mean(inner * scaled_f, axis=-1, keepdims=True))
        bg = after_grad.astype(BF16)
        bgrad[at, :] = bg
        attg[...] = mm_nt(bg, w_out[...]).astype(BF16)
        hg = None
        for c in range(4):
            cs = slice(c * 512, c * 512 + 512)
            eg = (slope[:, cs] * mm_nt(bg, w_down[cs, :])).astype(BF16)
            egrad[at, cs] = eg
            term = mm_nt(eg, w_up[:, cs])
            hg = term if hg is None else hg + term

        def attend_back(b, _):
            ra = pl.ds(pl.multiple_of(b * 128, 128), 128)
            rg = pl.ds(pl.multiple_of(t * tile + b * 128, 128), 128)
            for pair in range(4):
                cs = slice(pair * 128, pair * 128 + 128)
                qs = stack(proj[ra, cs] * jnp.asarray(0.125, BF16))
                kp = proj[ra, LD + pair * 128 : LD + pair * 128 + 128]
                vp = proj[ra, 2 * LD + pair * 128 : 2 * LD + pair * 128 + 128]
                das = stack(attg[ra, cs])
                p = probs[b * 4 + pair]
                dp = mm_nt(das, vp)
                ds = (p * (dp - jnp.sum(p * dp, axis=-1, keepdims=True))).astype(BF16)
                wide = jnp.concatenate([ds[:128], ds[128:]], axis=1)
                projg[rg, cs] = (mm(wide, stack(kp)) * 0.125).astype(BF16)
                projg[rg, LD + pair * 128 : LD + pair * 128 + 128] = mm_tn(ds, qs).astype(BF16)
                projg[rg, 2 * LD + pair * 128 : 2 * LD + pair * 128 + 128] = mm_tn(p.astype(BF16), das).astype(BF16)
            return 0

        lax.fori_loop(0, blocks, attend_back, 0)
        for c in range(3):
            hg = hg + mm_nt(projg[at, c * LD : (c + 1) * LD], w_in[:, c * LD : (c + 1) * LD])
        start = startv[...]
        scaled, factor = norm(start)
        gl = gl + jnp.sum(hg * scaled, axis=0, keepdims=True)
        inner = hg * g_gain_local
        sg = (after_grad + factor * (inner - scaled * jnp.mean(inner * scaled, axis=-1, keepdims=True))).astype(BF16)
        sgrad[at, :] = sg
        inputg_ref[at, :] = mm_nt(sg, w_bridge[...]).astype(BF16)
        return loss, gl, gf

    init = (jnp.zeros((1, 1), F32), jnp.zeros((1, LD), F32), jnp.zeros((1, LD), F32))
    loss, gl, gf = lax.fori_loop(0, steps, step, init)

    def put(ref, index, value, which):
        if base is not None:
            value = value + base[which][index].astype(F32)
        ref[index] = value.astype(ref.dtype)

    every = slice(None)
    if base is not None:
        loss = loss + base[8][...]
        gl = gl + base[7][0:1, :]
        gf = gf + base[7][1:2, :]
    loss_ref[...] = loss
    g_gain[0:1, :] = gl
    g_gain[1:2, :] = gf
    hidden_t = jnp.transpose(hid[...])
    for c in range(3):
        cs = slice(c * 512, c * 512 + 512)
        put(g_in, (every, cs), mm(hidden_t, projg[:, cs]), 0)
    for c in range(4):
        cs = slice(c * 512, c * 512 + 512)
        put(g_up, (every, cs), mm(hidden_t, egrad[:, cs]), 1)
    put(g_out, (every, every), mm_tn(att[...], bgrad[...]), 2)
    for c in range(4):
        cs = slice(c * 512, c * 512 + 512)
        put(g_down, (cs, every), mm_tn(act[:, cs], bgrad[...]), 3)
    put(g_head, (every, every), mm_tn(fin[...], lgrad[...]), 4)
    lookup_all = jnp.where(
        ids_ref[:, 0:1] == lax.broadcasted_iota(jnp.int32, (rows, VOCAB), 1), 1.0, 0.0
    ).astype(BF16)
    put(g_embed, (every, every), mm_tn(lookup_all, sgrad[...]), 5)
    put(g_bridge, (every, every), mm_tn(inputs_ref[...], sgrad[...]), 6)


def byte_layer(inputs, ids, weighting, weights, gains, base=None, tile=256):
    rows = inputs.shape[0]
    shapes = [(LD, 3 * LD), (LD, LFF), (LD, LD), (LFF, LD), (LD, VOCAB), (VOCAB, LD), (GSLOT, LD)]
    out_shape = [jax.ShapeDtypeStruct(s, BF16) for s in shapes] + [
        jax.ShapeDtypeStruct((2, LD), F32), jax.ShapeDtypeStruct((1, 1), F32),
        jax.ShapeDtypeStruct((rows, GSLOT), BF16)]
    args = [inputs, ids, weighting, *weights, gains] + (list(base) if base is not None else [])
    vm = pl.BlockSpec(memory_space=pltpu.VMEM)
    return pl.pallas_call(
        functools.partial(byte_kernel, rows, tile, base is not None),
        out_shape=out_shape,
        in_specs=[vm] * len(args),
        out_specs=[vm] * len(out_shape),
        scratch_shapes=[
            pltpu.VMEM((rows, LD), BF16),
            pltpu.VMEM((tile, 3 * LD), BF16),
            pltpu.VMEM((tile // 128 * 4, 256, 128), F32),
            pltpu.VMEM((rows, LD), BF16),
            pltpu.VMEM((rows, LFF), BF16),
            pltpu.VMEM((tile, LFF), F32),
            pltpu.VMEM((rows, LD), BF16),
            pltpu.VMEM((rows, VOCAB), BF16),
            pltpu.VMEM((rows, LD), BF16),
            pltpu.VMEM((rows, LFF), BF16),
            pltpu.VMEM((tile, LD), BF16),
            pltpu.VMEM((rows, 3 * LD), BF16),
            pltpu.VMEM((rows, LD), BF16),
            pltpu.VMEM((tile, LD), F32),
        ],
        compiler_params=pltpu.CompilerParams(vmem_limit_bytes=60 * 2**20),
        name="byte_layer",
    )(*args)


def other(index, offset, size):
    return index ^ offset if size & (size - 1) == 0 else lax.rem(index + offset, size)


def origin(index, offset, size):
    return index ^ offset if size & (size - 1) == 0 else lax.rem(index + size - offset, size)


def place_of(ref, by_column, extent, index):
    at = pl.ds(pl.multiple_of(index * extent, extent), extent)
    return ref.at[:, at] if by_column else ref.at[at, :]


def remote(src, dst, send, recv, device):
    return pltpu.make_async_remote_copy(
        src_ref=src, dst_ref=dst, send_sem=send, recv_sem=recv, device_id=device, device_id_type=MESH
    )


def greet(devices):
    barrier = pltpu.get_barrier_semaphore()
    for device in devices:
        pl.semaphore_signal(barrier, inc=1, device_id=device, device_id_type=MESH)
    pl.semaphore_wait(barrier, len(devices))


def group_peers(slots, groups):
    s, m, d = lax.axis_index("slot"), lax.axis_index("mp"), lax.axis_index("dp")
    across = [(other(s, j, slots), m, d) for j in range(1, slots)]
    beside = [(s, m, other(d, k, groups)) for k in range(1, groups)]
    return across, beside


def stack_peers(stacks):
    s, m, d = lax.axis_index("slot"), lax.axis_index("mp"), lax.axis_index("dp")
    return [(s, other(m, j, stacks), d) for j in range(1, stacks)]


def gather_kernel(sizes, columns, *refs):
    slots, stacks, groups = sizes
    count = len(columns)
    shards, tail = refs[:count], refs[count]
    outs, gain_out = refs[count + 1 : 2 * count + 1], refs[2 * count + 1]
    (tail_z, tail_s, tail_d, own_sem, xs, xr, cs, cr, zs, zr, ts, tr, ds, dr, gs) = refs[2 * count + 2 :]
    s, d = lax.axis_index("slot"), lax.axis_index("dp")
    across, beside = group_peers(slots, groups)
    above = stack_peers(stacks)
    greet(across + beside + above)

    def place(w, slot, group):
        extent = shards[w].shape[1 if columns[w] else 0]
        return place_of(outs[w], columns[w], extent, slot * groups + group)

    pending = []
    tail_copies = [
        remote(tail, tail_z.at[j], zs.at[j], zr.at[j], above[j - 1]) for j in range(1, stacks)
    ]
    own_tail = pltpu.make_async_copy(tail, tail_z.at[0], gs.at[0])
    own_tail.start()
    for copy in tail_copies:
        copy.start()
    sends = {}
    for w in range(count):
        for j in range(1, slots):
            copy = remote(shards[w], place(w, s, d), xs.at[w, j], xr.at[w, j], across[j - 1])
            copy.start()
            sends[w, j] = copy
        for k in range(1, groups):
            copy = remote(shards[w], place(w, s, d), cs.at[w, 0, k], cr.at[w, 0, k], beside[k - 1])
            copy.start()
            pending.append(copy)
        copy = pltpu.make_async_copy(shards[w], place(w, s, d), own_sem.at[w])
        copy.start()
        sends[w, 0] = copy

    m = lax.axis_index("mp")
    own_tail.wait()
    for copy in tail_copies:
        copy.wait()
    chosen = tail_z[0]
    for j in range(1, stacks):
        chosen = jnp.where(origin(m, j, stacks) == stacks - 1, tail_z[j], chosen)
    tail_s[0] = chosen
    step = [remote(tail_s.at[0], tail_s.at[j], ts.at[j], tr.at[j], across[j - 1]) for j in range(1, slots)]
    for copy in step:
        copy.start()
    for copy in step:
        copy.wait()
    chosen = tail_s[0]
    for j in range(1, slots):
        chosen = jnp.where(origin(s, j, slots) == slots - 1, tail_s[j], chosen)
    tail_d[0] = chosen
    step = [remote(tail_d.at[0], tail_d.at[k], ds.at[k], dr.at[k], beside[k - 1]) for k in range(1, groups)]
    for copy in step:
        copy.start()
    for copy in step:
        copy.wait()
    chosen = tail_d[0]
    for k in range(1, groups):
        chosen = jnp.where(origin(d, k, groups) == groups - 1, tail_d[k], chosen)
    gain_out[...] = chosen.astype(F32)

    for w in range(count):
        for j in range(1, slots):
            here = place(w, origin(s, j, slots), d)
            remote(here, here, xs.at[w, j], xr.at[w, j], across[j - 1]).wait_recv()
            for k in range(1, groups):
                copy = remote(here, here, cs.at[w, j, k], cr.at[w, j, k], beside[k - 1])
                copy.start()
                pending.append(copy)
    for w in range(count):
        sends[w, 0].wait()
        for j in range(1, slots):
            sends[w, j].wait_send()
    for copy in pending:
        copy.wait()


def gather_weights(shards, columns, tail):
    sizes = tuple(lax.axis_size(axis) for axis in ("slot", "mp", "dp"))
    slots, stacks, groups = sizes
    count = len(shards)
    parts = slots * groups
    shapes = [
        (v.shape[0], v.shape[1] * parts) if c else (v.shape[0] * parts, v.shape[1])
        for v, c in zip(shards, columns)
    ]
    anywhere = pl.BlockSpec(memory_space=pl.ANY)
    dma = pltpu.SemaphoreType.DMA
    return pl.pallas_call(
        functools.partial(gather_kernel, sizes, columns),
        out_shape=[jax.ShapeDtypeStruct(shape, BF16) for shape in shapes]
        + [jax.ShapeDtypeStruct(tail.shape, F32)],
        in_specs=[anywhere] * (count + 1),
        out_specs=[anywhere] * count + [pl.BlockSpec(memory_space=pltpu.VMEM)],
        scratch_shapes=[
            pltpu.VMEM((stacks,) + tail.shape, BF16),
            pltpu.VMEM((slots,) + tail.shape, BF16),
            pltpu.VMEM((groups,) + tail.shape, BF16),
            dma((count,)),
            dma((count, slots)), dma((count, slots)),
            dma((count, slots, groups)), dma((count, slots, groups)),
            dma((stacks,)), dma((stacks,)),
            dma((slots,)), dma((slots,)),
            dma((groups,)), dma((groups,)),
            dma((1,)),
        ],
        compiler_params=pltpu.CompilerParams(collective_id=1, has_side_effects=True),
        name="gather_weights",
    )(*shards, tail)


def scatter_kernel(sizes, columns, extents, *refs):
    slots, stacks, groups = sizes
    count = len(columns)
    partials, outs = refs[:count], refs[count : 2 * count]
    rest = refs[2 * count :]
    from_core, stage, from_slot = rest[:count], rest[count : 2 * count], rest[2 * count : 3 * count]
    from_z, own_c, from_c, cs, cr, xs, xr, zs, zr, ts, tr = rest[3 * count :]
    s, m, d = lax.axis_index("slot"), lax.axis_index("mp"), lax.axis_index("dp")
    across, beside = group_peers(slots, groups)
    above = stack_peers(stacks)
    greet(across + beside + above)
    order = (count - 1,) + tuple(range(count - 1))

    def part(w, slot, group):
        return place_of(partials[w], columns[w], extents[w], slot * groups + group)

    first = {}
    for w in order:
        for j in tuple(range(1, slots)) + (0,):
            t = other(s, j, slots)
            for k in range(1, groups):
                copy = remote(
                    part(w, t, other(d, k, groups)), from_core[w].at[j, k - 1],
                    cs.at[w, j, k], cr.at[w, j, k], beside[k - 1],
                )
                copy.start()
                first[w, j, k] = copy
    second = {}
    for w in order:
        for j in tuple(range(1, slots)) + (0,):
            t = other(s, j, slots)
            for k in range(1, groups):
                first[w, j, k].wait_recv()
            total = part(w, t, d)[...].astype(F32)
            for k in range(1, groups):
                total = total + from_core[w][j, k - 1].astype(F32)
            if j:
                stage[w][j] = total.astype(BF16)
                copy = remote(stage[w].at[j], from_slot[w].at[j], xs.at[w, j], xr.at[w, j], across[j - 1])
                copy.start()
                second[w, j] = copy
            else:
                outs[w][: total.shape[0]] = total
    for w in order:
        for j in range(1, slots):
            second[w, j].wait_recv()
        total = outs[w][: from_slot[w].shape[1]]
        for j in range(1, slots):
            total = total + from_slot[w][j].astype(F32)
        outs[w][: total.shape[0]] = total
        if w == order[0]:
            from_z[m] = total.astype(BF16)
            third = [
                remote(from_z.at[m], from_z.at[m], zs.at[j], zr.at[j], above[j - 1])
                for j in range(1, stacks)
            ]
            for copy in third:
                copy.start()
    w = order[0]
    size = from_slot[w].shape[1]
    for copy in third:
        copy.wait()
    total = from_z[0].astype(F32)
    for j in range(1, stacks):
        total = total + from_z[j].astype(F32)
    own_c[...] = total.astype(BF16)
    fourth = [remote(own_c, from_c.at[k], ts.at[k], tr.at[k], beside[k - 1]) for k in range(1, groups)]
    for copy in fourth:
        copy.start()
    outs[w][pl.ds(pl.multiple_of(d * size, size), size), :] = own_c[...].astype(F32)
    for k in range(1, groups):
        fourth[k - 1].wait()
        outs[w][pl.ds(pl.multiple_of(origin(d, k, groups) * size, size), size), :] = from_c[k].astype(F32)
    for copy in first.values():
        copy.wait_send()
    for copy in second.values():
        copy.wait_send()


def scatter_grads(partials, columns):
    sizes = tuple(lax.axis_size(axis) for axis in ("slot", "mp", "dp"))
    slots, stacks, groups = sizes
    count = len(partials)
    parts = slots * groups
    blocks = [
        (v.shape[0], v.shape[1] // parts) if c else (v.shape[0] // parts, v.shape[1])
        for v, c in zip(partials, columns)
    ]
    extents = tuple(b[1] if c else b[0] for b, c in zip(blocks, columns))
    shapes = blocks[:-1] + [(blocks[-1][0] * groups, blocks[-1][1])]
    vm = pl.BlockSpec(memory_space=pltpu.VMEM)
    dma = pltpu.SemaphoreType.DMA
    last = blocks[-1]
    return pl.pallas_call(
        functools.partial(scatter_kernel, sizes, columns, extents),
        out_shape=[jax.ShapeDtypeStruct(shape, F32) for shape in shapes],
        in_specs=[vm] * count,
        out_specs=[vm] * count,
        scratch_shapes=[pltpu.VMEM((slots, groups - 1) + b, BF16) for b in blocks]
        + [pltpu.VMEM((slots,) + b, BF16) for b in blocks]
        + [pltpu.VMEM((slots,) + b, BF16) for b in blocks]
        + [
            pltpu.VMEM((stacks,) + last, BF16),
            pltpu.VMEM(last, BF16), pltpu.VMEM((groups,) + last, BF16),
            dma((count, slots, groups)), dma((count, slots, groups)),
            dma((count, slots)), dma((count, slots)),
            dma((stacks,)), dma((stacks,)),
            dma((groups,)), dma((groups,)),
        ],
        compiler_params=pltpu.CompilerParams(
            collective_id=2, has_side_effects=True, vmem_limit_bytes=48 * 2**20
        ),
        name="scatter_grads",
    )(*partials)


def total_kernel(sizes, value, out, held_z, held_s, held_d, zs, zr, xs, xr, cs, cr):
    slots, stacks, groups = sizes
    across, beside = group_peers(slots, groups)
    above = stack_peers(stacks)
    greet(across + beside + above)
    total = value[...]
    for axis, peers, held, send, recv in (
        ("mp", above, held_z, zs, zr), ("slot", across, held_s, xs, xr), ("dp", beside, held_d, cs, cr)
    ):
        index = lax.axis_index(axis)
        held[index] = total
        copies = [
            remote(held.at[index], held.at[index], send.at[j], recv.at[j], peer)
            for j, peer in enumerate(peers)
        ]
        for copy in copies:
            copy.start()
        for copy in copies:
            copy.wait()
        total = held[0]
        for j in range(1, len(peers) + 1):
            total = total + held[j]
    out[...] = total


def total_of(value):
    sizes = tuple(lax.axis_size(axis) for axis in ("slot", "mp", "dp"))
    slots, stacks, groups = sizes
    vm = pl.BlockSpec(memory_space=pltpu.VMEM)
    dma = pltpu.SemaphoreType.DMA
    return pl.pallas_call(
        functools.partial(total_kernel, sizes),
        out_shape=jax.ShapeDtypeStruct(value.shape, F32),
        in_specs=[vm],
        out_specs=vm,
        scratch_shapes=[pltpu.VMEM((size,) + value.shape, F32) for size in (stacks, slots, groups)]
        + [dma((size,)) for size in (stacks, stacks, slots, slots, groups, groups)],
        compiler_params=pltpu.CompilerParams(collective_id=3, has_side_effects=True),
        name="total_of",
    )(value)


def pieces_of(size):
    return max(step for step in range(16, 129, 16) if size % step == 0)


def pack_layout():
    layout = []
    offset = 0
    for height, breadth in (
        (LD, 3 * LD), (LD, LFF), (LD, LD), (LFF, LD), (LD, VOCAB), (VOCAB, LD), (GSLOT, LD)
    ):
        layout.append((offset, height, breadth // 128))
        offset += height * breadth // 128
    return layout, offset


def unpack_kernel(share, rows, count, blocks_ref, *refs):
    outs, flat = refs[:-1], refs[-1]
    chunk = pieces_of(rows)
    flat[0:8, :] = jnp.zeros((8, 128), F32)

    def block(b, _):
        top = lax.div(b * share, 128)
        held = flat[pl.ds(top, 1), :]
        for i in range(0, rows, chunk):
            source = pl.ds(pl.multiple_of(b * rows, 16) + i, chunk)
            flat[pl.ds(top + i, chunk), :] = blocks_ref[source, :].astype(F32)
        flat[pl.ds(top, 1), :] = flat[pl.ds(top, 1), :] + held
        return 0

    lax.fori_loop(0, count, block, 0)
    layout, _ = pack_layout()
    for out, (offset, height, breadth) in zip(outs, layout):
        def part(i, _, out=out, offset=offset, breadth=breadth):
            for c in range(breadth):
                values = flat[pl.ds(offset + i * (128 * breadth) + c, 128, stride=breadth), :]
                out[pl.ds(pl.multiple_of(i * 128, 128), 128), c * 128 : (c + 1) * 128] = values.astype(BF16)
            return 0
        lax.fori_loop(0, height // 128, part, 0)


def unpack(blocks, share):
    rows = block_rows(share)
    count = blocks.shape[0] // rows
    layout, used = pack_layout()
    vm = pl.BlockSpec(memory_space=pltpu.VMEM)
    return pl.pallas_call(
        functools.partial(unpack_kernel, share, rows, count),
        out_shape=[jax.ShapeDtypeStruct((h, b * 128), BF16) for _, h, b in layout],
        in_specs=[vm],
        out_specs=[vm] * len(layout),
        scratch_shapes=[pltpu.VMEM((share * count // 128 + rows + 8, 128), F32)],
        compiler_params=pltpu.CompilerParams(vmem_limit_bytes=48 * 2**20),
        name="unpack",
    )(blocks)


def pack_kernel(share, rows, count, *refs):
    matrices, out, flat = refs[:-2], refs[-2], refs[-1]
    chunk = pieces_of(rows)
    layout, used = pack_layout()
    for matrix, (offset, height, breadth) in zip(matrices, layout):
        def part(i, _, matrix=matrix, offset=offset, breadth=breadth):
            for c in range(breadth):
                values = matrix[pl.ds(pl.multiple_of(i * 128, 128), 128), c * 128 : (c + 1) * 128]
                flat[pl.ds(offset + i * (128 * breadth) + c, 128, stride=breadth), :] = values.astype(F32)
            return 0
        lax.fori_loop(0, height // 128, part, 0)
    spare = flat.shape[0] - used
    flat[used:, :] = jnp.zeros((spare, 128), F32)

    def block(b, _):
        top = lax.div(b * share, 128)
        for i in range(0, rows, chunk):
            target = pl.ds(pl.multiple_of(b * rows, 16) + i, chunk)
            out[target, :] = flat[pl.ds(top + i, chunk), :].astype(BF16)
        return 0

    lax.fori_loop(0, count, block, 0)


def pack(matrices, share):
    rows = block_rows(share)
    layout, used = pack_layout()
    total = used + (D + 2 * LD) // 128
    count = total * 128 // share
    vm = pl.BlockSpec(memory_space=pltpu.VMEM)
    return pl.pallas_call(
        functools.partial(pack_kernel, share, rows, count),
        out_shape=jax.ShapeDtypeStruct((count * rows, 128), BF16),
        in_specs=[vm] * len(layout),
        out_specs=vm,
        scratch_shapes=[pltpu.VMEM((total + rows + 8, 128), F32)],
        compiler_params=pltpu.CompilerParams(vmem_limit_bytes=48 * 2**20),
        name="pack",
    )(*matrices)


def partner(index, offset, size):
    return index ^ offset if size & (size - 1) == 0 else (index + offset) % size


def swap(value, axis, offset):
    size = lax.axis_size(axis)
    if size & (size - 1) == 0:
        pairs = [(i, i ^ offset) for i in range(size)]
    else:
        pairs = [(i, (i + offset) % size) for i in range(size)]
    return lax.ppermute(value, axis, pairs)


def source(index, offset, size):
    return index ^ offset if size & (size - 1) == 0 else (index + size - offset) % size


def scatter_rows(partial, axis):
    size = lax.axis_size(axis)
    index = lax.axis_index(axis)
    share = partial.shape[0] // size
    pieces = []
    for offset in range(1, size):
        block = lax.dynamic_slice_in_dim(partial, partner(index, offset, size) * share, share, 0)
        pieces.append(swap(block.astype(BF16), axis, offset))
    total = lax.dynamic_slice_in_dim(partial, index * share, share, 0).astype(F32)
    for piece in pieces:
        total = total + piece.astype(F32)
    return total


def gather_rows(block, axis):
    size = lax.axis_size(axis)
    index = lax.axis_index(axis)
    share = block.shape[0]
    whole = jnp.zeros((size * share,) + block.shape[1:], block.dtype)
    whole = lax.dynamic_update_slice_in_dim(whole, block, index * share, 0)
    for offset in range(1, size):
        whole = lax.dynamic_update_slice_in_dim(
            whole, swap(block, axis, offset), source(index, offset, size) * share, 0
        )
    return whole


def shift_chunks(value, distance, forward):
    size = lax.axis_size("slot")
    if forward:
        pairs = [(i, i + distance) for i in range(size - distance)]
    else:
        pairs = [(i + distance, i) for i in range(size - distance)]
    return lax.ppermute(value, "slot", pairs)


def update(weight, moment, average, gradient, factor, rate):
    step_grad = factor * gradient
    moment_next = momentum_keep * moment + step_grad
    weight_next = weight - rate * (step_grad + momentum_keep * moment_next)
    average_next = average_keep * average + (1.0 - average_keep) * weight_next
    return (weight_next, moment_next, average_next)


def block_rows(share):
    return -(-(-(-share // 128) + 1) // 16) * 16


def gather_pack(local_pack):
    share = local_pack.shape[0]
    index = lax.axis_index(("slot", "mp", "dp"))
    offset = lax.rem(index * share, 128)
    rows = block_rows(share)
    block = lax.dynamic_update_slice_in_dim(
        jnp.zeros((rows * 128,), BF16), local_pack.astype(BF16), offset, 0
    )
    return lax.all_gather(block.reshape(rows, 128), ("slot", "mp", "dp"), axis=0, tiled=True)


def scatter_pack(blocks, share):
    own = lax.psum_scatter(blocks, ("slot", "mp", "dp"), scatter_dimension=0, tiled=True)
    index = lax.axis_index(("slot", "mp", "dp"))
    offset = lax.rem(index * share, 128)
    return lax.dynamic_slice_in_dim(own.reshape(-1), offset, share, 0).astype(F32)


def local(
    byte_ids, item_ids, loss_mask,
    attend_in, expand_in, attend_out, expand_out, slot_table, local_pack,
    moment_attend_in, moment_expand_in, moment_attend_out, moment_expand_out,
    moment_slot_table, moment_local_pack,
    average_attend_in, average_expand_in, average_attend_out, average_expand_out,
    average_slot_table, average_local_pack,
):
    slot_size, mp_size = lax.axis_size("slot"), lax.axis_size("mp")
    slot_index, mp_index, dp_index = (
        lax.axis_index("slot"), lax.axis_index("mp"), lax.axis_index("dp"),
    )
    mask_count = lax.psum(jnp.sum(loss_mask.astype(F32)), "dp")
    part = attend_in.shape[0]
    width = attend_in.shape[2]
    piece = slot_table.shape[0] * VOCAB // lax.axis_size("dp")
    table_shard = lax.dynamic_slice_in_dim(
        slot_table.reshape(-1, GSLOT), dp_index * piece, piece, 0
    ).astype(BF16)
    tail = local_pack[-(D + 2 * LD) :].astype(BF16).reshape(-1, 128)
    pack_whole = gather_pack(local_pack)
    shards = [table_shard, attend_in.astype(BF16).reshape(part, 3 * width), expand_in.astype(BF16)]
    late = [attend_out.astype(BF16), expand_out.astype(BF16)]
    wide = attend_out.shape[1] % 128 == 0
    if wide:
        table, full_in_flat, full_expand, full_out, full_shrink, gains = gather_weights(
            shards + late, (False, False, False, True, True), tail
        )
    else:
        table, full_in_flat, full_expand, gains = gather_weights(shards, (False, False, False), tail)
        full_out, full_shrink = (
            lax.all_gather(v, ("slot", "dp"), axis=1, tiled=True) for v in late
        )
    table = table.reshape(SLOTS, VOCAB, GSLOT)
    gains = gains.reshape(-1)
    gain_global = gains[:D]
    local_gains = gains[D:].reshape(2, LD)
    unpacked = unpack(pack_whole, local_pack.shape[0])
    group_rows = byte_ids.shape[1]
    rows = group_rows // slot_size
    local_rows = rows // mp_size
    vocab_ids = jnp.arange(VOCAB)
    reach = min(slot_size - 1, -(-(longest_item - 1) // rows))
    micros = []
    for micro in range(byte_ids.shape[0]):
        forward = micro % 2 == 0
        chunk = slot_index if forward else slot_size - 1 - slot_index
        group_ids = byte_ids[micro]
        items = item_ids[micro, 0]
        begin = chunk * rows
        previous = jnp.concatenate([jnp.full((1, SLOTS), -1, jnp.int32), group_ids[:-1]], axis=0)
        earlier_item = jnp.concatenate([items[:1], items[:-1]])
        previous = jnp.where((items == earlier_item)[:, None], previous, -1)
        own_previous = lax.dynamic_slice_in_dim(previous, begin, rows, 0)
        own_items = lax.dynamic_slice_in_dim(items, begin, rows, 0)
        first = jnp.sum((items[None, :] < own_items[:, None]).astype(jnp.int32), axis=1)
        first = jnp.maximum(first - (chunk - reach) * rows, 0)
        lookup = (own_previous[:, :, None] == vocab_ids).astype(BF16)
        start_rows = (
            jnp.einsum("pjv,jvg->pjg", lookup, table, preferred_element_type=F32)
            .astype(BF16).reshape(rows, D).astype(F32)
        )
        normed, scaled, factor = norm_forward(start_rows, gain_global)
        hidden = normed.astype(BF16)
        projected = product(hidden, full_in_flat).astype(BF16)
        own_kv = projected[:, width:]
        earlier = [shift_chunks(own_kv, d, forward) for d in range(1, reach + 1)]
        expanded = product(hidden, full_expand)
        active = gelu_tanh(expanded).astype(BF16)
        begin_local = begin + mp_index * local_rows
        micros.append(dict(
            forward=forward, group_ids=group_ids, begin_local=begin_local, start_rows=start_rows,
            hidden=hidden, projected=projected, earlier=earlier,
            expanded=expanded, active=active, low=first[::BLK] // BLK,
            first=first.reshape(-1, 1, BLK), own_previous=own_previous, mask=loss_mask[micro],
        ))
    for m in micros:
        m["attended"], m["lse"] = attention_fwd(m["low"], m["first"], m["projected"], m["earlier"])
        branch = scatter_rows(
            product(m["attended"], full_out) + product(m["active"], full_shrink), "mp"
        )
        m["own_start"] = lax.dynamic_slice_in_dim(
            m["start_rows"], mp_index * local_rows, local_rows, 0
        )
        m["middle"] = m["own_start"] + branch
    base = None
    for m in micros:
        ids = lax.dynamic_slice_in_dim(m["group_ids"], m["begin_local"], local_rows, 0)
        mask = lax.dynamic_slice_in_dim(m["mask"], m["begin_local"], local_rows, 0)
        before = jnp.concatenate([jnp.full((local_rows, 1), -1, jnp.int32), ids[:, :-1]], axis=1)
        weighting = mask.reshape(-1, 1).astype(F32) / mask_count
        out = byte_layer(
            m["middle"].astype(BF16).reshape(-1, GSLOT),
            jnp.stack([before.reshape(-1), ids.reshape(-1)], axis=1),
            weighting, unpacked[:7], local_gains, base,
        )
        base = out[:9]
        m["own_back"] = out[9].reshape(local_rows, D)
        m["branch_grad"] = gather_rows(m["own_back"], "mp")
    matrices, local_gain_grads, loss_sum = base[:7], base[7], base[8][0, 0]
    sums = None
    table_grad = None
    gain_global_grad = None
    for m in micros:
        branch_grad = m["branch_grad"]
        grad_out = gram_product(m["attended"], branch_grad)
        grad_shrink = gram_product(m["active"], branch_grad)
        attended_grad = back_product(branch_grad, full_out).astype(BF16)
        expanded_grad = gelu_back(m["expanded"], back_product(branch_grad, full_shrink)).astype(BF16)
        grad_expand = gram_product(m["hidden"], expanded_grad)
        query_grad, kv_grads = attention_bwd(
            m["low"], m["first"], m["projected"], m["earlier"], m["attended"], attended_grad, m["lse"]
        )
        kv_total = kv_grads[0].astype(F32)
        for d in range(1, reach + 1):
            kv_total = kv_total + shift_chunks(kv_grads[d], d, not m["forward"]).astype(F32)
        projected_grad = jnp.concatenate([query_grad, kv_total.astype(BF16)], axis=1)
        grad_in = gram_product(m["hidden"], projected_grad)
        hidden_grad = scatter_rows(
            back_product(projected_grad, full_in_flat) + back_product(expanded_grad, full_expand), "mp"
        )
        _, scaled, factor = norm_forward(m["own_start"], gain_global)
        gain_term = jnp.sum(hidden_grad * scaled, axis=0)
        start_grad = (
            m["own_back"].astype(F32) + norm_backward(scaled, factor, gain_global, hidden_grad)
        ).astype(BF16)
        own_lookup = lax.dynamic_slice_in_dim(m["own_previous"], mp_index * local_rows, local_rows, 0)
        own_lookup = (own_lookup[:, :, None] == vocab_ids).astype(BF16)
        table_term = jnp.einsum(
            "pjv,pjg->jvg", own_lookup, start_grad.reshape(local_rows, SLOTS, GSLOT),
            preferred_element_type=F32,
        )
        terms = (grad_in, grad_expand, grad_out, grad_shrink)
        if sums is None:
            sums, table_grad, gain_global_grad = terms, table_term, gain_term
        else:
            sums = tuple(a + b for a, b in zip(sums, terms))
            table_grad = table_grad + table_term
            gain_global_grad = gain_global_grad + gain_term
    sums = tuple(s.astype(BF16) for s in sums)
    gain_grads = jnp.concatenate([gain_global_grad, local_gain_grads.reshape(-1)])
    parts = slot_size * lax.axis_size("dp")
    small = jnp.concatenate(
        [
            table_grad.astype(BF16).reshape(parts, -1, GSLOT),
            jnp.broadcast_to(gain_grads.astype(BF16).reshape(1, -1, GSLOT), (parts, 16, GSLOT)),
        ],
        axis=1,
    ).reshape(-1, GSLOT)
    if wide:
        own_in, own_expand, own_out, own_shrink, own_small = scatter_grads(
            [*sums, small], (False, False, True, True, False)
        )
    else:
        own_in, own_expand, own_small = scatter_grads([*sums[:2], small], (False, False, False))
        own_out, own_shrink = (
            lax.psum_scatter(v, ("slot", "dp"), scatter_dimension=1, tiled=True).astype(F32)
            for v in sums[2:]
        )
    own_in = own_in.reshape(attend_in.shape)
    own_small = own_small.reshape(lax.axis_size("dp"), piece + 16, GSLOT)
    own_table = own_small[:, :piece].reshape(slot_table.shape)
    gain_total = own_small[0, piece:].reshape(-1)
    own_pack = scatter_pack(pack(matrices, local_pack.shape[0]), local_pack.shape[0])
    last = (slot_index == slot_size - 1) & (mp_index == mp_size - 1)
    last = last & (dp_index == lax.axis_size("dp") - 1)
    own_pack = jnp.concatenate(
        [own_pack[: -gain_total.shape[0]], jnp.where(last, gain_total, own_pack[-gain_total.shape[0] :])]
    )
    owner = ((mp_index == 0) & (dp_index == 0)).astype(F32)
    squares = jnp.sum(own_pack * own_pack) + owner * jnp.sum(own_table * own_table)
    for gradient in (own_in, own_expand, own_out, own_shrink):
        squares = squares + jnp.sum(gradient * gradient)
    both = total_of(jnp.stack([jnp.full((8, 128), squares), jnp.full((8, 128), loss_sum)]))
    total_squares, loss_value = both[0, 0, 0], both[1, 0, 0]
    clip_norm = jnp.sqrt(total_squares)
    factor = clip_max / jnp.maximum(clip_norm, clip_max)
    results = [loss_value * mask_count, mask_count, clip_norm]
    for weight, moment, average, gradient, rate in (
        (attend_in, moment_attend_in, average_attend_in, own_in, rate_dense),
        (expand_in, moment_expand_in, average_expand_in, own_expand, rate_dense),
        (attend_out, moment_attend_out, average_attend_out, own_out, rate_project),
        (expand_out, moment_expand_out, average_expand_out, own_shrink, rate_dense),
        (slot_table, moment_slot_table, average_slot_table, own_table, rate_table),
        (local_pack, moment_local_pack, average_local_pack, own_pack, rate_dense),
    ):
        results.extend(update(weight, moment, average, gradient, factor, rate))
    return tuple(results)


def solution(mesh):
    placed = (
        P(None, "dp", None),
        P(None, "dp", None),
        P(None, "dp", None),
        P(("slot", "dp"), None, "mp"),
        P(("slot", "dp"), "mp"),
        P("mp", ("slot", "dp")),
        P("mp", ("slot", "dp")),
        P("slot", None, None),
        P(("slot", "mp", "dp")),
        P(("slot", "dp"), None, "mp"),
        P(("slot", "dp"), "mp"),
        P("mp", ("slot", "dp")),
        P("mp", ("slot", "dp")),
        P("slot", None, None),
        P(("slot", "mp", "dp")),
        P(("slot", "dp"), None, "mp"),
        P(("slot", "dp"), "mp"),
        P("mp", ("slot", "dp")),
        P("mp", ("slot", "dp")),
        P("slot", None, None),
        P(("slot", "mp", "dp")),
    )
    return jax.shard_map(
        local,
        mesh=mesh,
        in_specs=placed,
        out_specs=(
            P(),
            P(),
            P(),
            P(("slot", "dp"), None, "mp"),
            P(("slot", "dp"), None, "mp"),
            P(("slot", "dp"), None, "mp"),
            P(("slot", "dp"), "mp"),
            P(("slot", "dp"), "mp"),
            P(("slot", "dp"), "mp"),
            P("mp", ("slot", "dp")),
            P("mp", ("slot", "dp")),
            P("mp", ("slot", "dp")),
            P("mp", ("slot", "dp")),
            P("mp", ("slot", "dp")),
            P("mp", ("slot", "dp")),
            P("slot", None, None),
            P("slot", None, None),
            P("slot", None, None),
            P(("slot", "mp", "dp")),
            P(("slot", "mp", "dp")),
            P(("slot", "mp", "dp")),
        ),
        check_vma=False,
    )
```

```python
import functools

import jax
import jax.numpy as jnp
from jax import lax
from jax.experimental import pallas as pl
from jax.experimental.pallas import tpu as pltpu
from jax.sharding import PartitionSpec as P

D = 1024
LD = 512
LH = 8
LFF = 2048
VOCAB = 256
SLOTS = 8
HEADDIM = 64
LHEADDIM = 64
GSLOT = 128
BLK = 256
F32 = jnp.float32
BF16 = jnp.bfloat16
MESH = pl.DeviceIdType.MESH

longest_item = 1024


epsilon = 1e-06
clip_max = 0.01
momentum_keep = 0.9
average_keep = 0.9
rate_dense = 3000.0
rate_table = 60000.0
rate_project = 15000.0
masked_score = -1e30


def product(left, right):
    return jnp.dot(left, right, preferred_element_type=jnp.float32)


def gram_product(left, right):
    return lax.dot_general(
        left, right, (((0,), (0,)), ((), ())), preferred_element_type=jnp.float32
    )


def back_product(left, right):
    return lax.dot_general(
        left, right, (((1,), (1,)), ((), ())), preferred_element_type=jnp.float32
    )


def gelu_tanh(values):
    return jax.nn.gelu(values, approximate=True)


def gelu_back(values, gradient):
    return jax.vjp(gelu_tanh, values)[1](gradient)[0]


def norm_forward(values, gain):
    factor = lax.rsqrt(jnp.mean(values * values, axis=-1, keepdims=True) + epsilon)
    scaled = values * factor
    return (scaled * gain, scaled, factor)


def norm_backward(scaled, factor, gain, gradient):
    inner = gradient * gain
    return factor * (inner - scaled * jnp.mean(inner * scaled, axis=-1, keepdims=True))


def split_pack(packed):
    layouts = (
        (LD, 3 * LD),
        (LD, LFF),
        (LD, LD),
        (LFF, LD),
        (LD, VOCAB),
        (VOCAB, LD),
        (GSLOT, LD),
        (D + 2 * LD,),
    )
    pieces = []
    offset = 0
    for layout in layouts:
        length = 1
        for extent in layout:
            length = length * extent
        pieces.append(packed[offset : offset + length].reshape(layout))
        offset = offset + length
    return pieces


def mm(a, b):
    return lax.dot_general(a, b, (((1,), (0,)), ((), ())), preferred_element_type=F32)


def mm_tn(a, b):
    return lax.dot_general(a, b, (((0,), (0,)), ((), ())), preferred_element_type=F32)


def mm_nt(a, b):
    return lax.dot_general(a, b, (((1,), (1,)), ((), ())), preferred_element_type=F32)


def stack_heads(x):
    lane = lax.broadcasted_iota(jnp.int32, x.shape, 1)
    zero = jnp.zeros_like(x)
    return jnp.concatenate([jnp.where(lane < 64, x, zero), jnp.where(lane < 64, zero, x)], axis=0)


def window_fill(rows, width, own_ref, earlier, keys, values_t, values, keys_t):
    for place, ref in enumerate(earlier):
        at = (len(earlier) - 1 - place) * rows
        if keys is not None:
            keys[at : at + rows, :] = ref[:, :width]
        if values is not None:
            values[at : at + rows, :] = ref[:, width:]
        if values_t is not None:
            values_t[:, at : at + rows] = jnp.transpose(ref[:, width:])
        if keys_t is not None:
            keys_t[:, at : at + rows] = jnp.transpose(ref[:, :width])
    at = len(earlier) * rows
    if keys is not None:
        keys[at : at + rows, :] = own_ref[:, width : 2 * width]
    if values is not None:
        values[at : at + rows, :] = own_ref[:, 2 * width :]
    if values_t is not None:
        values_t[:, at : at + rows] = jnp.transpose(own_ref[:, 2 * width :])
    if keys_t is not None:
        keys_t[:, at : at + rows] = jnp.transpose(own_ref[:, width : 2 * width])


def fwd_kernel(rows, width, count, low_ref, start_ref, own_ref, *rest):
    earlier, (att_ref, lse_ref, keys, values_t) = rest[:count], rest[count:]
    window_fill(rows, width, own_ref, earlier, keys, values_t, None, None)
    base = count * rows
    key_iota = lax.broadcasted_iota(jnp.int32, (BLK, 2 * BLK), 0)
    q_iota = lax.broadcasted_iota(jnp.int32, (1, 2 * BLK), 1) % BLK
    pairs = width // 128
    for qt in range(rows // BLK):
        q_pos = q_iota + (base + qt * BLK)
        start = start_ref[qt]
        start = jnp.concatenate([start, start], axis=1)
        for pair in range(pairs):
            cs = slice(pair * 128, pair * 128 + 128)
            qs = stack_heads(own_ref[qt * BLK : (qt + 1) * BLK, cs] * jnp.asarray(0.125, BF16))

            def block(i, carry):
                top, total, acc = carry
                kb = base // BLK + qt - i
                at = pl.ds(pl.multiple_of(kb * BLK, BLK), BLK)
                s = mm_nt(keys[at, cs], qs)
                pos = key_iota + kb * BLK
                s = jnp.where((pos >= start) & (pos <= q_pos), s, masked_score)
                new = jnp.maximum(top, jnp.max(s, axis=0, keepdims=True))
                p = jnp.exp(s - new)
                alpha = jnp.exp(top - new)
                total = total * alpha + jnp.sum(p, axis=0, keepdims=True)
                acc = acc * alpha + mm(values_t[cs, at], p.astype(BF16))
                return new, total, acc

            init = (
                jnp.full((1, 2 * BLK), masked_score, F32),
                jnp.zeros((1, 2 * BLK), F32),
                jnp.zeros((128, 2 * BLK), F32),
            )
            top, total, acc = lax.fori_loop(0, base // BLK + qt + 1 - low_ref[qt], block, init)
            acc = acc * (1.0 / total)
            sub = lax.broadcasted_iota(jnp.int32, (128, BLK), 0)
            both = jnp.where(sub < 64, acc[:, :BLK], acc[:, BLK:])
            att_ref[qt * BLK : (qt + 1) * BLK, cs] = jnp.transpose(both).astype(BF16)
            lse_ref[qt * pairs + pair] = top + jnp.log(total)


def bwd_kernel(rows, width, count, pieces, low_ref, start_ref, own_ref, *rest):
    earlier = rest[:count]
    att_ref, lse_ref, weight_ref = rest[count : count + 3]
    rest = rest[count + 3 :]
    piece_refs, rest = rest[:pieces], rest[pieces:]
    branch_ref, dq_ref, dkv_refs = rest[0], rest[1], rest[2 : count + 3]
    keys, values, keys_t, dkeys, dvalues, attg_ref = rest[count + 3 :]
    place, share = lax.axis_index("mp"), rows // pieces
    for j in range(pieces):
        at = pl.ds(pl.multiple_of(origin(place, j, pieces) * share, share), share)
        branch_ref[at, :] = piece_refs[j][...]
    attg_ref[...] = mm_nt(branch_ref[...], weight_ref[...]).astype(BF16)
    window_fill(rows, width, own_ref, earlier, keys, None, values, keys_t)
    base = count * rows
    dkeys[...] = jnp.zeros_like(dkeys)
    dvalues[...] = jnp.zeros_like(dvalues)
    key_iota = lax.broadcasted_iota(jnp.int32, (BLK, 2 * BLK), 0)
    q_iota = lax.broadcasted_iota(jnp.int32, (1, 2 * BLK), 1) % BLK
    pairs = width // 128
    for qt in range(rows // BLK):
        q_pos = q_iota + (base + qt * BLK)
        start = start_ref[qt]
        start = jnp.concatenate([start, start], axis=1)
        rq = slice(qt * BLK, (qt + 1) * BLK)
        for pair in range(pairs):
            cs = slice(pair * 128, pair * 128 + 128)
            qs = stack_heads(own_ref[rq, cs] * jnp.asarray(0.125, BF16))
            das = stack_heads(attg_ref[rq, cs])
            att = att_ref[rq, cs]
            both = jnp.concatenate([att, att], axis=0).astype(F32) * das.astype(F32)
            delta = jnp.sum(jnp.transpose(both), axis=0, keepdims=True)
            lse = lse_ref[qt * pairs + pair]

            def block(i, acc):
                kb = base // BLK + qt - i
                at = pl.ds(pl.multiple_of(kb * BLK, BLK), BLK)
                s = mm_nt(keys[at, cs], qs)
                pos = key_iota + kb * BLK
                p = jnp.where((pos >= start) & (pos <= q_pos), jnp.exp(s - lse), 0.0)
                dp = mm_nt(values[at, cs], das)
                ds = (p * (dp - delta)).astype(BF16)
                dkeys[at, cs] += mm(ds, qs)
                dvalues[at, cs] += mm(p.astype(BF16), das)
                return acc + mm(keys_t[cs, at], ds)

            acc = lax.fori_loop(
                0, base // BLK + qt + 1 - low_ref[qt], block, jnp.zeros((128, 2 * BLK), F32)
            )
            sub = lax.broadcasted_iota(jnp.int32, (128, BLK), 0)
            both = jnp.where(sub < 64, acc[:, :BLK], acc[:, BLK:]) * 0.125
            dq_ref[rq, cs] = jnp.transpose(both).astype(BF16)
    for place in range(count + 1):
        at = (count - place) * rows
        dkv_refs[place][:, :width] = dkeys[at : at + rows, :].astype(BF16)
        dkv_refs[place][:, width:] = dvalues[at : at + rows, :].astype(BF16)


def specs(n):
    return [pl.BlockSpec(memory_space=pltpu.SMEM)] + [pl.BlockSpec(memory_space=pltpu.VMEM)] * n


def attention_fwd(low, start, own, earlier):
    rows, width = own.shape[0], own.shape[1] // 3
    count = len(earlier)
    span = (count + 1) * rows
    units = rows // BLK * (width // 128)
    return pl.pallas_call(
        functools.partial(fwd_kernel, rows, width, count),
        out_shape=[
            jax.ShapeDtypeStruct((rows, width), BF16),
            jax.ShapeDtypeStruct((units, 1, 2 * BLK), F32),
        ],
        in_specs=specs(2 + count),
        out_specs=[pl.BlockSpec(memory_space=pltpu.VMEM)] * 2,
        scratch_shapes=[pltpu.VMEM((span, width), BF16), pltpu.VMEM((width, span), BF16)],
        cost_estimate=pl.CostEstimate(flops=6 * 10**9, bytes_accessed=20 * 10**6, transcendentals=10**6),
        compiler_params=pltpu.CompilerParams(vmem_limit_bytes=32 * 2**20),
        name="patch_attention",
    )(low, start, own, *earlier)


def attention_bwd(low, start, own, earlier, attended, lse, weight, pieces):
    rows, width = own.shape[0], own.shape[1] // 3
    count = len(earlier)
    span = (count + 1) * rows
    out = pl.pallas_call(
        functools.partial(bwd_kernel, rows, width, count, len(pieces)),
        out_shape=[jax.ShapeDtypeStruct((rows, pieces[0].shape[1]), BF16), jax.ShapeDtypeStruct((rows, width), BF16)]
        + [jax.ShapeDtypeStruct((rows, 2 * width), BF16)] * (count + 1),
        in_specs=specs(5 + count + len(pieces)),
        out_specs=[pl.BlockSpec(memory_space=pltpu.VMEM)] * (count + 3),
        scratch_shapes=[
            pltpu.VMEM((span, width), BF16),
            pltpu.VMEM((span, width), BF16),
            pltpu.VMEM((width, span), BF16),
            pltpu.VMEM((span, width), F32),
            pltpu.VMEM((span, width), F32),
            pltpu.VMEM((rows, width), BF16),
        ],
        cost_estimate=pl.CostEstimate(flops=8 * 10**9, bytes_accessed=25 * 10**6, transcendentals=10**6),
        compiler_params=pltpu.CompilerParams(vmem_limit_bytes=32 * 2**20),
        name="patch_attention_back",
    )(low, start, own, *earlier, attended, lse, weight, *pieces)
    return out[0], out[1], out[2:]


def embed_kernel(width, ids_ref, table_ref, w_ref, gain_ref, start_ref, hidden_ref, proj_ref, kv_ref):
    rows = ids_ref.shape[0]
    ids = ids_ref[...].astype(F32)
    low = lax.broadcasted_iota(jnp.int32, (rows, 128), 1).astype(F32)
    squares = jnp.zeros((rows, 1), F32)
    parts = []
    for j in range(SLOTS):
        own = jnp.broadcast_to(ids[:, j : j + 1], (rows, 128))
        hot = jnp.concatenate(
            [jnp.where(own == low, 1.0, 0.0), jnp.where(own == low + 128.0, 1.0, 0.0)], axis=1
        ).astype(BF16)
        part = mm(hot, table_ref[j * VOCAB : (j + 1) * VOCAB, :])
        parts.append(part)
        squares = squares + jnp.sum(part * part, axis=-1, keepdims=True)
    factor = lax.rsqrt(squares * (1.0 / D) + epsilon)
    for j in range(SLOTS):
        cs = slice(j * GSLOT, (j + 1) * GSLOT)
        start_ref[:, cs] = parts[j].astype(BF16)
        hidden_ref[:, cs] = (parts[j] * factor * gain_ref[:, cs]).astype(BF16)
    hidden = hidden_ref[...]
    for c in range(3):
        cs = slice(c * width, (c + 1) * width)
        part = mm(hidden, w_ref[:, cs]).astype(BF16)
        proj_ref[:, cs] = part
        if c:
            kv_ref[:, (c - 1) * width : c * width] = part


def embed_rows(ids, table, weight, gain):
    rows, width = ids.shape[0], weight.shape[1] // 3
    vm = pl.BlockSpec(memory_space=pltpu.VMEM)
    return pl.pallas_call(
        functools.partial(embed_kernel, width),
        out_shape=[
            jax.ShapeDtypeStruct((rows, D), BF16),
            jax.ShapeDtypeStruct((rows, D), BF16),
            jax.ShapeDtypeStruct((rows, 3 * width), BF16),
            jax.ShapeDtypeStruct((rows, 2 * width), BF16),
        ],
        in_specs=[vm] * 4,
        out_specs=[vm] * 4,
        cost_estimate=pl.CostEstimate(flops=2 * 10**9, bytes_accessed=6 * 10**6, transcendentals=1000),
        compiler_params=pltpu.CompilerParams(vmem_limit_bytes=32 * 2**20),
        name="embed_rows",
    )(ids, table, weight, gain)


def gelu_pair(x):
    c = 0.7978845608028654
    x2 = x * x
    t = jnp.tanh(c * (x + 0.044715 * (x2 * x)))
    half = 0.5 * (1.0 + t)
    slope = half + (0.5 * c) * x * (1.0 - t * t) * (1.0 + (3 * 0.044715) * x2)
    return x * half, slope


def byte_kernel(
    rows, tile, with_base,
    pieces, start_ref, own_ref, *rest
):
    piece_refs, rest = rest[:pieces], rest[pieces:]
    ids_ref, mask_ref, count_ref, w_in, w_up, w_out, w_down, w_head, w_embed, w_bridge, gains_ref = rest[:11]
    rest = rest[11:]
    if with_base:
        base, rest = rest[:9], rest[9:]
    else:
        base = None
    (g_in, g_up, g_out, g_down, g_head, g_embed, g_bridge, g_gain, loss_ref, inputg_ref,
     hid, proj, probs, att, act, slope, fin, lgrad, bgrad, egrad, attg, projg, sgrad, startv, att_t, projg_t,
     wide_rows, own_ids, prev_ids, weights, inputs_ref) = rest
    steps = rows // tile
    blocks = tile // 128
    g_gain_local = gains_ref[0:1, :]
    g_gain_final = gains_ref[1:2, :]
    first = lax.broadcasted_iota(jnp.int32, (128, 128), 1) < 64
    lane = lax.broadcasted_iota(jnp.int32, (SLOTS, 256), 1) % 128
    patch = lane // SLOTS
    causal = lax.broadcasted_iota(jnp.int32, (SLOTS, 256), 0) <= lane % SLOTS
    none = jnp.zeros((SLOTS, 256), F32)
    patches = rows // SLOTS
    for j in range(SLOTS):
        cs = slice(j * GSLOT, (j + 1) * GSLOT)
        at = pl.ds(j, patches, stride=SLOTS)
        total = own_ref[:, cs] + start_ref[:, cs].astype(F32)
        for piece in piece_refs:
            total = total + piece[:, cs].astype(F32)
        wide_rows[at, :] = total
        spread = functools.partial(jnp.broadcast_to, shape=(patches, 128))
        own_ids[at, :] = spread(ids_ref[:, j : j + 1].astype(F32))
        prev_ids[at, :] = spread(ids_ref[:, j - 1 : j].astype(F32)) if j else jnp.full((patches, 128), -1.0, F32)
        weights[at, :] = spread(mask_ref[:, j : j + 1].astype(F32) / count_ref[0, 0])
    inputs_ref[...] = wide_rows[...].astype(BF16)

    def one_hot(ids):
        low = lax.broadcasted_iota(jnp.int32, ids.shape, 1).astype(F32)
        return jnp.concatenate(
            [jnp.where(ids == low, 1.0, 0.0), jnp.where(ids == low + 128.0, 1.0, 0.0)], axis=1
        )

    zero_low = jnp.zeros((128, 128), BF16)

    def stack(x):
        return jnp.concatenate([jnp.where(first, x, zero_low), jnp.where(first, zero_low, x)], axis=0)

    def narrow(x):
        out = x[:SLOTS]
        for j in range(1, 16):
            out = jnp.where(patch == j, x[j * SLOTS : (j + 1) * SLOTS], out)
        return out

    def widen(x):
        return jnp.concatenate([jnp.where(patch == j, x, none) for j in range(16)], axis=0)

    def norm(v):
        factor = lax.rsqrt(jnp.mean(v * v, axis=-1, keepdims=True) + epsilon)
        return v * factor, factor

    def step(t, carry):
        loss, gl, gf = carry
        at = pl.ds(pl.multiple_of(t * tile, tile), tile)
        inputs = inputs_ref[at, :]
        weighting = weights[at, :]
        lookup = one_hot(prev_ids[at, :]).astype(BF16)
        start = mm(inputs, w_bridge[...]) + mm(lookup, w_embed[...])
        startv[...] = start
        scaled, factor = norm(start)
        hidden = (scaled * g_gain_local).astype(BF16)
        hid[at, :] = hidden
        for c in range(3):
            proj[:, c * LD : (c + 1) * LD] = mm(hidden, w_in[:, c * LD : (c + 1) * LD]).astype(BF16)

        def attend(b, _):
            ra = pl.ds(b * 128 if isinstance(b, int) else pl.multiple_of(b * 128, 128), 128)
            for pair in range(4):
                cs = slice(pair * 128, pair * 128 + 128)
                qs = stack(proj[ra, cs] * jnp.asarray(0.125, BF16))
                kp = proj[ra, LD + pair * 128 : LD + pair * 128 + 128]
                vp = proj[ra, 2 * LD + pair * 128 : 2 * LD + pair * 128 + 128]
                s = jnp.where(causal, narrow(mm_nt(kp, qs)), masked_score)
                e = jnp.exp(s - jnp.max(s, axis=0, keepdims=True))
                p = e * (1.0 / jnp.sum(e, axis=0, keepdims=True))
                probs[b * 4 + pair] = p
                flipped = jnp.transpose(widen(p).astype(BF16))
                wide = jnp.concatenate([flipped[:128], flipped[128:]], axis=1)
                att_t[ra, cs] = mm(wide, stack(vp)).astype(BF16)
            return 0

        def two(i, _):
            attend(2 * i, 0)
            return attend(2 * i + 1, 0)

        lax.fori_loop(0, blocks // 2, two, 0)
        attended = att_t[...]
        att[at, :] = attended
        after = start + mm(attended, w_out[...])
        for c in range(4):
            cs = slice(c * 512, c * 512 + 512)
            a, s = gelu_pair(mm(hidden, w_up[:, cs]))
            a = a.astype(BF16)
            act[at, cs] = a
            slope[:, cs] = s.astype(BF16)
            after = after + mm(a, w_down[cs, :])
        scaled_f, factor_f = norm(after)
        final = (scaled_f * g_gain_final).astype(BF16)
        fin[at, :] = final
        logits = mm(final, w_head[...])
        hot = one_hot(own_ids[at, :])
        top = jnp.max(logits, axis=-1, keepdims=True)
        log_total = top + jnp.log(jnp.sum(jnp.exp(logits - top), axis=-1, keepdims=True))
        loss = loss + jnp.sum(
            weighting[:, :1] * (log_total - jnp.sum(logits * hot, axis=-1, keepdims=True)), axis=0, keepdims=True
        )
        lg = ((jnp.exp(logits - log_total) - hot) * jnp.concatenate([weighting, weighting], axis=1)).astype(BF16)
        lgrad[at, :] = lg
        fg = mm_nt(lg, w_head[...])
        gf = gf + jnp.sum(fg * scaled_f, axis=0, keepdims=True)
        inner = fg * g_gain_final
        after_grad = factor_f * (inner - scaled_f * jnp.mean(inner * scaled_f, axis=-1, keepdims=True))
        bg = after_grad.astype(BF16)
        bgrad[at, :] = bg
        attg[...] = mm_nt(bg, w_out[...]).astype(BF16)
        hg = None
        for c in range(4):
            cs = slice(c * 512, c * 512 + 512)
            eg = (slope[:, cs] * mm_nt(bg, w_down[cs, :])).astype(BF16)
            egrad[at, cs] = eg
            term = mm_nt(eg, w_up[:, cs])
            hg = term if hg is None else hg + term

        def attend_back(b, _):
            ra = pl.ds(b * 128 if isinstance(b, int) else pl.multiple_of(b * 128, 128), 128)
            for pair in range(4):
                cs = slice(pair * 128, pair * 128 + 128)
                qs = stack(proj[ra, cs] * jnp.asarray(0.125, BF16))
                kp = proj[ra, LD + pair * 128 : LD + pair * 128 + 128]
                vp = proj[ra, 2 * LD + pair * 128 : 2 * LD + pair * 128 + 128]
                das = stack(attg[ra, cs])
                p = probs[b * 4 + pair]
                dp = narrow(mm_nt(vp, das))
                ds = widen(p * (dp - jnp.sum(p * dp, axis=0, keepdims=True)))
                flipped = jnp.transpose(ds.astype(BF16))
                wide = jnp.concatenate([flipped[:128], flipped[128:]], axis=1)
                projg_t[ra, cs] = (mm(wide, stack(kp)) * 0.125).astype(BF16)
                projg_t[ra, LD + pair * 128 : LD + pair * 128 + 128] = mm(ds.astype(BF16), qs).astype(BF16)
                projg_t[ra, 2 * LD + pair * 128 : 2 * LD + pair * 128 + 128] = mm(widen(p).astype(BF16), das).astype(BF16)
            return 0

        for b in range(blocks):
            attend_back(b, 0)
        for c in range(3):
            own = projg_t[:, c * LD : (c + 1) * LD]
            projg[at, c * LD : (c + 1) * LD] = own
            hg = hg + mm_nt(own, w_in[:, c * LD : (c + 1) * LD])
        start = startv[...]
        scaled, factor = norm(start)
        gl = gl + jnp.sum(hg * scaled, axis=0, keepdims=True)
        inner = hg * g_gain_local
        sg = (after_grad + factor * (inner - scaled * jnp.mean(inner * scaled, axis=-1, keepdims=True))).astype(BF16)
        sgrad[at, :] = sg
        wide_rows[at, :] = mm_nt(sg, w_bridge[...])
        return loss, gl, gf

    init = (jnp.zeros((1, 1), F32), jnp.zeros((1, LD), F32), jnp.zeros((1, LD), F32))
    loss, gl, gf = lax.fori_loop(0, steps, step, init)

    for j in range(SLOTS):
        inputg_ref[:, j * GSLOT : (j + 1) * GSLOT] = wide_rows[pl.ds(j, patches, stride=SLOTS), :].astype(BF16)

    def put(ref, index, value, which):
        if base is not None:
            value = value + base[which][index].astype(F32)
        ref[index] = value.astype(ref.dtype)

    every = slice(None)
    if base is not None:
        loss = loss + base[8][...]
        gl = gl + base[7][0:1, :]
        gf = gf + base[7][1:2, :]
    loss_ref[...] = loss
    g_gain[0:1, :] = gl
    g_gain[1:2, :] = gf
    hidden_t = jnp.transpose(hid[...])
    for c in range(3):
        cs = slice(c * 512, c * 512 + 512)
        put(g_in, (every, cs), mm(hidden_t, projg[:, cs]), 0)
    for c in range(4):
        cs = slice(c * 512, c * 512 + 512)
        put(g_up, (every, cs), mm(hidden_t, egrad[:, cs]), 1)
    put(g_out, (every, every), mm_tn(att[...], bgrad[...]), 2)
    for c in range(4):
        cs = slice(c * 512, c * 512 + 512)
        put(g_down, (cs, every), mm_tn(act[:, cs], bgrad[...]), 3)
    put(g_head, (every, every), mm_tn(fin[...], lgrad[...]), 4)
    lookup_all = one_hot(prev_ids[...]).astype(BF16)
    put(g_embed, (every, every), mm_tn(lookup_all, sgrad[...]), 5)
    put(g_bridge, (every, every), mm_tn(inputs_ref[...], sgrad[...]), 6)


def byte_layer(start, own, pieces, ids, mask, count, weights, gains, base=None, tile=512):
    rows = start.shape[0] * SLOTS
    shapes = [(LD, 3 * LD), (LD, LFF), (LD, LD), (LFF, LD), (LD, VOCAB), (VOCAB, LD), (GSLOT, LD)]
    out_shape = [jax.ShapeDtypeStruct(s, BF16) for s in shapes] + [
        jax.ShapeDtypeStruct((2, LD), F32), jax.ShapeDtypeStruct((1, 1), F32),
        jax.ShapeDtypeStruct(start.shape, BF16)]
    args = [start, own, *pieces, ids, mask, count, *weights, gains] + (list(base) if base is not None else [])
    vm = pl.BlockSpec(memory_space=pltpu.VMEM)
    in_specs = [vm] * len(args)
    in_specs[4 + len(pieces)] = pl.BlockSpec(memory_space=pltpu.SMEM)
    return pl.pallas_call(
        functools.partial(byte_kernel, rows, tile, base is not None, len(pieces)),
        out_shape=out_shape,
        in_specs=in_specs,
        out_specs=[vm] * len(out_shape),
        cost_estimate=pl.CostEstimate(flops=43 * 10**9, bytes_accessed=150 * 10**6, transcendentals=10**6),
        scratch_shapes=[
            pltpu.VMEM((rows, LD), BF16),
            pltpu.VMEM((tile, 3 * LD), BF16),
            pltpu.VMEM((tile // 128 * 4, SLOTS, 256), F32),
            pltpu.VMEM((rows, LD), BF16),
            pltpu.VMEM((rows, LFF), BF16),
            pltpu.VMEM((tile, LFF), BF16),
            pltpu.VMEM((rows, LD), BF16),
            pltpu.VMEM((rows, VOCAB), BF16),
            pltpu.VMEM((rows, LD), BF16),
            pltpu.VMEM((rows, LFF), BF16),
            pltpu.VMEM((tile, LD), BF16),
            pltpu.VMEM((rows, 3 * LD), BF16),
            pltpu.VMEM((rows, LD), BF16),
            pltpu.VMEM((tile, LD), F32),
            pltpu.VMEM((tile, LD), BF16),
            pltpu.VMEM((tile, 3 * LD), BF16),
            pltpu.VMEM((rows, GSLOT), F32),
            pltpu.VMEM((rows, GSLOT), F32),
            pltpu.VMEM((rows, GSLOT), F32),
            pltpu.VMEM((rows, GSLOT), F32),
            pltpu.VMEM((rows, GSLOT), BF16),
        ],
        compiler_params=pltpu.CompilerParams(vmem_limit_bytes=61 * 2**20),
        name="byte_layer",
    )(*args)


def other(index, offset, size):
    return index ^ offset if size & (size - 1) == 0 else lax.rem(index + offset, size)


def origin(index, offset, size):
    return index ^ offset if size & (size - 1) == 0 else lax.rem(index + size - offset, size)


def place_of(ref, by_column, extent, index):
    at = pl.ds(pl.multiple_of(index * extent, extent), extent)
    return ref.at[:, at] if by_column else ref.at[at, :]


def remote(src, dst, send, recv, device):
    return pltpu.make_async_remote_copy(
        src_ref=src, dst_ref=dst, send_sem=send, recv_sem=recv, device_id=device, device_id_type=MESH
    )


def greet(devices):
    barrier = pltpu.get_barrier_semaphore()
    for device in devices:
        pl.semaphore_signal(barrier, inc=1, device_id=device, device_id_type=MESH)
    pl.semaphore_wait(barrier, len(devices))


def group_peers(slots, groups):
    s, m, d = lax.axis_index("slot"), lax.axis_index("mp"), lax.axis_index("dp")
    across = [(other(s, j, slots), m, d) for j in range(1, slots)]
    beside = [(s, m, other(d, k, groups)) for k in range(1, groups)]
    return across, beside


def stack_peers(stacks):
    s, m, d = lax.axis_index("slot"), lax.axis_index("mp"), lax.axis_index("dp")
    return [(s, other(m, j, stacks), d) for j in range(1, stacks)]


def gather_kernel(sizes, columns, forwarded, *refs):
    slots, stacks, groups = sizes
    count = len(columns)
    wide, tail, counted = refs[:count], refs[count], refs[count + 1]
    outs, gain_out, count_out = refs[count + 2 : 2 * count + 2], refs[2 * count + 2], refs[2 * count + 3]
    shards, rest = refs[2 * count + 4 : 3 * count + 4], refs[3 * count + 4 :]
    (tail_z, tail_s, tail_d, held_count, own_sem, xs, xr, cs, cr, zs, zr, ts, tr, ds, dr, ns, nr) = rest
    s, m, d = lax.axis_index("slot"), lax.axis_index("mp"), lax.axis_index("dp")
    across, beside = group_peers(slots, groups)
    above = stack_peers(stacks)
    for w in range(count):
        if len(wide[w].shape) == 3:
            breadth = wide[w].shape[2]
            for i in range(wide[w].shape[0]):
                shards[w][:, i * breadth : (i + 1) * breadth] = wide[w][i].astype(BF16)
        else:
            shards[w][...] = wide[w][...].astype(BF16)
    tail_z[m] = tail[...].astype(BF16)
    held_count[d] = counted[...]
    greet(across + beside + above)

    def place(w, slot, group, half=None):
        rows, breadth = shards[w].shape
        index = slot * groups + group
        if half is None:
            return place_of(outs[w], columns[w], breadth if columns[w] else rows, index)
        size = rows // 2
        if columns[w]:
            return outs[w].at[pl.ds(half * size, size), pl.ds(pl.multiple_of(index * breadth, breadth), breadth)]
        return outs[w].at[pl.ds(pl.multiple_of(index * rows + half * size, size), size), :]

    tail_copies = [remote(tail_z.at[m], tail_z.at[m], zs.at[j], zr.at[j], above[j - 1]) for j in range(1, stacks)]
    tail_copies += [
        remote(held_count.at[d], held_count.at[d], ns.at[k], nr.at[k], beside[k - 1]) for k in range(1, groups)
    ]
    for copy in tail_copies:
        copy.start()
    sends, pending = [], []
    direct = (1, 2) if forwarded else tuple(range(1, slots))
    for w in range(count):
        for j in direct:
            copy = remote(shards[w], place(w, s, d), xs.at[w, j], xr.at[w, j], across[j - 1])
            copy.start()
            sends.append(copy)
    for w in range(count):
        for k in range(1, groups):
            copy = remote(shards[w], place(w, s, d), cs.at[w, 0, k], cr.at[w, 0, k], beside[k - 1])
            copy.start()
            pending.append(copy)
        copy = pltpu.make_async_copy(shards[w], place(w, s, d), own_sem.at[w])
        copy.start()
        pending.append(copy)

    for copy in tail_copies:
        copy.wait()
    total = held_count[0]
    for k in range(1, groups):
        total = total + held_count[k]
    count_out[...] = total
    tail_s[s] = tail_z[stacks - 1]
    step = [remote(tail_s.at[s], tail_s.at[s], ts.at[j], tr.at[j], across[j - 1]) for j in range(1, slots)]
    for copy in step:
        copy.start()
    for copy in step:
        copy.wait()
    tail_d[d] = tail_s[slots - 1]
    step = [remote(tail_d.at[d], tail_d.at[d], ds.at[k], dr.at[k], beside[k - 1]) for k in range(1, groups)]
    for copy in step:
        copy.start()
    for copy in step:
        copy.wait()
    gain_out[...] = tail_d[groups - 1].astype(F32)

    def spread(w, j, slot):
        here = place(w, slot, d)
        for k in range(1, groups):
            copy = remote(here, here, cs.at[w, j, k], cr.at[w, j, k], beside[k - 1])
            copy.start()
            pending.append(copy)

    for w in range(count):
        for j in direct:
            slot = origin(s, j, slots)
            here = place(w, slot, d)
            remote(here, here, xs.at[w, j], xr.at[w, j], across[j - 1]).wait_recv()
            if forwarded:
                half = 0 if j == 1 else 1
                part, index = place(w, slot, d, half), 3 if j == 1 else 0
                copy = remote(part, part, xs.at[w, index], xr.at[w, index], across[2 - j])
                copy.start()
                sends.append(copy)
            spread(w, j, slot)
    if forwarded:
        for w in range(count):
            slot = s ^ 3
            for half, index in ((0, 3), (1, 0)):
                part = place(w, slot, d, half)
                remote(part, part, xs.at[w, index], xr.at[w, index], across[1 - half]).wait_recv()
            spread(w, 3, slot)
    for copy in sends:
        copy.wait_send()
    for copy in pending:
        copy.wait()


def gather_weights(shards, columns, tail, counted):
    sizes = tuple(lax.axis_size(axis) for axis in ("slot", "mp", "dp"))
    slots, stacks, groups = sizes
    count = len(shards)
    parts = slots * groups
    flats = [(v.shape[1], v.shape[0] * v.shape[2]) if v.ndim == 3 else v.shape for v in shards]
    shapes = [
        (v[0], v[1] * parts) if c else (v[0] * parts, v[1]) for v, c in zip(flats, columns)
    ]
    forwarded = slots == 4 and all(v[0] % 32 == 0 for v in flats)
    anywhere = pl.BlockSpec(memory_space=pl.ANY)
    vm = pl.BlockSpec(memory_space=pltpu.VMEM)
    dma = pltpu.SemaphoreType.DMA
    return pl.pallas_call(
        functools.partial(gather_kernel, sizes, columns, forwarded),
        out_shape=[jax.ShapeDtypeStruct(shape, BF16) for shape in shapes]
        + [jax.ShapeDtypeStruct(tail.shape, F32), jax.ShapeDtypeStruct(counted.shape, F32)],
        in_specs=[vm] * (count + 2),
        out_specs=[anywhere] * count + [vm] * 2,
        scratch_shapes=[pltpu.VMEM(v, BF16) for v in flats]
        + [
            pltpu.VMEM((stacks,) + tail.shape, BF16),
            pltpu.VMEM((slots,) + tail.shape, BF16),
            pltpu.VMEM((groups,) + tail.shape, BF16),
            pltpu.VMEM((groups,) + counted.shape, F32),
            dma((count,)),
            dma((count, slots)), dma((count, slots)),
            dma((count, slots, groups)), dma((count, slots, groups)),
            dma((stacks,)), dma((stacks,)),
            dma((slots,)), dma((slots,)),
            dma((groups,)), dma((groups,)),
            dma((groups,)), dma((groups,)),
        ],
        compiler_params=pltpu.CompilerParams(
            collective_id=1, has_side_effects=True, vmem_limit_bytes=24 * 2**20
        ),
        cost_estimate=pl.CostEstimate(flops=10**6, bytes_accessed=120 * 10**6, transcendentals=0),
        name="gather_weights",
    )(*shards, tail, counted)


def scatter_kernel(sizes, columns, extents, shared, *refs):
    slots, stacks, groups = sizes
    count = len(columns)
    partials, outs = refs[:count], refs[count : 2 * count]
    rest = refs[2 * count :]
    from_core, stage, from_slot = rest[:count], rest[count : 2 * count], rest[2 * count : 3 * count]
    cs, cr, xs, xr = rest[3 * count : 3 * count + 4]
    if shared:
        from_z, own_c, from_c, zs, zr, ts, tr = rest[3 * count + 4 :]
    s, m, d = lax.axis_index("slot"), lax.axis_index("mp"), lax.axis_index("dp")
    across, beside = group_peers(slots, groups)
    above = stack_peers(stacks)
    greet(across + beside + above if shared else across + beside)
    order = tuple(range(count))

    def part(w, slot, group):
        return place_of(partials[w], columns[w], extents[w], slot * groups + group)

    first = {}
    for w in order:
        for j in tuple(range(1, slots)) + (0,):
            t = other(s, j, slots)
            for k in range(1, groups):
                copy = remote(
                    part(w, t, other(d, k, groups)), from_core[w].at[j, k - 1],
                    cs.at[w, j, k], cr.at[w, j, k], beside[k - 1],
                )
                copy.start()
                first[w, j, k] = copy
    second = {}
    for w in order:
        for j in tuple(range(1, slots)) + (0,):
            t = other(s, j, slots)
            for k in range(1, groups):
                first[w, j, k].wait_recv()
            total = part(w, t, d)[...].astype(F32)
            for k in range(1, groups):
                total = total + from_core[w][j, k - 1].astype(F32)
            if j:
                stage[w][j] = total.astype(BF16)
                copy = remote(stage[w].at[j], from_slot[w].at[j], xs.at[w, j], xr.at[w, j], across[j - 1])
                copy.start()
                second[w, j] = copy
            else:
                outs[w][: total.shape[0]] = total
    for w in order:
        for j in range(1, slots):
            second[w, j].wait_recv()
        total = outs[w][: from_slot[w].shape[1]]
        for j in range(1, slots):
            total = total + from_slot[w][j].astype(F32)
        outs[w][: total.shape[0]] = total
        if shared:
            from_z[m] = total.astype(BF16)
            third = [
                remote(from_z.at[m], from_z.at[m], zs.at[j], zr.at[j], above[j - 1])
                for j in range(1, stacks)
            ]
            for copy in third:
                copy.start()
    if shared:
        w = 0
        size = from_slot[w].shape[1]
        for copy in third:
            copy.wait()
        total = from_z[0].astype(F32)
        for j in range(1, stacks):
            total = total + from_z[j].astype(F32)
        own_c[...] = total.astype(BF16)
        fourth = [remote(own_c, from_c.at[k], ts.at[k], tr.at[k], beside[k - 1]) for k in range(1, groups)]
        for copy in fourth:
            copy.start()
        outs[w][pl.ds(pl.multiple_of(d * size, size), size), :] = own_c[...].astype(F32)
        for k in range(1, groups):
            fourth[k - 1].wait()
            outs[w][pl.ds(pl.multiple_of(origin(d, k, groups) * size, size), size), :] = from_c[k].astype(F32)
    for copy in first.values():
        copy.wait_send()
    for copy in second.values():
        copy.wait_send()


def scatter_grads(partials, columns, shared=False):
    sizes = tuple(lax.axis_size(axis) for axis in ("slot", "mp", "dp"))
    slots, stacks, groups = sizes
    count = len(partials)
    parts = slots * groups
    blocks = [
        (v.shape[0], v.shape[1] // parts) if c else (v.shape[0] // parts, v.shape[1])
        for v, c in zip(partials, columns)
    ]
    extents = tuple(b[1] if c else b[0] for b, c in zip(blocks, columns))
    shapes = [(b[0] * groups, b[1]) for b in blocks] if shared else blocks
    vm = pl.BlockSpec(memory_space=pltpu.VMEM)
    dma = pltpu.SemaphoreType.DMA
    last = blocks[-1]
    return pl.pallas_call(
        functools.partial(scatter_kernel, sizes, columns, extents, shared),
        out_shape=[jax.ShapeDtypeStruct(shape, F32) for shape in shapes],
        in_specs=[vm] * count,
        out_specs=[vm] * count,
        scratch_shapes=[pltpu.VMEM((slots, groups - 1) + b, BF16) for b in blocks]
        + [pltpu.VMEM((slots,) + b, BF16) for b in blocks]
        + [pltpu.VMEM((slots,) + b, BF16) for b in blocks]
        + [dma((count, slots, groups))] * 2
        + [dma((count, slots))] * 2
        + (
            [
                pltpu.VMEM((stacks,) + last, BF16),
                pltpu.VMEM(last, BF16), pltpu.VMEM((groups,) + last, BF16),
                dma((stacks,)), dma((stacks,)), dma((groups,)), dma((groups,)),
            ]
            if shared
            else []
        ),
        compiler_params=pltpu.CompilerParams(
            collective_id=4 if shared else 2, has_side_effects=True, vmem_limit_bytes=48 * 2**20
        ),
        cost_estimate=pl.CostEstimate(
            flops=10**6, bytes_accessed=(10 if shared else 120) * 10**6, transcendentals=0
        ),
        name="scatter_small" if shared else "scatter_grads",
    )(*partials)


def total_kernel(sizes, value, out, held_z, held_s, held_d, zs, zr, xs, xr, cs, cr):
    slots, stacks, groups = sizes
    across, beside = group_peers(slots, groups)
    above = stack_peers(stacks)
    greet(across + beside + above)
    total = value[...]
    for axis, peers, held, send, recv in (
        ("mp", above, held_z, zs, zr), ("slot", across, held_s, xs, xr), ("dp", beside, held_d, cs, cr)
    ):
        index = lax.axis_index(axis)
        held[index] = total
        copies = [
            remote(held.at[index], held.at[index], send.at[j], recv.at[j], peer)
            for j, peer in enumerate(peers)
        ]
        for copy in copies:
            copy.start()
        for copy in copies:
            copy.wait()
        total = held[0]
        for j in range(1, len(peers) + 1):
            total = total + held[j]
    out[...] = total


def total_of(value):
    sizes = tuple(lax.axis_size(axis) for axis in ("slot", "mp", "dp"))
    slots, stacks, groups = sizes
    vm = pl.BlockSpec(memory_space=pltpu.VMEM)
    dma = pltpu.SemaphoreType.DMA
    return pl.pallas_call(
        functools.partial(total_kernel, sizes),
        out_shape=jax.ShapeDtypeStruct(value.shape, F32),
        in_specs=[vm],
        out_specs=vm,
        scratch_shapes=[pltpu.VMEM((size,) + value.shape, F32) for size in (stacks, slots, groups)]
        + [dma((size,)) for size in (stacks, stacks, slots, slots, groups, groups)],
        compiler_params=pltpu.CompilerParams(collective_id=3, has_side_effects=True),
        name="total_of",
    )(value)


def pieces_of(size):
    return max(step for step in range(16, 129, 16) if size % step == 0)


def pack_layout():
    layout = []
    offset = 0
    for height, breadth in (
        (LD, 3 * LD), (LD, LFF), (LD, LD), (LFF, LD), (LD, VOCAB), (VOCAB, LD), (GSLOT, LD)
    ):
        layout.append((offset, height, breadth // 128))
        offset += height * breadth // 128
    return layout, offset


def unpack_kernel(share, rows, count, blocks_ref, *refs):
    outs, flat = refs[:-1], refs[-1]
    chunk = pieces_of(rows)
    flat[0:8, :] = jnp.zeros((8, 128), F32)

    def block(b, _):
        top = lax.div(b * share, 128)
        held = flat[pl.ds(top, 1), :]
        for i in range(0, rows, chunk):
            source = pl.ds(pl.multiple_of(b * rows, 16) + i, chunk)
            flat[pl.ds(top + i, chunk), :] = blocks_ref[source, :].astype(F32)
        flat[pl.ds(top, 1), :] = flat[pl.ds(top, 1), :] + held
        return 0

    lax.fori_loop(0, count, block, 0)
    layout, _ = pack_layout()
    for out, (offset, height, breadth) in zip(outs, layout):
        def part(i, _, out=out, offset=offset, breadth=breadth):
            for c in range(breadth):
                values = flat[pl.ds(offset + i * (128 * breadth) + c, 128, stride=breadth), :]
                out[pl.ds(pl.multiple_of(i * 128, 128), 128), c * 128 : (c + 1) * 128] = values.astype(BF16)
            return 0
        lax.fori_loop(0, height // 128, part, 0)


def unpack(blocks, share):
    rows = block_rows(share)
    count = blocks.shape[0] // rows
    layout, used = pack_layout()
    vm = pl.BlockSpec(memory_space=pltpu.VMEM)
    return pl.pallas_call(
        functools.partial(unpack_kernel, share, rows, count),
        out_shape=[jax.ShapeDtypeStruct((h, b * 128), BF16) for _, h, b in layout],
        in_specs=[vm],
        out_specs=[vm] * len(layout),
        scratch_shapes=[pltpu.VMEM((share * count // 128 + rows + 8, 128), F32)],
        compiler_params=pltpu.CompilerParams(vmem_limit_bytes=48 * 2**20),
        name="unpack",
    )(blocks)


def pack_kernel(share, rows, count, *refs):
    matrices, out, flat = refs[:-2], refs[-2], refs[-1]
    chunk = pieces_of(rows)
    layout, used = pack_layout()
    for matrix, (offset, height, breadth) in zip(matrices, layout):
        def part(i, _, matrix=matrix, offset=offset, breadth=breadth):
            for c in range(breadth):
                values = matrix[pl.ds(pl.multiple_of(i * 128, 128), 128), c * 128 : (c + 1) * 128]
                flat[pl.ds(offset + i * (128 * breadth) + c, 128, stride=breadth), :] = values.astype(F32)
            return 0
        lax.fori_loop(0, height // 128, part, 0)
    spare = flat.shape[0] - used
    flat[used:, :] = jnp.zeros((spare, 128), F32)

    def block(b, _):
        top = lax.div(b * share, 128)
        for i in range(0, rows, chunk):
            target = pl.ds(pl.multiple_of(b * rows, 16) + i, chunk)
            out[target, :] = flat[pl.ds(top + i, chunk), :].astype(BF16)
        return 0

    lax.fori_loop(0, count, block, 0)


def pack(matrices, share):
    rows = block_rows(share)
    layout, used = pack_layout()
    total = used + (D + 2 * LD) // 128
    count = total * 128 // share
    vm = pl.BlockSpec(memory_space=pltpu.VMEM)
    return pl.pallas_call(
        functools.partial(pack_kernel, share, rows, count),
        out_shape=jax.ShapeDtypeStruct((count * rows, 128), BF16),
        in_specs=[vm] * len(layout),
        out_specs=vm,
        scratch_shapes=[pltpu.VMEM((total + rows + 8, 128), F32)],
        compiler_params=pltpu.CompilerParams(vmem_limit_bytes=48 * 2**20),
        name="pack",
    )(*matrices)


def partner(index, offset, size):
    return index ^ offset if size & (size - 1) == 0 else (index + offset) % size


def swap(value, axis, offset):
    size = lax.axis_size(axis)
    if size & (size - 1) == 0:
        pairs = [(i, i ^ offset) for i in range(size)]
    else:
        pairs = [(i, (i + offset) % size) for i in range(size)]
    return lax.ppermute(value, axis, pairs)


def source(index, offset, size):
    return index ^ offset if size & (size - 1) == 0 else (index + size - offset) % size


def trade_rows(partial, axis):
    size = lax.axis_size(axis)
    index = lax.axis_index(axis)
    share = partial.shape[0] // size
    pieces = []
    for offset in range(1, size):
        block = lax.dynamic_slice_in_dim(partial, partner(index, offset, size) * share, share, 0)
        pieces.append(swap(block.astype(BF16), axis, offset))
    return lax.dynamic_slice_in_dim(partial, index * share, share, 0), pieces


def share_rows(block, axis):
    return [block] + [swap(block, axis, offset) for offset in range(1, lax.axis_size(axis))]


def shift_chunks(value, distance, forward):
    size = lax.axis_size("slot")
    if forward:
        pairs = [(i, i + distance) for i in range(size - distance)]
    else:
        pairs = [(i + distance, i) for i in range(size - distance)]
    return lax.ppermute(value, "slot", pairs)


def update(weight, moment, average, gradient, factor, rate):
    step_grad = factor * gradient
    moment_next = momentum_keep * moment + step_grad
    weight_next = weight - rate * (step_grad + momentum_keep * moment_next)
    average_next = average_keep * average + (1.0 - average_keep) * weight_next
    return (weight_next, moment_next, average_next)


def block_rows(share):
    return -(-(-(-share // 128) + 1) // 16) * 16


def gather_pack(local_pack):
    share = local_pack.shape[0]
    index = lax.axis_index(("slot", "mp", "dp"))
    offset = lax.rem(index * share, 128)
    rows = block_rows(share)
    block = lax.dynamic_update_slice_in_dim(
        jnp.zeros((rows * 128,), BF16), local_pack.astype(BF16), offset, 0
    )
    return lax.all_gather(block.reshape(rows, 128), ("slot", "mp", "dp"), axis=0, tiled=True)


def scatter_pack(blocks, share):
    own = lax.psum_scatter(blocks, ("slot", "mp", "dp"), scatter_dimension=0, tiled=True)
    index = lax.axis_index(("slot", "mp", "dp"))
    offset = lax.rem(index * share, 128)
    return lax.dynamic_slice_in_dim(own.reshape(-1), offset, share, 0).astype(F32)


def local(
    byte_ids, item_ids, loss_mask,
    attend_in, expand_in, attend_out, expand_out, slot_table, local_pack,
    moment_attend_in, moment_expand_in, moment_attend_out, moment_expand_out,
    moment_slot_table, moment_local_pack,
    average_attend_in, average_expand_in, average_attend_out, average_expand_out,
    average_slot_table, average_local_pack,
):
    slot_size, mp_size = lax.axis_size("slot"), lax.axis_size("mp")
    slot_index, mp_index, dp_index = (
        lax.axis_index("slot"), lax.axis_index("mp"), lax.axis_index("dp"),
    )
    counted = jnp.full((8, 128), jnp.sum(loss_mask.astype(F32)))
    width = attend_in.shape[2]
    piece = slot_table.shape[0] * VOCAB // lax.axis_size("dp")
    table_shard = lax.dynamic_slice_in_dim(
        slot_table.reshape(-1, GSLOT), dp_index * piece, piece, 0
    )
    tail = local_pack[-(D + 2 * LD) :].reshape(-1, 128)
    shards = [table_shard, jnp.transpose(attend_in, (1, 0, 2)), expand_in]
    late = [attend_out, expand_out]
    wide = attend_out.shape[1] % 128 == 0
    if wide:
        table, full_in_flat, full_expand, full_out, full_shrink, gains, counted = gather_weights(
            shards + late, (False, False, False, True, True), tail, counted
        )
    else:
        table, full_in_flat, full_expand, gains, counted = gather_weights(
            shards, (False, False, False), tail, counted
        )
        full_out, full_shrink = (
            lax.all_gather(v.astype(BF16), ("slot", "dp"), axis=1, tiled=True) for v in late
        )
    local_pack_later, gains = lax.optimization_barrier((local_pack, gains))
    pack_whole = gather_pack(local_pack_later)
    gains = gains.reshape(-1)
    mask_count = counted[0, 0]
    gain_global = gains[:D]
    local_gains = gains[D:].reshape(2, LD)
    unpacked = unpack(pack_whole, local_pack.shape[0])
    group_rows = byte_ids.shape[1]
    rows = group_rows // slot_size
    local_rows = rows // mp_size
    vocab_ids = jnp.arange(VOCAB)
    reach = min(slot_size - 1, -(-(longest_item - 1) // rows))
    micros = []
    for micro in range(byte_ids.shape[0]):
        forward = micro % 2 == 0
        chunk = slot_index if forward else slot_size - 1 - slot_index
        group_ids = byte_ids[micro]
        items = item_ids[micro, 0]
        begin = chunk * rows
        previous = jnp.concatenate([jnp.full((1, SLOTS), -1, jnp.int32), group_ids[:-1]], axis=0)
        earlier_item = jnp.concatenate([items[:1], items[:-1]])
        previous = jnp.where((items == earlier_item)[:, None], previous, -1)
        own_previous = lax.dynamic_slice_in_dim(previous, begin, rows, 0)
        own_items = lax.dynamic_slice_in_dim(items, begin, rows, 0)
        first = jnp.sum((items[None, :] < own_items[:, None]).astype(jnp.int32), axis=1)
        first = jnp.maximum(first - (chunk - reach) * rows, 0)
        start_rows, hidden, projected, own_kv = embed_rows(
            own_previous, table, full_in_flat, gain_global[None]
        )
        earlier = [shift_chunks(own_kv, d, forward) for d in range(1, reach + 1)]
        expanded = product(hidden, full_expand)
        active = gelu_tanh(expanded).astype(BF16)
        begin_local = begin + mp_index * local_rows
        micros.append(dict(
            forward=forward, group_ids=group_ids, begin_local=begin_local, start_rows=start_rows,
            hidden=hidden, projected=projected, earlier=earlier,
            expanded=expanded, active=active, low=first[::BLK] // BLK,
            first=first.reshape(-1, 1, BLK), own_previous=own_previous, mask=loss_mask[micro],
        ))
    for m in micros:
        m["attended"], m["lse"] = attention_fwd(m["low"], m["first"], m["projected"], m["earlier"])
        m["own"], m["pieces"] = trade_rows(
            product(m["attended"], full_out) + product(m["active"], full_shrink), "mp"
        )
        m["own_start"] = lax.dynamic_slice_in_dim(
            m["start_rows"], mp_index * local_rows, local_rows, 0
        )
    base = None
    for m in micros:
        ids = lax.dynamic_slice_in_dim(m["group_ids"], m["begin_local"], local_rows, 0)
        mask = lax.dynamic_slice_in_dim(m["mask"], m["begin_local"], local_rows, 0)
        out = byte_layer(
            m["own_start"], m["own"], m["pieces"], ids, mask, mask_count.reshape(1, 1),
            unpacked[:7], local_gains, base,
        )
        base = out[:9]
        m["own_back"] = out[9]
        m["branch_pieces"] = share_rows(out[9], "mp")
    matrices, local_gain_grads, loss_sum = base[:7], base[7], base[8][0, 0]
    sums = None
    table_grad = None
    gain_global_grad = None
    for m in micros:
        branch_grad, m["query_grad"], m["kv_grads"] = attention_bwd(
            m["low"], m["first"], m["projected"], m["earlier"], m["attended"], m["lse"],
            full_out, m["branch_pieces"],
        )
        m["branch_grad"] = branch_grad
        m["returned"] = [
            shift_chunks(m["kv_grads"][d], d, not m["forward"]) for d in range(1, reach + 1)
        ]
        m["expanded_grad"] = gelu_back(
            m["expanded"], back_product(branch_grad, full_shrink)
        ).astype(BF16)
    for m in micros:
        kv_total = m["kv_grads"][0].astype(F32)
        for value in m["returned"]:
            kv_total = kv_total + value.astype(F32)
        m["projected_grad"] = jnp.concatenate([m["query_grad"], kv_total.astype(BF16)], axis=1)
        m["partial"] = back_product(m["projected_grad"], full_in_flat) + back_product(
            m["expanded_grad"], full_expand
        )
        m["back"] = trade_rows(m["partial"], "mp")
    sums = None
    for m in micros:
        terms = (
            gram_product(m["hidden"], m["projected_grad"]),
            gram_product(m["hidden"], m["expanded_grad"]),
            gram_product(m["attended"], m["branch_grad"]),
            gram_product(m["active"], m["branch_grad"]),
        )
        sums = terms if sums is None else tuple(a + b for a, b in zip(sums, terms))
    sums = tuple(s.astype(BF16) for s in sums)
    if wide:
        sums, _ = lax.optimization_barrier((sums, [m["back"][0] for m in micros]))
        own_in, own_expand, own_out, own_shrink = scatter_grads(sums, (False, False, True, True))
    else:
        own_in, own_expand = scatter_grads(sums[:2], (False, False))
        own_out, own_shrink = (
            lax.psum_scatter(v, ("slot", "dp"), scatter_dimension=1, tiled=True).astype(F32)
            for v in sums[2:]
        )
    backs, own_in = lax.optimization_barrier(([m["back"] for m in micros], own_in))
    table_grad = None
    for m, (hidden_grad, pieces) in zip(micros, backs):
        for value in pieces:
            hidden_grad = hidden_grad + value.astype(F32)
        _, scaled, factor = norm_forward(m["own_start"].astype(F32), gain_global)
        gain_term = jnp.sum(hidden_grad * scaled, axis=0)
        start_grad = (
            m["own_back"].astype(F32) + norm_backward(scaled, factor, gain_global, hidden_grad)
        ).astype(BF16)
        own_lookup = lax.dynamic_slice_in_dim(m["own_previous"], mp_index * local_rows, local_rows, 0)
        own_lookup = (own_lookup[:, :, None] == vocab_ids).astype(BF16)
        table_term = jnp.einsum(
            "pjv,pjg->jvg", own_lookup, start_grad.reshape(local_rows, SLOTS, GSLOT),
            preferred_element_type=F32,
        )
        if table_grad is None:
            table_grad, gain_global_grad = table_term, gain_term
        else:
            table_grad = table_grad + table_term
            gain_global_grad = gain_global_grad + gain_term
    gain_grads = jnp.concatenate([gain_global_grad, local_gain_grads.reshape(-1)])
    parts = slot_size * lax.axis_size("dp")
    small = jnp.concatenate(
        [
            table_grad.astype(BF16).reshape(parts, -1, GSLOT),
            jnp.broadcast_to(gain_grads.astype(BF16).reshape(1, -1, GSLOT), (parts, 16, GSLOT)),
        ],
        axis=1,
    ).reshape(-1, GSLOT)
    own_small = scatter_grads([small], (False,), True)[0]
    own_in = own_in.reshape(attend_in.shape)
    own_small = own_small.reshape(lax.axis_size("dp"), piece + 16, GSLOT)
    own_table = own_small[:, :piece].reshape(slot_table.shape)
    gain_total = own_small[0, piece:].reshape(-1)
    own_pack = scatter_pack(pack(matrices, local_pack.shape[0]), local_pack.shape[0])
    last = (slot_index == slot_size - 1) & (mp_index == mp_size - 1)
    last = last & (dp_index == lax.axis_size("dp") - 1)
    own_pack = jnp.concatenate(
        [own_pack[: -gain_total.shape[0]], jnp.where(last, gain_total, own_pack[-gain_total.shape[0] :])]
    )
    owner = ((mp_index == 0) & (dp_index == 0)).astype(F32)
    squares = jnp.sum(own_pack * own_pack) + owner * jnp.sum(own_table * own_table)
    for gradient in (own_in, own_expand, own_out, own_shrink):
        squares = squares + jnp.sum(gradient * gradient)
    both = total_of(jnp.stack([jnp.full((8, 128), squares), jnp.full((8, 128), loss_sum)]))
    total_squares, loss_value = both[0, 0, 0], both[1, 0, 0]
    clip_norm = jnp.sqrt(total_squares)
    factor = clip_max / jnp.maximum(clip_norm, clip_max)
    results = [loss_value * mask_count, mask_count, clip_norm]
    for weight, moment, average, gradient, rate in (
        (attend_in, moment_attend_in, average_attend_in, own_in, rate_dense),
        (expand_in, moment_expand_in, average_expand_in, own_expand, rate_dense),
        (attend_out, moment_attend_out, average_attend_out, own_out, rate_project),
        (expand_out, moment_expand_out, average_expand_out, own_shrink, rate_dense),
        (slot_table, moment_slot_table, average_slot_table, own_table, rate_table),
        (local_pack, moment_local_pack, average_local_pack, own_pack, rate_dense),
    ):
        results.extend(update(weight, moment, average, gradient, factor, rate))
    return tuple(results)


def solution(mesh):
    placed = (
        P(None, "dp", None),
        P(None, "dp", None),
        P(None, "dp", None),
        P(("slot", "dp"), None, "mp"),
        P(("slot", "dp"), "mp"),
        P("mp", ("slot", "dp")),
        P("mp", ("slot", "dp")),
        P("slot", None, None),
        P(("slot", "mp", "dp")),
        P(("slot", "dp"), None, "mp"),
        P(("slot", "dp"), "mp"),
        P("mp", ("slot", "dp")),
        P("mp", ("slot", "dp")),
        P("slot", None, None),
        P(("slot", "mp", "dp")),
        P(("slot", "dp"), None, "mp"),
        P(("slot", "dp"), "mp"),
        P("mp", ("slot", "dp")),
        P("mp", ("slot", "dp")),
        P("slot", None, None),
        P(("slot", "mp", "dp")),
    )
    return jax.shard_map(
        local,
        mesh=mesh,
        in_specs=placed,
        out_specs=(
            P(),
            P(),
            P(),
            P(("slot", "dp"), None, "mp"),
            P(("slot", "dp"), None, "mp"),
            P(("slot", "dp"), None, "mp"),
            P(("slot", "dp"), "mp"),
            P(("slot", "dp"), "mp"),
            P(("slot", "dp"), "mp"),
            P("mp", ("slot", "dp")),
            P("mp", ("slot", "dp")),
            P("mp", ("slot", "dp")),
            P("mp", ("slot", "dp")),
            P("mp", ("slot", "dp")),
            P("mp", ("slot", "dp")),
            P("slot", None, None),
            P("slot", None, None),
            P("slot", None, None),
            P(("slot", "mp", "dp")),
            P(("slot", "mp", "dp")),
            P(("slot", "mp", "dp")),
        ),
        check_vma=False,
    )
```

```python
import functools
import types

import jax
import jax.numpy as jnp
from jax import lax
from jax.experimental import pallas as pl
from jax.experimental.pallas import tpu as pltpu
from jax.sharding import PartitionSpec as P

D = 1024
LD = 512
LH = 8
LFF = 2048
VOCAB = 256
SLOTS = 8
HEADDIM = 64
LHEADDIM = 64
GSLOT = 128
BLK = 256
ITEMS = 5
F32 = jnp.float32
BF16 = jnp.bfloat16
MESH = pl.DeviceIdType.MESH
SLOT, STACK, CORE = "slot", "mp", "dp"

longest_item = 1024


epsilon = 1e-06
clip_max = 0.01
momentum_keep = 0.9
average_keep = 0.9
rate_dense = 3000.0
rate_table = 60000.0
rate_project = 15000.0
masked_score = -1e30


def product(left, right):
    return jnp.dot(left, right, preferred_element_type=jnp.float32)


def gram_product(left, right):
    return lax.dot_general(
        left, right, (((0,), (0,)), ((), ())), preferred_element_type=jnp.float32
    )


def back_product(left, right):
    return lax.dot_general(
        left, right, (((1,), (1,)), ((), ())), preferred_element_type=jnp.float32
    )


def gelu_tanh(values):
    return jax.nn.gelu(values, approximate=True)


def gelu_back(values, gradient):
    return jax.vjp(gelu_tanh, values)[1](gradient)[0]


def norm_forward(values, gain):
    factor = lax.rsqrt(jnp.mean(values * values, axis=-1, keepdims=True) + epsilon)
    scaled = values * factor
    return (scaled * gain, scaled, factor)


def norm_backward(scaled, factor, gain, gradient):
    inner = gradient * gain
    return factor * (inner - scaled * jnp.mean(inner * scaled, axis=-1, keepdims=True))


def split_pack(packed):
    layouts = (
        (LD, 3 * LD),
        (LD, LFF),
        (LD, LD),
        (LFF, LD),
        (LD, VOCAB),
        (VOCAB, LD),
        (GSLOT, LD),
        (D + 2 * LD,),
    )
    pieces = []
    offset = 0
    for layout in layouts:
        length = 1
        for extent in layout:
            length = length * extent
        pieces.append(packed[offset : offset + length].reshape(layout))
        offset = offset + length
    return pieces


def mm(a, b):
    return lax.dot_general(a, b, (((1,), (0,)), ((), ())), preferred_element_type=F32)


def mm_tn(a, b):
    return lax.dot_general(a, b, (((0,), (0,)), ((), ())), preferred_element_type=F32)


def mm_nt(a, b):
    return lax.dot_general(a, b, (((1,), (1,)), ((), ())), preferred_element_type=F32)


def stack_heads(x):
    lane = lax.broadcasted_iota(jnp.int32, x.shape, 1)
    zero = jnp.zeros_like(x)
    return jnp.concatenate([jnp.where(lane < 64, x, zero), jnp.where(lane < 64, zero, x)], axis=0)


def window_fill(rows, width, own_ref, earlier, keys, values_t, values, keys_t):
    for place, ref in enumerate(earlier):
        at = (len(earlier) - 1 - place) * rows
        if keys is not None:
            keys[at : at + rows, :] = ref[:, :width]
        if values is not None:
            values[at : at + rows, :] = ref[:, width:]
        if values_t is not None:
            values_t[:, at : at + rows] = jnp.transpose(ref[:, width:])
        if keys_t is not None:
            keys_t[:, at : at + rows] = jnp.transpose(ref[:, :width])
    at = len(earlier) * rows
    if keys is not None:
        keys[at : at + rows, :] = own_ref[:, width : 2 * width]
    if values is not None:
        values[at : at + rows, :] = own_ref[:, 2 * width :]
    if values_t is not None:
        values_t[:, at : at + rows] = jnp.transpose(own_ref[:, 2 * width :])
    if keys_t is not None:
        keys_t[:, at : at + rows] = jnp.transpose(own_ref[:, width : 2 * width])


def chunk_begin(forward, rows):
    slot, slots = lax.axis_index(SLOT), lax.axis_size(SLOT)
    return (slot if forward else slots - 1 - slot) * rows


def item_starts(items_ref, micro, begin, rows, reach):
    items = items_ref[micro]
    starts = []
    for qt in range(rows // BLK):
        own = items_ref[micro, :, pl.ds(pl.multiple_of(begin + qt * BLK, BLK), BLK)]
        first = jnp.zeros((1, BLK), F32)
        for value in range(1, ITEMS):
            ahead = jnp.sum(jnp.where(items < value, 1.0, 0.0), axis=1, keepdims=True)
            first = jnp.where(own == value, ahead, first)
        first = jnp.maximum(first - (begin - reach * rows).astype(F32), 0.0)
        low = lax.div(jnp.min(first).astype(jnp.int32), BLK)
        first = first.astype(jnp.int32)
        starts.append((jnp.concatenate([first, first], axis=1), low))
    return starts


def fwd_kernel(rows, width, count, micro, forward, items_ref, own_ref, *rest):
    earlier, (att_ref, lse_ref, keys, values_t) = rest[:count], rest[count:]
    window_fill(rows, width, own_ref, earlier, keys, values_t, None, None)
    starts = item_starts(items_ref, micro, chunk_begin(forward, rows), rows, count)
    base = count * rows
    key_iota = lax.broadcasted_iota(jnp.int32, (BLK, 2 * BLK), 0)
    q_iota = lax.broadcasted_iota(jnp.int32, (1, 2 * BLK), 1) % BLK
    pairs = width // 128
    for qt in range(rows // BLK):
        q_pos = q_iota + (base + qt * BLK)
        start, low = starts[qt]
        for pair in range(pairs):
            cs = slice(pair * 128, pair * 128 + 128)
            qs = stack_heads(own_ref[qt * BLK : (qt + 1) * BLK, cs] * jnp.asarray(0.125, BF16))

            def block(i, carry):
                top, total, acc = carry
                kb = base // BLK + qt - i
                at = pl.ds(pl.multiple_of(kb * BLK, BLK), BLK)
                s = mm_nt(keys[at, cs], qs)
                pos = key_iota + kb * BLK
                s = jnp.where((pos >= start) & (pos <= q_pos), s, masked_score)
                new = jnp.maximum(top, jnp.max(s, axis=0, keepdims=True))
                p = jnp.exp(s - new)
                alpha = jnp.exp(top - new)
                total = total * alpha + jnp.sum(p, axis=0, keepdims=True)
                acc = acc * alpha + mm(values_t[cs, at], p.astype(BF16))
                return new, total, acc

            init = (
                jnp.full((1, 2 * BLK), masked_score, F32),
                jnp.zeros((1, 2 * BLK), F32),
                jnp.zeros((128, 2 * BLK), F32),
            )
            top, total, acc = lax.fori_loop(0, base // BLK + qt + 1 - low, block, init)
            acc = acc * (1.0 / total)
            sub = lax.broadcasted_iota(jnp.int32, (128, BLK), 0)
            both = jnp.where(sub < 64, acc[:, :BLK], acc[:, BLK:])
            att_ref[qt * BLK : (qt + 1) * BLK, cs] = jnp.transpose(both).astype(BF16)
            lse_ref[qt * pairs + pair] = top + jnp.log(total)


def bwd_kernel(rows, width, count, pieces, micro, forward, items_ref, own_ref, *rest):
    earlier = rest[:count]
    att_ref, lse_ref, weight_ref = rest[count : count + 3]
    rest = rest[count + 3 :]
    piece_refs, rest = rest[:pieces], rest[pieces:]
    branch_ref, dq_ref, dkv_refs = rest[0], rest[1], rest[2 : count + 3]
    keys, values, keys_t, dkeys, dvalues, attg_ref = rest[count + 3 :]
    place, share = lax.axis_index(STACK), rows // pieces
    for j in range(pieces):
        at = pl.ds(pl.multiple_of(origin(place, j, pieces) * share, share), share)
        branch_ref[at, :] = piece_refs[j][...]
    attg_ref[...] = mm_nt(branch_ref[...], weight_ref[...]).astype(BF16)
    window_fill(rows, width, own_ref, earlier, keys, None, values, keys_t)
    starts = item_starts(items_ref, micro, chunk_begin(forward, rows), rows, count)
    base = count * rows
    dkeys[...] = jnp.zeros_like(dkeys)
    dvalues[...] = jnp.zeros_like(dvalues)
    key_iota = lax.broadcasted_iota(jnp.int32, (BLK, 2 * BLK), 0)
    q_iota = lax.broadcasted_iota(jnp.int32, (1, 2 * BLK), 1) % BLK
    pairs = width // 128
    for qt in range(rows // BLK):
        q_pos = q_iota + (base + qt * BLK)
        start, low = starts[qt]
        rq = slice(qt * BLK, (qt + 1) * BLK)
        for pair in range(pairs):
            cs = slice(pair * 128, pair * 128 + 128)
            qs = stack_heads(own_ref[rq, cs] * jnp.asarray(0.125, BF16))
            das = stack_heads(attg_ref[rq, cs])
            att = att_ref[rq, cs]
            both = jnp.concatenate([att, att], axis=0).astype(F32) * das.astype(F32)
            delta = jnp.sum(jnp.transpose(both), axis=0, keepdims=True)
            lse = lse_ref[qt * pairs + pair]

            def block(i, acc):
                kb = base // BLK + qt - i
                at = pl.ds(pl.multiple_of(kb * BLK, BLK), BLK)
                s = mm_nt(keys[at, cs], qs)
                pos = key_iota + kb * BLK
                p = jnp.where((pos >= start) & (pos <= q_pos), jnp.exp(s - lse), 0.0)
                dp = mm_nt(values[at, cs], das)
                ds = (p * (dp - delta)).astype(BF16)
                dkeys[at, cs] += mm(ds, qs)
                dvalues[at, cs] += mm(p.astype(BF16), das)
                return acc + mm(keys_t[cs, at], ds)

            acc = lax.fori_loop(
                0, base // BLK + qt + 1 - low, block, jnp.zeros((128, 2 * BLK), F32)
            )
            sub = lax.broadcasted_iota(jnp.int32, (128, BLK), 0)
            both = jnp.where(sub < 64, acc[:, :BLK], acc[:, BLK:]) * 0.125
            dq_ref[rq, cs] = jnp.transpose(both).astype(BF16)
    for place in range(count + 1):
        at = (count - place) * rows
        dkv_refs[place][:, :width] = dkeys[at : at + rows, :].astype(BF16)
        dkv_refs[place][:, width:] = dvalues[at : at + rows, :].astype(BF16)


def specs(n):
    return [pl.BlockSpec(memory_space=pltpu.VMEM)] * n


def attention_fwd(items, micro, forward, own, earlier):
    rows, width = own.shape[0], own.shape[1] // 3
    count = len(earlier)
    span = (count + 1) * rows
    units = rows // BLK * (width // 128)
    return pl.pallas_call(
        functools.partial(fwd_kernel, rows, width, count, micro, forward),
        out_shape=[
            jax.ShapeDtypeStruct((rows, width), BF16),
            jax.ShapeDtypeStruct((units, 1, 2 * BLK), F32),
        ],
        in_specs=specs(2 + count),
        out_specs=[pl.BlockSpec(memory_space=pltpu.VMEM)] * 2,
        scratch_shapes=[pltpu.VMEM((span, width), BF16), pltpu.VMEM((width, span), BF16)],
        cost_estimate=pl.CostEstimate(flops=6 * 10**9, bytes_accessed=20 * 10**6, transcendentals=10**6),
        compiler_params=pltpu.CompilerParams(vmem_limit_bytes=32 * 2**20),
        name="patch_attention",
    )(items, own, *earlier)


def attention_bwd(items, micro, forward, own, earlier, attended, lse, weight, pieces):
    rows, width = own.shape[0], own.shape[1] // 3
    count = len(earlier)
    span = (count + 1) * rows
    out = pl.pallas_call(
        functools.partial(bwd_kernel, rows, width, count, len(pieces), micro, forward),
        out_shape=[jax.ShapeDtypeStruct((rows, pieces[0].shape[1]), BF16), jax.ShapeDtypeStruct((rows, width), BF16)]
        + [jax.ShapeDtypeStruct((rows, 2 * width), BF16)] * (count + 1),
        in_specs=specs(5 + count + len(pieces)),
        out_specs=[pl.BlockSpec(memory_space=pltpu.VMEM)] * (count + 3),
        scratch_shapes=[
            pltpu.VMEM((span, width), BF16),
            pltpu.VMEM((span, width), BF16),
            pltpu.VMEM((width, span), BF16),
            pltpu.VMEM((span, width), F32),
            pltpu.VMEM((span, width), F32),
            pltpu.VMEM((rows, width), BF16),
        ],
        cost_estimate=pl.CostEstimate(flops=8 * 10**9, bytes_accessed=25 * 10**6, transcendentals=10**6),
        compiler_params=pltpu.CompilerParams(vmem_limit_bytes=32 * 2**20),
        name="patch_attention_back",
    )(items, own, *earlier, attended, lse, weight, *pieces)
    return out[0], out[1], out[2:]


def embed_kernel(
    width, rows, micro, forward, ids_ref, items_ref, table_ref, w_ref, gain_ref,
    start_ref, hidden_ref, proj_ref, kv_ref, previous_ref,
):
    begin = pl.multiple_of(chunk_begin(forward, rows), 128)
    edge = pl.multiple_of(jnp.maximum(begin - 128, 0), 128)

    def delayed(ref):
        own, before = ref[micro, :, pl.ds(begin, rows)], ref[micro, :, pl.ds(edge, 128)]
        place = lax.broadcasted_iota(jnp.int32, own.shape, 1)
        return own, jnp.where(place == 0, before[:, 127:128], pltpu.roll(own, 1, axis=1))

    own_items, earlier_items = delayed(items_ref)
    place = lax.broadcasted_iota(jnp.int32, own_items.shape, 1)
    keep = (own_items == earlier_items) & ((place > 0) | (begin > 0))
    ids = jnp.where(keep, delayed(ids_ref)[1], -1).astype(F32)
    ids = jnp.transpose(ids)
    previous_ref[...] = ids.astype(jnp.int32)
    low = lax.broadcasted_iota(jnp.int32, (rows, 128), 1).astype(F32)
    squares = jnp.zeros((rows, 1), F32)
    parts = []
    for j in range(SLOTS):
        own = jnp.broadcast_to(ids[:, j : j + 1], (rows, 128))
        hot = jnp.concatenate(
            [jnp.where(own == low, 1.0, 0.0), jnp.where(own == low + 128.0, 1.0, 0.0)], axis=1
        ).astype(BF16)
        part = mm(hot, table_ref[j * VOCAB : (j + 1) * VOCAB, :])
        parts.append(part)
        squares = squares + jnp.sum(part * part, axis=-1, keepdims=True)
    factor = lax.rsqrt(squares * (1.0 / D) + epsilon)
    for j in range(SLOTS):
        cs = slice(j * GSLOT, (j + 1) * GSLOT)
        start_ref[:, cs] = parts[j].astype(BF16)
        hidden_ref[:, cs] = (parts[j] * factor * gain_ref[:, cs]).astype(BF16)
    hidden = hidden_ref[...]
    for c in range(3):
        cs = slice(c * width, (c + 1) * width)
        part = mm(hidden, w_ref[:, cs]).astype(BF16)
        proj_ref[:, cs] = part
        if c:
            kv_ref[:, (c - 1) * width : c * width] = part


def embed_rows(ids, items, micro, forward, rows, table, weight, gain):
    width = weight.shape[1] // 3
    vm = pl.BlockSpec(memory_space=pltpu.VMEM)
    return pl.pallas_call(
        functools.partial(embed_kernel, width, rows, micro, forward),
        out_shape=[
            jax.ShapeDtypeStruct((rows, D), BF16),
            jax.ShapeDtypeStruct((rows, D), BF16),
            jax.ShapeDtypeStruct((rows, 3 * width), BF16),
            jax.ShapeDtypeStruct((rows, 2 * width), BF16),
            jax.ShapeDtypeStruct((rows, SLOTS), jnp.int32),
        ],
        in_specs=[vm] * 5,
        out_specs=[vm] * 5,
        cost_estimate=pl.CostEstimate(flops=2 * 10**9, bytes_accessed=6 * 10**6, transcendentals=1000),
        compiler_params=pltpu.CompilerParams(vmem_limit_bytes=32 * 2**20),
        name="embed_rows",
    )(ids, items, table, weight, gain)


def up_kernel(count, *refs):
    hidden, weight, outs = refs[:count], refs[count], refs[count + 1 :]
    for i in range(count):
        for c in range(0, weight.shape[1], 256):
            value, slope = gelu_pair(mm(hidden[i][...], weight[:, c : c + 256]))
            outs[2 * i][:, c : c + 256] = value.astype(BF16)
            outs[2 * i + 1][:, c : c + 256] = slope.astype(BF16)


def up_rows(hidden, weight):
    count = len(hidden)
    vm = pl.BlockSpec(memory_space=pltpu.VMEM)
    shape = jax.ShapeDtypeStruct((hidden[0].shape[0], weight.shape[1]), BF16)
    out = pl.pallas_call(
        functools.partial(up_kernel, count),
        out_shape=[shape] * (2 * count),
        in_specs=[vm] * (count + 1),
        out_specs=[vm] * (2 * count),
        cost_estimate=pl.CostEstimate(flops=4 * 10**9, bytes_accessed=10**7, transcendentals=10**6),
        compiler_params=pltpu.CompilerParams(vmem_limit_bytes=32 * 2**20),
        name="up_rows",
    )(*hidden, weight)
    return [(out[2 * i], out[2 * i + 1]) for i in range(count)]


def gelu_pair(x):
    c = 0.7978845608028654
    x2 = x * x
    t = jnp.tanh(c * (x + 0.044715 * (x2 * x)))
    half = 0.5 * (1.0 + t)
    slope = half + (0.5 * c) * x * (1.0 - t * t) * (1.0 + (3 * 0.044715) * x2)
    return x * half, slope


def byte_kernel(
    rows, tile, with_base,
    pieces, micro, forward, slot_rows, start_ref, own_ref, *rest
):
    piece_refs, rest = rest[:pieces], rest[pieces:]
    ids_ref, mask_ref, count_ref, w_in, w_up, w_out, w_down, w_head, w_embed, w_bridge, gains_ref = rest[:11]
    rest = rest[11:]
    if with_base:
        base, rest = rest[:9], rest[9:]
    else:
        base = None
    (g_in, g_up, g_out, g_down, g_head, g_embed, g_bridge, g_gain, loss_ref, inputg_ref,
     hid, proj, probs, att, act, slope, fin, lgrad, bgrad, egrad, attg, projg, sgrad, startv, att_t, projg_t,
     wide_rows, own_ids, prev_ids, weights, inputs_ref) = rest
    steps = rows // tile
    blocks = tile // 128
    g_gain_local = gains_ref[0:1, :]
    g_gain_final = gains_ref[1:2, :]
    first = lax.broadcasted_iota(jnp.int32, (128, 128), 1) < 64
    lane = lax.broadcasted_iota(jnp.int32, (SLOTS, 256), 1) % 128
    patch = lane // SLOTS
    causal = lax.broadcasted_iota(jnp.int32, (SLOTS, 256), 0) <= lane % SLOTS
    none = jnp.zeros((SLOTS, 256), F32)
    patches = rows // SLOTS
    begin = chunk_begin(forward, slot_rows) + lax.axis_index(STACK) * patches
    here = pl.ds(pl.multiple_of(begin, 128), patches)
    ids = jnp.transpose(ids_ref[micro, :, here].astype(F32))
    counts = jnp.transpose(mask_ref[micro, :, here].astype(F32))
    for j in range(SLOTS):
        cs = slice(j * GSLOT, (j + 1) * GSLOT)
        at = pl.ds(j, patches, stride=SLOTS)
        total = own_ref[:, cs] + start_ref[:, cs].astype(F32)
        for piece in piece_refs:
            total = total + piece[:, cs].astype(F32)
        wide_rows[at, :] = total
        spread = functools.partial(jnp.broadcast_to, shape=(patches, 128))
        own_ids[at, :] = spread(ids[:, j : j + 1])
        prev_ids[at, :] = spread(ids[:, j - 1 : j]) if j else jnp.full((patches, 128), -1.0, F32)
        weights[at, :] = spread(counts[:, j : j + 1] / count_ref[0, 0])
    inputs_ref[...] = wide_rows[...].astype(BF16)

    def one_hot(ids):
        low = lax.broadcasted_iota(jnp.int32, ids.shape, 1).astype(F32)
        return jnp.concatenate(
            [jnp.where(ids == low, 1.0, 0.0), jnp.where(ids == low + 128.0, 1.0, 0.0)], axis=1
        )

    zero_low = jnp.zeros((128, 128), BF16)

    def stack(x):
        return jnp.concatenate([jnp.where(first, x, zero_low), jnp.where(first, zero_low, x)], axis=0)

    def narrow(x):
        out = x[:SLOTS]
        for j in range(1, 16):
            out = jnp.where(patch == j, x[j * SLOTS : (j + 1) * SLOTS], out)
        return out

    def widen(x):
        return jnp.concatenate([jnp.where(patch == j, x, none) for j in range(16)], axis=0)

    def norm(v):
        factor = lax.rsqrt(jnp.mean(v * v, axis=-1, keepdims=True) + epsilon)
        return v * factor, factor

    def step(t, carry):
        loss, gl, gf = carry
        at = pl.ds(pl.multiple_of(t * tile, tile), tile)
        inputs = inputs_ref[at, :]
        weighting = weights[at, :]
        lookup = one_hot(prev_ids[at, :]).astype(BF16)
        start = mm(inputs, w_bridge[...]) + mm(lookup, w_embed[...])
        startv[...] = start
        scaled, factor = norm(start)
        hidden = (scaled * g_gain_local).astype(BF16)
        hid[at, :] = hidden
        for c in range(3):
            proj[:, c * LD : (c + 1) * LD] = mm(hidden, w_in[:, c * LD : (c + 1) * LD]).astype(BF16)

        def attend(b, _):
            ra = pl.ds(b * 128 if isinstance(b, int) else pl.multiple_of(b * 128, 128), 128)
            for pair in range(4):
                cs = slice(pair * 128, pair * 128 + 128)
                qs = stack(proj[ra, cs] * jnp.asarray(0.125, BF16))
                kp = proj[ra, LD + pair * 128 : LD + pair * 128 + 128]
                vp = proj[ra, 2 * LD + pair * 128 : 2 * LD + pair * 128 + 128]
                s = jnp.where(causal, narrow(mm_nt(kp, qs)), masked_score)
                e = jnp.exp(s - jnp.max(s, axis=0, keepdims=True))
                p = e * (1.0 / jnp.sum(e, axis=0, keepdims=True))
                probs[b * 4 + pair] = p
                flipped = jnp.transpose(widen(p).astype(BF16))
                wide = jnp.concatenate([flipped[:128], flipped[128:]], axis=1)
                att_t[ra, cs] = mm(wide, stack(vp)).astype(BF16)
            return 0

        def two(i, _):
            attend(2 * i, 0)
            return attend(2 * i + 1, 0)

        lax.fori_loop(0, blocks // 2, two, 0)
        attended = att_t[...]
        att[at, :] = attended
        after = start + mm(attended, w_out[...])
        for c in range(4):
            cs = slice(c * 512, c * 512 + 512)
            a, s = gelu_pair(mm(hidden, w_up[:, cs]))
            a = a.astype(BF16)
            act[at, cs] = a
            slope[:, cs] = s.astype(BF16)
            after = after + mm(a, w_down[cs, :])
        scaled_f, factor_f = norm(after)
        final = (scaled_f * g_gain_final).astype(BF16)
        fin[at, :] = final
        logits = mm(final, w_head[...])
        hot = one_hot(own_ids[at, :])
        top = jnp.max(logits, axis=-1, keepdims=True)
        log_total = top + jnp.log(jnp.sum(jnp.exp(logits - top), axis=-1, keepdims=True))
        loss = loss + jnp.sum(
            weighting[:, :1] * (log_total - jnp.sum(logits * hot, axis=-1, keepdims=True)), axis=0, keepdims=True
        )
        lg = ((jnp.exp(logits - log_total) - hot) * jnp.concatenate([weighting, weighting], axis=1)).astype(BF16)
        lgrad[at, :] = lg
        fg = mm_nt(lg, w_head[...])
        gf = gf + jnp.sum(fg * scaled_f, axis=0, keepdims=True)
        inner = fg * g_gain_final
        after_grad = factor_f * (inner - scaled_f * jnp.mean(inner * scaled_f, axis=-1, keepdims=True))
        bg = after_grad.astype(BF16)
        bgrad[at, :] = bg
        attg[...] = mm_nt(bg, w_out[...]).astype(BF16)
        hg = None
        for c in range(4):
            cs = slice(c * 512, c * 512 + 512)
            eg = (slope[:, cs] * mm_nt(bg, w_down[cs, :])).astype(BF16)
            egrad[at, cs] = eg
            term = mm_nt(eg, w_up[:, cs])
            hg = term if hg is None else hg + term

        def attend_back(b, _):
            ra = pl.ds(b * 128 if isinstance(b, int) else pl.multiple_of(b * 128, 128), 128)
            for pair in range(4):
                cs = slice(pair * 128, pair * 128 + 128)
                qs = stack(proj[ra, cs] * jnp.asarray(0.125, BF16))
                kp = proj[ra, LD + pair * 128 : LD + pair * 128 + 128]
                vp = proj[ra, 2 * LD + pair * 128 : 2 * LD + pair * 128 + 128]
                das = stack(attg[ra, cs])
                p = probs[b * 4 + pair]
                dp = narrow(mm_nt(vp, das))
                ds = widen(p * (dp - jnp.sum(p * dp, axis=0, keepdims=True)))
                flipped = jnp.transpose(ds.astype(BF16))
                wide = jnp.concatenate([flipped[:128], flipped[128:]], axis=1)
                projg_t[ra, cs] = (mm(wide, stack(kp)) * 0.125).astype(BF16)
                projg_t[ra, LD + pair * 128 : LD + pair * 128 + 128] = mm(ds.astype(BF16), qs).astype(BF16)
                projg_t[ra, 2 * LD + pair * 128 : 2 * LD + pair * 128 + 128] = mm(widen(p).astype(BF16), das).astype(BF16)
            return 0

        for b in range(blocks):
            attend_back(b, 0)
        for c in range(3):
            own = projg_t[:, c * LD : (c + 1) * LD]
            projg[at, c * LD : (c + 1) * LD] = own
            hg = hg + mm_nt(own, w_in[:, c * LD : (c + 1) * LD])
        start = startv[...]
        scaled, factor = norm(start)
        gl = gl + jnp.sum(hg * scaled, axis=0, keepdims=True)
        inner = hg * g_gain_local
        sg = (after_grad + factor * (inner - scaled * jnp.mean(inner * scaled, axis=-1, keepdims=True))).astype(BF16)
        sgrad[at, :] = sg
        wide_rows[at, :] = mm_nt(sg, w_bridge[...])
        return loss, gl, gf

    init = (jnp.zeros((1, 1), F32), jnp.zeros((1, LD), F32), jnp.zeros((1, LD), F32))
    loss, gl, gf = lax.fori_loop(0, steps, step, init)

    for j in range(SLOTS):
        inputg_ref[:, j * GSLOT : (j + 1) * GSLOT] = wide_rows[pl.ds(j, patches, stride=SLOTS), :].astype(BF16)

    def put(ref, index, value, which):
        if base is not None:
            value = value + base[which][index].astype(F32)
        ref[index] = value.astype(ref.dtype)

    every = slice(None)
    if base is not None:
        loss = loss + base[8][...]
        gl = gl + base[7][0:1, :]
        gf = gf + base[7][1:2, :]
    loss_ref[...] = loss
    g_gain[0:1, :] = gl
    g_gain[1:2, :] = gf
    hidden_t = jnp.transpose(hid[...])
    for c in range(3):
        cs = slice(c * 512, c * 512 + 512)
        put(g_in, (every, cs), mm(hidden_t, projg[:, cs]), 0)
    for c in range(4):
        cs = slice(c * 512, c * 512 + 512)
        put(g_up, (every, cs), mm(hidden_t, egrad[:, cs]), 1)
    put(g_out, (every, every), mm_tn(att[...], bgrad[...]), 2)
    for c in range(4):
        cs = slice(c * 512, c * 512 + 512)
        put(g_down, (cs, every), mm_tn(act[:, cs], bgrad[...]), 3)
    put(g_head, (every, every), mm_tn(fin[...], lgrad[...]), 4)
    lookup_all = one_hot(prev_ids[...]).astype(BF16)
    put(g_embed, (every, every), mm_tn(lookup_all, sgrad[...]), 5)
    put(g_bridge, (every, every), mm_tn(inputs_ref[...], sgrad[...]), 6)


def byte_layer(start, own, pieces, ids, mask, micro, forward, slot_rows, count, weights, gains, base=None, tile=512):
    rows = start.shape[0] * SLOTS
    shapes = [(LD, 3 * LD), (LD, LFF), (LD, LD), (LFF, LD), (LD, VOCAB), (VOCAB, LD), (GSLOT, LD)]
    out_shape = [jax.ShapeDtypeStruct(s, BF16) for s in shapes] + [
        jax.ShapeDtypeStruct((2, LD), F32), jax.ShapeDtypeStruct((1, 1), F32),
        jax.ShapeDtypeStruct(start.shape, BF16)]
    args = [start, own, *pieces, ids, mask, count, *weights, gains] + (list(base) if base is not None else [])
    vm = pl.BlockSpec(memory_space=pltpu.VMEM)
    in_specs = [vm] * len(args)
    in_specs[4 + len(pieces)] = pl.BlockSpec(memory_space=pltpu.SMEM)
    return pl.pallas_call(
        functools.partial(byte_kernel, rows, tile, base is not None, len(pieces), micro, forward, slot_rows),
        out_shape=out_shape,
        in_specs=in_specs,
        out_specs=[vm] * len(out_shape),
        cost_estimate=pl.CostEstimate(flops=43 * 10**9, bytes_accessed=150 * 10**6, transcendentals=10**6),
        scratch_shapes=[
            pltpu.VMEM((rows, LD), BF16),
            pltpu.VMEM((tile, 3 * LD), BF16),
            pltpu.VMEM((tile // 128 * 4, SLOTS, 256), F32),
            pltpu.VMEM((rows, LD), BF16),
            pltpu.VMEM((rows, LFF), BF16),
            pltpu.VMEM((tile, LFF), BF16),
            pltpu.VMEM((rows, LD), BF16),
            pltpu.VMEM((rows, VOCAB), BF16),
            pltpu.VMEM((rows, LD), BF16),
            pltpu.VMEM((rows, LFF), BF16),
            pltpu.VMEM((tile, LD), BF16),
            pltpu.VMEM((rows, 3 * LD), BF16),
            pltpu.VMEM((rows, LD), BF16),
            pltpu.VMEM((tile, LD), F32),
            pltpu.VMEM((tile, LD), BF16),
            pltpu.VMEM((tile, 3 * LD), BF16),
            pltpu.VMEM((rows, GSLOT), F32),
            pltpu.VMEM((rows, GSLOT), F32),
            pltpu.VMEM((rows, GSLOT), F32),
            pltpu.VMEM((rows, GSLOT), F32),
            pltpu.VMEM((rows, GSLOT), BF16),
        ],
        compiler_params=pltpu.CompilerParams(vmem_limit_bytes=61 * 2**20),
        name="byte_layer",
    )(*args)


def other(index, offset, size):
    return index ^ offset if size & (size - 1) == 0 else lax.rem(index + offset, size)


def origin(index, offset, size):
    return index ^ offset if size & (size - 1) == 0 else lax.rem(index + size - offset, size)


def place_of(ref, by_column, extent, index):
    at = pl.ds(pl.multiple_of(index * extent, extent), extent)
    return ref.at[:, at] if by_column else ref.at[at, :]


def remote(src, dst, send, recv, device):
    return pltpu.make_async_remote_copy(
        src_ref=src, dst_ref=dst, send_sem=send, recv_sem=recv, device_id=device, device_id_type=MESH
    )


def greet(devices):
    barrier = pltpu.get_barrier_semaphore()
    for device in devices:
        pl.semaphore_signal(barrier, inc=1, device_id=device, device_id_type=MESH)
    pl.semaphore_wait(barrier, len(devices))


def group_peers(slots, groups):
    s, m, d = lax.axis_index(SLOT), lax.axis_index(STACK), lax.axis_index(CORE)
    across = [(other(s, j, slots), m, d) for j in range(1, slots)]
    beside = [(s, m, other(d, k, groups)) for k in range(1, groups)]
    return across, beside


def stack_peers(stacks):
    s, m, d = lax.axis_index(SLOT), lax.axis_index(STACK), lax.axis_index(CORE)
    return [(s, other(m, j, stacks), d) for j in range(1, stacks)]


def gather_kernel(sizes, columns, forwarded, *refs):
    slots, stacks, groups = sizes
    count = len(columns)
    wide, tail, counted = refs[:count], refs[count], refs[count + 1]
    outs, gain_out, count_out = refs[count + 2 : 2 * count + 2], refs[2 * count + 2], refs[2 * count + 3]
    shards, rest = refs[2 * count + 4 : 3 * count + 4], refs[3 * count + 4 :]
    (tail_z, tail_s, tail_d, held_count, own_sem, xs, xr, cs, cr, zs, zr, ts, tr, ds, dr, ns, nr) = rest
    s, m, d = lax.axis_index(SLOT), lax.axis_index(STACK), lax.axis_index(CORE)
    across, beside = group_peers(slots, groups)
    above = stack_peers(stacks)
    for w in range(count):
        if len(wide[w].shape) == 3:
            breadth = wide[w].shape[2]
            for i in range(wide[w].shape[0]):
                shards[w][:, i * breadth : (i + 1) * breadth] = wide[w][i].astype(BF16)
        else:
            shards[w][...] = wide[w][...].astype(BF16)
    tail_z[m] = tail[...].astype(BF16)
    held_count[d] = counted[...]
    greet(across + beside + above)

    def place(w, slot, group, half=None):
        rows, breadth = shards[w].shape
        index = slot * groups + group
        if half is None:
            return place_of(outs[w], columns[w], breadth if columns[w] else rows, index)
        size = rows // 2
        if columns[w]:
            return outs[w].at[pl.ds(half * size, size), pl.ds(pl.multiple_of(index * breadth, breadth), breadth)]
        return outs[w].at[pl.ds(pl.multiple_of(index * rows + half * size, size), size), :]

    tail_copies = [remote(tail_z.at[m], tail_z.at[m], zs.at[j], zr.at[j], above[j - 1]) for j in range(1, stacks)]
    tail_copies += [
        remote(held_count.at[d], held_count.at[d], ns.at[k], nr.at[k], beside[k - 1]) for k in range(1, groups)
    ]
    for copy in tail_copies:
        copy.start()
    sends, pending = [], []
    direct = (1, 2) if forwarded else tuple(range(1, slots))
    for w in range(count):
        for j in direct:
            copy = remote(shards[w], place(w, s, d), xs.at[w, j], xr.at[w, j], across[j - 1])
            copy.start()
            sends.append(copy)
    for w in range(count):
        for k in range(1, groups):
            copy = remote(shards[w], place(w, s, d), cs.at[w, 0, k], cr.at[w, 0, k], beside[k - 1])
            copy.start()
            pending.append(copy)
        copy = pltpu.make_async_copy(shards[w], place(w, s, d), own_sem.at[w])
        copy.start()
        pending.append(copy)

    for copy in tail_copies:
        copy.wait()
    total = held_count[0]
    for k in range(1, groups):
        total = total + held_count[k]
    count_out[...] = total
    tail_s[s] = tail_z[stacks - 1]
    step = [remote(tail_s.at[s], tail_s.at[s], ts.at[j], tr.at[j], across[j - 1]) for j in range(1, slots)]
    for copy in step:
        copy.start()
    for copy in step:
        copy.wait()
    tail_d[d] = tail_s[slots - 1]
    step = [remote(tail_d.at[d], tail_d.at[d], ds.at[k], dr.at[k], beside[k - 1]) for k in range(1, groups)]
    for copy in step:
        copy.start()
    for copy in step:
        copy.wait()
    gain_out[...] = tail_d[groups - 1].astype(F32)

    def spread(w, j, slot):
        here = place(w, slot, d)
        for k in range(1, groups):
            copy = remote(here, here, cs.at[w, j, k], cr.at[w, j, k], beside[k - 1])
            copy.start()
            pending.append(copy)

    for w in range(count):
        for j in direct:
            slot = origin(s, j, slots)
            here = place(w, slot, d)
            remote(here, here, xs.at[w, j], xr.at[w, j], across[j - 1]).wait_recv()
            if forwarded:
                half = 0 if j == 1 else 1
                part, index = place(w, slot, d, half), 3 if j == 1 else 0
                copy = remote(part, part, xs.at[w, index], xr.at[w, index], across[2 - j])
                copy.start()
                sends.append(copy)
            spread(w, j, slot)
    if forwarded:
        for w in range(count):
            slot = s ^ 3
            for half, index in ((0, 3), (1, 0)):
                part = place(w, slot, d, half)
                remote(part, part, xs.at[w, index], xr.at[w, index], across[1 - half]).wait_recv()
            spread(w, 3, slot)
    for copy in sends:
        copy.wait_send()
    for copy in pending:
        copy.wait()


def gather_weights(shards, columns, tail, counted):
    sizes = tuple(lax.axis_size(axis) for axis in (SLOT, STACK, CORE))
    slots, stacks, groups = sizes
    count = len(shards)
    parts = slots * groups
    flats = [(v.shape[1], v.shape[0] * v.shape[2]) if v.ndim == 3 else v.shape for v in shards]
    shapes = [
        (v[0], v[1] * parts) if c else (v[0] * parts, v[1]) for v, c in zip(flats, columns)
    ]
    forwarded = slots == 4 and all(v[0] % 32 == 0 for v in flats)
    anywhere = pl.BlockSpec(memory_space=pl.ANY)
    vm = pl.BlockSpec(memory_space=pltpu.VMEM)
    dma = pltpu.SemaphoreType.DMA
    return pl.pallas_call(
        functools.partial(gather_kernel, sizes, columns, forwarded),
        out_shape=[jax.ShapeDtypeStruct(shape, BF16) for shape in shapes]
        + [jax.ShapeDtypeStruct(tail.shape, F32), jax.ShapeDtypeStruct(counted.shape, F32)],
        in_specs=[vm] * (count + 2),
        out_specs=[anywhere] * count + [vm] * 2,
        scratch_shapes=[pltpu.VMEM(v, BF16) for v in flats]
        + [
            pltpu.VMEM((stacks,) + tail.shape, BF16),
            pltpu.VMEM((slots,) + tail.shape, BF16),
            pltpu.VMEM((groups,) + tail.shape, BF16),
            pltpu.VMEM((groups,) + counted.shape, F32),
            dma((count,)),
            dma((count, slots)), dma((count, slots)),
            dma((count, slots, groups)), dma((count, slots, groups)),
            dma((stacks,)), dma((stacks,)),
            dma((slots,)), dma((slots,)),
            dma((groups,)), dma((groups,)),
            dma((groups,)), dma((groups,)),
        ],
        compiler_params=pltpu.CompilerParams(
            collective_id=1, has_side_effects=True, vmem_limit_bytes=24 * 2**20
        ),
        cost_estimate=pl.CostEstimate(flops=10**6, bytes_accessed=120 * 10**6, transcendentals=0),
        name="gather_weights",
    )(*shards, tail, counted)


def scatter_kernel(sizes, columns, extents, shared, *refs):
    slots, stacks, groups = sizes
    count = len(columns)
    partials, outs = refs[:count], refs[count : 2 * count]
    rest = refs[2 * count :]
    from_core, stage, from_slot = rest[:count], rest[count : 2 * count], rest[2 * count : 3 * count]
    cs, cr, xs, xr = rest[3 * count : 3 * count + 4]
    if shared:
        from_z, own_c, from_c, zs, zr, ts, tr = rest[3 * count + 4 :]
    s, m, d = lax.axis_index(SLOT), lax.axis_index(STACK), lax.axis_index(CORE)
    across, beside = group_peers(slots, groups)
    above = stack_peers(stacks)
    greet(across + beside + above if shared else across + beside)
    order = tuple(range(count))

    def part(w, slot, group):
        return place_of(partials[w], columns[w], extents[w], slot * groups + group)

    first = {}
    for w in order:
        for j in tuple(range(1, slots)) + (0,):
            t = other(s, j, slots)
            for k in range(1, groups):
                copy = remote(
                    part(w, t, other(d, k, groups)), from_core[w].at[j, k - 1],
                    cs.at[w, j, k], cr.at[w, j, k], beside[k - 1],
                )
                copy.start()
                first[w, j, k] = copy
    second = {}
    for w in order:
        for j in tuple(range(1, slots)) + (0,):
            t = other(s, j, slots)
            for k in range(1, groups):
                first[w, j, k].wait_recv()
            total = part(w, t, d)[...].astype(F32)
            for k in range(1, groups):
                total = total + from_core[w][j, k - 1].astype(F32)
            if j:
                stage[w][j] = total.astype(BF16)
                copy = remote(stage[w].at[j], from_slot[w].at[j], xs.at[w, j], xr.at[w, j], across[j - 1])
                copy.start()
                second[w, j] = copy
            else:
                outs[w][: total.shape[0]] = total
    for w in order:
        for j in range(1, slots):
            second[w, j].wait_recv()
        total = outs[w][: from_slot[w].shape[1]]
        for j in range(1, slots):
            total = total + from_slot[w][j].astype(F32)
        outs[w][: total.shape[0]] = total
        if shared:
            from_z[m] = total.astype(BF16)
            third = [
                remote(from_z.at[m], from_z.at[m], zs.at[j], zr.at[j], above[j - 1])
                for j in range(1, stacks)
            ]
            for copy in third:
                copy.start()
    if shared:
        w = 0
        size = from_slot[w].shape[1]
        for copy in third:
            copy.wait()
        total = from_z[0].astype(F32)
        for j in range(1, stacks):
            total = total + from_z[j].astype(F32)
        own_c[...] = total.astype(BF16)
        fourth = [remote(own_c, from_c.at[k], ts.at[k], tr.at[k], beside[k - 1]) for k in range(1, groups)]
        for copy in fourth:
            copy.start()
        outs[w][pl.ds(pl.multiple_of(d * size, size), size), :] = own_c[...].astype(F32)
        for k in range(1, groups):
            fourth[k - 1].wait()
            outs[w][pl.ds(pl.multiple_of(origin(d, k, groups) * size, size), size), :] = from_c[k].astype(F32)
    for copy in first.values():
        copy.wait_send()
    for copy in second.values():
        copy.wait_send()


def scatter_grads(partials, columns, shared=False):
    sizes = tuple(lax.axis_size(axis) for axis in (SLOT, STACK, CORE))
    slots, stacks, groups = sizes
    count = len(partials)
    parts = slots * groups
    blocks = [
        (v.shape[0], v.shape[1] // parts) if c else (v.shape[0] // parts, v.shape[1])
        for v, c in zip(partials, columns)
    ]
    extents = tuple(b[1] if c else b[0] for b, c in zip(blocks, columns))
    shapes = [(b[0] * groups, b[1]) for b in blocks] if shared else blocks
    vm = pl.BlockSpec(memory_space=pltpu.VMEM)
    dma = pltpu.SemaphoreType.DMA
    last = blocks[-1]
    return pl.pallas_call(
        functools.partial(scatter_kernel, sizes, columns, extents, shared),
        out_shape=[jax.ShapeDtypeStruct(shape, F32) for shape in shapes],
        in_specs=[vm] * count,
        out_specs=[vm] * count,
        scratch_shapes=[pltpu.VMEM((slots, groups - 1) + b, BF16) for b in blocks]
        + [pltpu.VMEM((slots,) + b, BF16) for b in blocks]
        + [pltpu.VMEM((slots,) + b, BF16) for b in blocks]
        + [dma((count, slots, groups))] * 2
        + [dma((count, slots))] * 2
        + (
            [
                pltpu.VMEM((stacks,) + last, BF16),
                pltpu.VMEM(last, BF16), pltpu.VMEM((groups,) + last, BF16),
                dma((stacks,)), dma((stacks,)), dma((groups,)), dma((groups,)),
            ]
            if shared
            else []
        ),
        compiler_params=pltpu.CompilerParams(
            collective_id=4 if shared else 2, has_side_effects=True, vmem_limit_bytes=48 * 2**20
        ),
        cost_estimate=pl.CostEstimate(
            flops=10**6, bytes_accessed=(10 if shared else 120) * 10**6, transcendentals=0
        ),
        name="scatter_small" if shared else "scatter_grads",
    )(*partials)


def total_kernel(sizes, value, out, held_z, held_s, held_d, zs, zr, xs, xr, cs, cr):
    slots, stacks, groups = sizes
    across, beside = group_peers(slots, groups)
    above = stack_peers(stacks)
    greet(across + beside + above)
    total = value[...]
    for axis, peers, held, send, recv in (
        (STACK, above, held_z, zs, zr), (SLOT, across, held_s, xs, xr), (CORE, beside, held_d, cs, cr)
    ):
        index = lax.axis_index(axis)
        held[index] = total
        copies = [
            remote(held.at[index], held.at[index], send.at[j], recv.at[j], peer)
            for j, peer in enumerate(peers)
        ]
        for copy in copies:
            copy.start()
        for copy in copies:
            copy.wait()
        total = held[0]
        for j in range(1, len(peers) + 1):
            total = total + held[j]
    out[...] = total


def total_of(value):
    sizes = tuple(lax.axis_size(axis) for axis in (SLOT, STACK, CORE))
    slots, stacks, groups = sizes
    vm = pl.BlockSpec(memory_space=pltpu.VMEM)
    dma = pltpu.SemaphoreType.DMA
    return pl.pallas_call(
        functools.partial(total_kernel, sizes),
        out_shape=jax.ShapeDtypeStruct(value.shape, F32),
        in_specs=[vm],
        out_specs=vm,
        scratch_shapes=[pltpu.VMEM((size,) + value.shape, F32) for size in (stacks, slots, groups)]
        + [dma((size,)) for size in (stacks, stacks, slots, slots, groups, groups)],
        compiler_params=pltpu.CompilerParams(collective_id=3, has_side_effects=True),
        name="total_of",
    )(value)


def pieces_of(size):
    return max(step for step in range(16, 129, 16) if size % step == 0)


def pack_layout():
    layout = []
    offset = 0
    for height, breadth in (
        (LD, 3 * LD), (LD, LFF), (LD, LD), (LFF, LD), (LD, VOCAB), (VOCAB, LD), (GSLOT, LD)
    ):
        layout.append((offset, height, breadth // 128))
        offset += height * breadth // 128
    return layout, offset


def unpack_kernel(share, rows, count, blocks_ref, *refs):
    outs, flat = refs[:-1], refs[-1]
    chunk = pieces_of(rows)
    flat[0:8, :] = jnp.zeros((8, 128), F32)

    def block(b, _):
        top = lax.div(b * share, 128)
        held = flat[pl.ds(top, 1), :]
        for i in range(0, rows, chunk):
            source = pl.ds(pl.multiple_of(b * rows, 16) + i, chunk)
            flat[pl.ds(top + i, chunk), :] = blocks_ref[source, :].astype(F32)
        flat[pl.ds(top, 1), :] = flat[pl.ds(top, 1), :] + held
        return 0

    lax.fori_loop(0, count, block, 0)
    layout, _ = pack_layout()
    for out, (offset, height, breadth) in zip(outs, layout):
        def part(i, _, out=out, offset=offset, breadth=breadth):
            for c in range(breadth):
                values = flat[pl.ds(offset + i * (128 * breadth) + c, 128, stride=breadth), :]
                out[pl.ds(pl.multiple_of(i * 128, 128), 128), c * 128 : (c + 1) * 128] = values.astype(BF16)
            return 0
        lax.fori_loop(0, height // 128, part, 0)


def unpack(blocks, share):
    rows = block_rows(share)
    count = blocks.shape[0] // rows
    layout, used = pack_layout()
    vm = pl.BlockSpec(memory_space=pltpu.VMEM)
    return pl.pallas_call(
        functools.partial(unpack_kernel, share, rows, count),
        out_shape=[jax.ShapeDtypeStruct((h, b * 128), BF16) for _, h, b in layout],
        in_specs=[vm],
        out_specs=[vm] * len(layout),
        scratch_shapes=[pltpu.VMEM((share * count // 128 + rows + 8, 128), F32)],
        compiler_params=pltpu.CompilerParams(vmem_limit_bytes=48 * 2**20),
        name="unpack",
    )(blocks)


def pack_kernel(share, rows, count, *refs):
    matrices, out, flat = refs[:-2], refs[-2], refs[-1]
    chunk = pieces_of(rows)
    layout, used = pack_layout()
    for matrix, (offset, height, breadth) in zip(matrices, layout):
        def part(i, _, matrix=matrix, offset=offset, breadth=breadth):
            for c in range(breadth):
                values = matrix[pl.ds(pl.multiple_of(i * 128, 128), 128), c * 128 : (c + 1) * 128]
                flat[pl.ds(offset + i * (128 * breadth) + c, 128, stride=breadth), :] = values.astype(F32)
            return 0
        lax.fori_loop(0, height // 128, part, 0)
    spare = flat.shape[0] - used
    flat[used:, :] = jnp.zeros((spare, 128), F32)

    def block(b, _):
        top = lax.div(b * share, 128)
        for i in range(0, rows, chunk):
            target = pl.ds(pl.multiple_of(b * rows, 16) + i, chunk)
            out[target, :] = flat[pl.ds(top + i, chunk), :].astype(BF16)
        return 0

    lax.fori_loop(0, count, block, 0)


def pack(matrices, share):
    rows = block_rows(share)
    layout, used = pack_layout()
    total = used + (D + 2 * LD) // 128
    count = total * 128 // share
    vm = pl.BlockSpec(memory_space=pltpu.VMEM)
    return pl.pallas_call(
        functools.partial(pack_kernel, share, rows, count),
        out_shape=jax.ShapeDtypeStruct((count * rows, 128), BF16),
        in_specs=[vm] * len(layout),
        out_specs=vm,
        scratch_shapes=[pltpu.VMEM((total + rows + 8, 128), F32)],
        compiler_params=pltpu.CompilerParams(vmem_limit_bytes=48 * 2**20),
        name="pack",
    )(*matrices)


def partner(index, offset, size):
    return index ^ offset if size & (size - 1) == 0 else (index + offset) % size


def swap(value, axis, offset):
    size = lax.axis_size(axis)
    if size & (size - 1) == 0:
        pairs = [(i, i ^ offset) for i in range(size)]
    else:
        pairs = [(i, (i + offset) % size) for i in range(size)]
    return lax.ppermute(value, axis, pairs)


def source(index, offset, size):
    return index ^ offset if size & (size - 1) == 0 else (index + size - offset) % size


def trade_rows(partial, axis):
    size = lax.axis_size(axis)
    index = lax.axis_index(axis)
    share = partial.shape[0] // size
    pieces = []
    for offset in range(1, size):
        block = lax.dynamic_slice_in_dim(partial, partner(index, offset, size) * share, share, 0)
        pieces.append(swap(block.astype(BF16), axis, offset))
    return lax.dynamic_slice_in_dim(partial, index * share, share, 0), pieces


def share_rows(block, axis):
    return [block] + [swap(block, axis, offset) for offset in range(1, lax.axis_size(axis))]


def shift_chunks(value, distance, forward):
    size = lax.axis_size(SLOT)
    if forward:
        pairs = [(i, i + distance) for i in range(size - distance)]
    else:
        pairs = [(i + distance, i) for i in range(size - distance)]
    return lax.ppermute(value, SLOT, pairs)


def update(weight, moment, average, gradient, factor, rate):
    step_grad = factor * gradient
    moment_next = momentum_keep * moment + step_grad
    weight_next = weight - rate * (step_grad + momentum_keep * moment_next)
    average_next = average_keep * average + (1.0 - average_keep) * weight_next
    return (weight_next, moment_next, average_next)


def block_rows(share):
    return -(-(-(-share // 128) + 1) // 16) * 16


def gather_pack(local_pack):
    share = local_pack.shape[0]
    index = lax.axis_index((SLOT, STACK, CORE))
    offset = lax.rem(index * share, 128)
    rows = block_rows(share)
    block = lax.dynamic_update_slice_in_dim(
        jnp.zeros((rows * 128,), BF16), local_pack.astype(BF16), offset, 0
    )
    return lax.all_gather(block.reshape(rows, 128), (SLOT, STACK, CORE), axis=0, tiled=True)


def local(
    byte_ids, item_ids, loss_mask,
    attend_in, expand_in, attend_out, expand_out, slot_table, local_pack,
    moment_attend_in, moment_expand_in, moment_attend_out, moment_expand_out,
    moment_slot_table, moment_local_pack,
    average_attend_in, average_expand_in, average_attend_out, average_expand_out,
    average_slot_table, average_local_pack,
):
    slot_size, mp_size = lax.axis_size(SLOT), lax.axis_size(STACK)
    slot_index, mp_index, dp_index = (
        lax.axis_index(SLOT), lax.axis_index(STACK), lax.axis_index(CORE),
    )
    counted = jnp.full((8, 128), jnp.sum(loss_mask.astype(F32)))
    width = attend_in.shape[2]
    piece = slot_table.shape[0] * VOCAB // lax.axis_size(CORE)
    table_shard = lax.dynamic_slice_in_dim(
        slot_table.reshape(-1, GSLOT), dp_index * piece, piece, 0
    )
    tail = local_pack[-(D + 2 * LD) :].reshape(-1, 128)
    shards = [table_shard, jnp.transpose(attend_in, (1, 0, 2)), expand_in]
    late = [attend_out, expand_out]
    wide = attend_out.shape[1] % 128 == 0
    if wide:
        table, full_in_flat, full_expand, full_out, full_shrink, gains, counted = gather_weights(
            shards + late, (False, False, False, True, True), tail, counted
        )
    else:
        table, full_in_flat, full_expand, gains, counted = gather_weights(
            shards, (False, False, False), tail, counted
        )
        full_out, full_shrink = (
            lax.all_gather(v.astype(BF16), (SLOT, CORE), axis=1, tiled=True) for v in late
        )
    pack_whole = gather_pack(local_pack)
    gains = gains.reshape(-1)
    mask_count = counted[0, 0]
    gain_global = gains[:D]
    local_gains = gains[D:].reshape(2, LD)
    unpacked = unpack(pack_whole, local_pack.shape[0])
    group_rows = byte_ids.shape[1]
    rows = group_rows // slot_size
    local_rows = rows // mp_size
    vocab_ids = jnp.arange(VOCAB)
    reach = min(slot_size - 1, -(-(longest_item - 1) // rows))
    ids_t, mask_t = jnp.transpose(byte_ids, (0, 2, 1)), jnp.transpose(loss_mask, (0, 2, 1))
    micros = []
    for micro in range(byte_ids.shape[0]):
        forward = micro % 2 == 0
        start_rows, hidden, projected, own_kv, own_previous = embed_rows(
            ids_t, item_ids, micro, forward, rows, table, full_in_flat, gain_global[None]
        )
        earlier = [shift_chunks(own_kv, d, forward) for d in range(1, reach + 1)]
        micros.append(types.SimpleNamespace(
            forward=forward, micro=micro, start_rows=start_rows, hidden=hidden, projected=projected,
            earlier=earlier, own_previous=own_previous,
        ))
    for m, pair in zip(micros, up_rows([m.hidden for m in micros], full_expand)):
        m.active, m.slope = pair
    for m in micros:
        m.attended, m.lse = attention_fwd(
            item_ids, m.micro, m.forward, m.projected, m.earlier
        )
        m.own, m.pieces = trade_rows(
            product(m.attended, full_out) + product(m.active, full_shrink), STACK
        )
        m.own_start = lax.dynamic_slice_in_dim(
            m.start_rows, mp_index * local_rows, local_rows, 0
        )
    base = None
    for m in micros:
        out = byte_layer(
            m.own_start, m.own, m.pieces, ids_t, mask_t, m.micro, m.forward, rows,
            mask_count.reshape(1, 1), unpacked[:7], local_gains, base,
        )
        base = out[:9]
        m.own_back = out[9]
        m.branch_pieces = share_rows(out[9], STACK)
    matrices, local_gain_grads, loss_sum = base[:7], base[7], base[8][0, 0]
    local_blocks = pack(matrices, local_pack.shape[0])
    sums = None
    table_grad = None
    gain_global_grad = None
    for m in micros:
        branch_grad, m.query_grad, m.kv_grads = attention_bwd(
            item_ids, m.micro, m.forward, m.projected, m.earlier, m.attended, m.lse,
            full_out, m.branch_pieces,
        )
        m.branch_grad = branch_grad
        m.returned = [
            shift_chunks(m.kv_grads[d], d, not m.forward) for d in range(1, reach + 1)
        ]
        m.expanded_grad = (
            m.slope.astype(F32) * back_product(branch_grad, full_shrink)
        ).astype(BF16)
    for m in micros:
        kv_total = m.kv_grads[0].astype(F32)
        for value in m.returned:
            kv_total = kv_total + value.astype(F32)
        m.projected_grad = jnp.concatenate([m.query_grad, kv_total.astype(BF16)], axis=1)
        m.partial = back_product(m.projected_grad, full_in_flat) + back_product(
            m.expanded_grad, full_expand
        )
        m.back = trade_rows(m.partial, STACK)
    sums = None
    for m in micros:
        terms = (
            gram_product(m.hidden, m.projected_grad),
            gram_product(m.hidden, m.expanded_grad),
            gram_product(m.attended, m.branch_grad),
            gram_product(m.active, m.branch_grad),
        )
        sums = terms if sums is None else tuple(a + b for a, b in zip(sums, terms))
    sums = tuple(s.astype(BF16) for s in sums)
    if wide:
        sums, _ = lax.optimization_barrier((sums, [m.back[0] for m in micros]))
        own_in, own_expand, own_out, own_shrink = scatter_grads(sums, (False, False, True, True))
    else:
        own_in, own_expand = scatter_grads(sums[:2], (False, False))
        own_out, own_shrink = (
            lax.psum_scatter(v, (SLOT, CORE), scatter_dimension=1, tiled=True).astype(F32)
            for v in sums[2:]
        )
    backs, own_in = lax.optimization_barrier(([m.back for m in micros], own_in))
    table_grad = None
    for m, (hidden_grad, pieces) in zip(micros, backs):
        for value in pieces:
            hidden_grad = hidden_grad + value.astype(F32)
        _, scaled, factor = norm_forward(m.own_start.astype(F32), gain_global)
        gain_term = jnp.sum(hidden_grad * scaled, axis=0)
        start_grad = (
            m.own_back.astype(F32) + norm_backward(scaled, factor, gain_global, hidden_grad)
        ).astype(BF16)
        own_lookup = lax.dynamic_slice_in_dim(m.own_previous, mp_index * local_rows, local_rows, 0)
        own_lookup = (own_lookup[:, :, None] == vocab_ids).astype(BF16)
        table_term = jnp.einsum(
            "pjv,pjg->jvg", own_lookup, start_grad.reshape(local_rows, SLOTS, GSLOT),
            preferred_element_type=F32,
        )
        if table_grad is None:
            table_grad, gain_global_grad = table_term, gain_term
        else:
            table_grad = table_grad + table_term
            gain_global_grad = gain_global_grad + gain_term
    gain_grads = jnp.concatenate([gain_global_grad, local_gain_grads.reshape(-1)])
    parts = slot_size * lax.axis_size(CORE)
    small = jnp.concatenate(
        [
            table_grad.astype(BF16).reshape(parts, -1, GSLOT),
            jnp.broadcast_to(gain_grads.astype(BF16).reshape(1, -1, GSLOT), (parts, 16, GSLOT)),
        ],
        axis=1,
    ).reshape(-1, GSLOT)
    squares = jnp.float32(0.0)
    for gradient in (own_in, own_expand, own_out, own_shrink):
        squares = squares + jnp.sum(gradient * gradient)
    small, squares = lax.optimization_barrier((small, squares))
    own_small = scatter_grads([small], (False,), True)[0]
    own_small = own_small.reshape(lax.axis_size(CORE), piece + 16, GSLOT)
    own_table = own_small[:, :piece].reshape(slot_table.shape)
    gain_total = own_small[0, piece:].reshape(-1)
    last = (slot_index == slot_size - 1) & (mp_index == mp_size - 1)
    last = last & (dp_index == lax.axis_size(CORE) - 1)
    owner = ((mp_index == 0) & (dp_index == 0)).astype(F32)
    squares = squares + owner * jnp.sum(own_table * own_table)
    squares = squares + jnp.where(last, jnp.sum(gain_total * gain_total), 0.0)
    own_in = jnp.stack([own_in[:, i * width : (i + 1) * width] for i in range(3)])
    own_block = lax.psum_scatter(local_blocks, (SLOT, STACK, CORE), scatter_dimension=0, tiled=True)
    pack_share, tail_size = local_pack.shape[0], D + 2 * LD
    offset = lax.rem(lax.axis_index((SLOT, STACK, CORE)) * pack_share, 128)
    index = jnp.arange(own_block.shape[0])[:, None] * 128 + jnp.arange(128)[None, :] - offset
    inside = (index >= 0) & (index < jnp.where(last, pack_share - tail_size, pack_share))
    squares = squares + jnp.sum(jnp.where(inside, own_block.astype(F32) ** 2, 0.0))
    own_pack = lax.dynamic_slice_in_dim(own_block.reshape(-1), offset, pack_share, 0).astype(F32)
    own_pack = jnp.concatenate(
        [own_pack[:-tail_size], jnp.where(last, gain_total, own_pack[-tail_size:])]
    )
    both = total_of(jnp.stack([jnp.full((8, 128), squares), jnp.full((8, 128), loss_sum)]))
    total_squares, loss_value = both[0, 0, 0], both[1, 0, 0]
    clip_norm = jnp.sqrt(total_squares)
    factor = clip_max / jnp.maximum(clip_norm, clip_max)
    results = [loss_value * mask_count, mask_count, clip_norm]
    for weight, moment, average, gradient, rate in (
        (attend_in, moment_attend_in, average_attend_in, own_in, rate_dense),
        (expand_in, moment_expand_in, average_expand_in, own_expand, rate_dense),
        (attend_out, moment_attend_out, average_attend_out, own_out, rate_project),
        (expand_out, moment_expand_out, average_expand_out, own_shrink, rate_dense),
        (slot_table, moment_slot_table, average_slot_table, own_table, rate_table),
        (local_pack, moment_local_pack, average_local_pack, own_pack, rate_dense),
    ):
        if gradient is own_in:
            weight, moment, average = (jnp.transpose(v, (1, 0, 2)) for v in (weight, moment, average))
        changed = update(weight, moment, average, gradient, factor, rate)
        if gradient is own_in:
            changed = tuple(jnp.transpose(v, (1, 0, 2)) for v in changed)
        results.extend(changed)
    return tuple(results)


def solution(mesh):
    placed = (
        P(None, CORE, None),
        P(None, CORE, None),
        P(None, CORE, None),
        P((SLOT, CORE), None, STACK),
        P((SLOT, CORE), STACK),
        P(STACK, (SLOT, CORE)),
        P(STACK, (SLOT, CORE)),
        P(SLOT, None, None),
        P((SLOT, STACK, CORE)),
        P((SLOT, CORE), None, STACK),
        P((SLOT, CORE), STACK),
        P(STACK, (SLOT, CORE)),
        P(STACK, (SLOT, CORE)),
        P(SLOT, None, None),
        P((SLOT, STACK, CORE)),
        P((SLOT, CORE), None, STACK),
        P((SLOT, CORE), STACK),
        P(STACK, (SLOT, CORE)),
        P(STACK, (SLOT, CORE)),
        P(SLOT, None, None),
        P((SLOT, STACK, CORE)),
    )
    return jax.shard_map(
        local,
        mesh=mesh,
        in_specs=placed,
        out_specs=(
            P(),
            P(),
            P(),
            P((SLOT, CORE), None, STACK),
            P((SLOT, CORE), None, STACK),
            P((SLOT, CORE), None, STACK),
            P((SLOT, CORE), STACK),
            P((SLOT, CORE), STACK),
            P((SLOT, CORE), STACK),
            P(STACK, (SLOT, CORE)),
            P(STACK, (SLOT, CORE)),
            P(STACK, (SLOT, CORE)),
            P(STACK, (SLOT, CORE)),
            P(STACK, (SLOT, CORE)),
            P(STACK, (SLOT, CORE)),
            P(SLOT, None, None),
            P(SLOT, None, None),
            P(SLOT, None, None),
            P((SLOT, STACK, CORE)),
            P((SLOT, STACK, CORE)),
            P((SLOT, STACK, CORE)),
        ),
        check_vma=False,
    )
```

```python
import functools
import types

import jax
import jax.numpy as jnp
from jax import lax
from jax.experimental import pallas as pl
from jax.experimental.pallas import tpu as pltpu
from jax.sharding import PartitionSpec as P

D = 1024
LD = 512
LH = 8
LFF = 2048
VOCAB = 256
SLOTS = 8
HEADDIM = 64
LHEADDIM = 64
GSLOT = 128
BLK = 256
ITEMS = 5
F32 = jnp.float32
BF16 = jnp.bfloat16
MESH = pl.DeviceIdType.MESH
SLOT, STACK, CORE = "slot", "mp", "dp"

longest_item = 1024


epsilon = 1e-06
clip_max = 0.01
momentum_keep = 0.9
average_keep = 0.9
rate_dense = 3000.0
rate_table = 60000.0
rate_project = 15000.0
masked_score = -1e30


def product(left, right):
    return jnp.dot(left, right, preferred_element_type=jnp.float32)


def gram_product(left, right):
    return lax.dot_general(
        left, right, (((0,), (0,)), ((), ())), preferred_element_type=jnp.float32
    )


def back_product(left, right):
    return lax.dot_general(
        left, right, (((1,), (1,)), ((), ())), preferred_element_type=jnp.float32
    )


def gelu_tanh(values):
    return jax.nn.gelu(values, approximate=True)


def gelu_back(values, gradient):
    return jax.vjp(gelu_tanh, values)[1](gradient)[0]


def norm_forward(values, gain):
    factor = lax.rsqrt(jnp.mean(values * values, axis=-1, keepdims=True) + epsilon)
    scaled = values * factor
    return (scaled * gain, scaled, factor)


def norm_backward(scaled, factor, gain, gradient):
    inner = gradient * gain
    return factor * (inner - scaled * jnp.mean(inner * scaled, axis=-1, keepdims=True))


def split_pack(packed):
    layouts = (
        (LD, 3 * LD),
        (LD, LFF),
        (LD, LD),
        (LFF, LD),
        (LD, VOCAB),
        (VOCAB, LD),
        (GSLOT, LD),
        (D + 2 * LD,),
    )
    pieces = []
    offset = 0
    for layout in layouts:
        length = 1
        for extent in layout:
            length = length * extent
        pieces.append(packed[offset : offset + length].reshape(layout))
        offset = offset + length
    return pieces


def mm(a, b):
    return lax.dot_general(a, b, (((1,), (0,)), ((), ())), preferred_element_type=F32)


def mm_tn(a, b):
    return lax.dot_general(a, b, (((0,), (0,)), ((), ())), preferred_element_type=F32)


def mm_nt(a, b):
    return lax.dot_general(a, b, (((1,), (1,)), ((), ())), preferred_element_type=F32)


def stack_heads(x):
    lane = lax.broadcasted_iota(jnp.int32, x.shape, 1)
    zero = jnp.zeros_like(x)
    return jnp.concatenate([jnp.where(lane < 64, x, zero), jnp.where(lane < 64, zero, x)], axis=0)


def window_fill(rows, width, own_ref, earlier, keys, values_t, values, keys_t):
    for place, ref in enumerate(earlier):
        at = (len(earlier) - 1 - place) * rows
        if keys is not None:
            keys[at : at + rows, :] = ref[:, :width]
        if values is not None:
            values[at : at + rows, :] = ref[:, width:]
        if values_t is not None:
            values_t[:, at : at + rows] = jnp.transpose(ref[:, width:])
        if keys_t is not None:
            keys_t[:, at : at + rows] = jnp.transpose(ref[:, :width])
    at = len(earlier) * rows
    if keys is not None:
        keys[at : at + rows, :] = own_ref[:, width : 2 * width]
    if values is not None:
        values[at : at + rows, :] = own_ref[:, 2 * width :]
    if values_t is not None:
        values_t[:, at : at + rows] = jnp.transpose(own_ref[:, 2 * width :])
    if keys_t is not None:
        keys_t[:, at : at + rows] = jnp.transpose(own_ref[:, width : 2 * width])


def chunk_begin(forward, rows):
    slot, slots = lax.axis_index(SLOT), lax.axis_size(SLOT)
    return (slot if forward else slots - 1 - slot) * rows


def item_starts(items_ref, micro, begin, rows, reach):
    items = items_ref[micro]
    starts = []
    for qt in range(rows // BLK):
        own = items_ref[micro, :, pl.ds(pl.multiple_of(begin + qt * BLK, BLK), BLK)]
        first = jnp.zeros((1, BLK), F32)
        for value in range(1, ITEMS):
            ahead = jnp.sum(jnp.where(items < value, 1.0, 0.0), axis=1, keepdims=True)
            first = jnp.where(own == value, ahead, first)
        first = jnp.maximum(first - (begin - reach * rows).astype(F32), 0.0)
        low = lax.div(jnp.min(first).astype(jnp.int32), BLK)
        first = first.astype(jnp.int32)
        starts.append((jnp.concatenate([first, first], axis=1), low))
    return starts


def fwd_kernel(rows, width, count, micro, forward, items_ref, own_ref, *rest):
    earlier, (att_ref, lse_ref, keys, values_t) = rest[:count], rest[count:]
    window_fill(rows, width, own_ref, earlier, keys, values_t, None, None)
    starts = item_starts(items_ref, micro, chunk_begin(forward, rows), rows, count)
    base = count * rows
    key_iota = lax.broadcasted_iota(jnp.int32, (BLK, 2 * BLK), 0)
    q_iota = lax.broadcasted_iota(jnp.int32, (1, 2 * BLK), 1) % BLK
    pairs = width // 128
    for qt in range(rows // BLK):
        q_pos = q_iota + (base + qt * BLK)
        start, low = starts[qt]
        for pair in range(pairs):
            cs = slice(pair * 128, pair * 128 + 128)
            qs = stack_heads(own_ref[qt * BLK : (qt + 1) * BLK, cs] * jnp.asarray(0.125, BF16))

            def block(i, carry):
                top, total, acc = carry
                kb = base // BLK + qt - i
                at = pl.ds(pl.multiple_of(kb * BLK, BLK), BLK)
                s = mm_nt(keys[at, cs], qs)
                pos = key_iota + kb * BLK
                s = jnp.where((pos >= start) & (pos <= q_pos), s, masked_score)
                new = jnp.maximum(top, jnp.max(s, axis=0, keepdims=True))
                p = jnp.exp(s - new)
                alpha = jnp.exp(top - new)
                total = total * alpha + jnp.sum(p, axis=0, keepdims=True)
                acc = acc * alpha + mm(values_t[cs, at], p.astype(BF16))
                return new, total, acc

            init = (
                jnp.full((1, 2 * BLK), masked_score, F32),
                jnp.zeros((1, 2 * BLK), F32),
                jnp.zeros((128, 2 * BLK), F32),
            )
            top, total, acc = lax.fori_loop(0, base // BLK + qt + 1 - low, block, init)
            acc = acc * (1.0 / total)
            sub = lax.broadcasted_iota(jnp.int32, (128, BLK), 0)
            both = jnp.where(sub < 64, acc[:, :BLK], acc[:, BLK:])
            att_ref[qt * BLK : (qt + 1) * BLK, cs] = jnp.transpose(both).astype(BF16)
            lse_ref[qt * pairs + pair] = top + jnp.log(total)


def bwd_kernel(rows, width, count, pieces, micro, forward, items_ref, own_ref, *rest):
    earlier = rest[:count]
    att_ref, lse_ref, weight_ref = rest[count : count + 3]
    rest = rest[count + 3 :]
    piece_refs, rest = rest[:pieces], rest[pieces:]
    branch_ref, dq_ref, dkv_refs = rest[0], rest[1], rest[2 : count + 3]
    keys, values, keys_t, dkeys, dvalues, attg_ref = rest[count + 3 :]
    place, share = lax.axis_index(STACK), rows // pieces
    for j in range(pieces):
        at = pl.ds(pl.multiple_of(origin(place, j, pieces) * share, share), share)
        branch_ref[at, :] = piece_refs[j][...]
    attg_ref[...] = mm_nt(branch_ref[...], weight_ref[...]).astype(BF16)
    window_fill(rows, width, own_ref, earlier, keys, None, values, keys_t)
    starts = item_starts(items_ref, micro, chunk_begin(forward, rows), rows, count)
    base = count * rows
    dkeys[...] = jnp.zeros_like(dkeys)
    dvalues[...] = jnp.zeros_like(dvalues)
    key_iota = lax.broadcasted_iota(jnp.int32, (BLK, 2 * BLK), 0)
    q_iota = lax.broadcasted_iota(jnp.int32, (1, 2 * BLK), 1) % BLK
    pairs = width // 128
    for qt in range(rows // BLK):
        q_pos = q_iota + (base + qt * BLK)
        start, low = starts[qt]
        rq = slice(qt * BLK, (qt + 1) * BLK)
        for pair in range(pairs):
            cs = slice(pair * 128, pair * 128 + 128)
            qs = stack_heads(own_ref[rq, cs] * jnp.asarray(0.125, BF16))
            das = stack_heads(attg_ref[rq, cs])
            att = att_ref[rq, cs]
            both = jnp.concatenate([att, att], axis=0).astype(F32) * das.astype(F32)
            delta = jnp.sum(jnp.transpose(both), axis=0, keepdims=True)
            lse = lse_ref[qt * pairs + pair]

            def block(i, acc):
                kb = base // BLK + qt - i
                at = pl.ds(pl.multiple_of(kb * BLK, BLK), BLK)
                s = mm_nt(keys[at, cs], qs)
                pos = key_iota + kb * BLK
                p = jnp.where((pos >= start) & (pos <= q_pos), jnp.exp(s - lse), 0.0)
                dp = mm_nt(values[at, cs], das)
                ds = (p * (dp - delta)).astype(BF16)
                dkeys[at, cs] += mm(ds, qs)
                dvalues[at, cs] += mm(p.astype(BF16), das)
                return acc + mm(keys_t[cs, at], ds)

            acc = lax.fori_loop(
                0, base // BLK + qt + 1 - low, block, jnp.zeros((128, 2 * BLK), F32)
            )
            sub = lax.broadcasted_iota(jnp.int32, (128, BLK), 0)
            both = jnp.where(sub < 64, acc[:, :BLK], acc[:, BLK:]) * 0.125
            dq_ref[rq, cs] = jnp.transpose(both).astype(BF16)
    for place in range(count + 1):
        at = (count - place) * rows
        dkv_refs[place][:, :width] = dkeys[at : at + rows, :].astype(BF16)
        dkv_refs[place][:, width:] = dvalues[at : at + rows, :].astype(BF16)


def specs(n):
    return [pl.BlockSpec(memory_space=pltpu.VMEM)] * n


def attention_fwd(items, micro, forward, own, earlier):
    rows, width = own.shape[0], own.shape[1] // 3
    count = len(earlier)
    span = (count + 1) * rows
    units = rows // BLK * (width // 128)
    return pl.pallas_call(
        functools.partial(fwd_kernel, rows, width, count, micro, forward),
        out_shape=[
            jax.ShapeDtypeStruct((rows, width), BF16),
            jax.ShapeDtypeStruct((units, 1, 2 * BLK), F32),
        ],
        in_specs=specs(2 + count),
        out_specs=[pl.BlockSpec(memory_space=pltpu.VMEM)] * 2,
        scratch_shapes=[pltpu.VMEM((span, width), BF16), pltpu.VMEM((width, span), BF16)],
        cost_estimate=pl.CostEstimate(flops=6 * 10**9, bytes_accessed=20 * 10**6, transcendentals=10**6),
        compiler_params=pltpu.CompilerParams(vmem_limit_bytes=32 * 2**20),
        name="patch_attention",
    )(items, own, *earlier)


def attention_bwd(items, micro, forward, own, earlier, attended, lse, weight, pieces):
    rows, width = own.shape[0], own.shape[1] // 3
    count = len(earlier)
    span = (count + 1) * rows
    out = pl.pallas_call(
        functools.partial(bwd_kernel, rows, width, count, len(pieces), micro, forward),
        out_shape=[jax.ShapeDtypeStruct((rows, pieces[0].shape[1]), BF16), jax.ShapeDtypeStruct((rows, width), BF16)]
        + [jax.ShapeDtypeStruct((rows, 2 * width), BF16)] * (count + 1),
        in_specs=specs(5 + count + len(pieces)),
        out_specs=[pl.BlockSpec(memory_space=pltpu.VMEM)] * (count + 3),
        scratch_shapes=[
            pltpu.VMEM((span, width), BF16),
            pltpu.VMEM((span, width), BF16),
            pltpu.VMEM((width, span), BF16),
            pltpu.VMEM((span, width), F32),
            pltpu.VMEM((span, width), F32),
            pltpu.VMEM((rows, width), BF16),
        ],
        cost_estimate=pl.CostEstimate(flops=8 * 10**9, bytes_accessed=25 * 10**6, transcendentals=10**6),
        compiler_params=pltpu.CompilerParams(vmem_limit_bytes=32 * 2**20),
        name="patch_attention_back",
    )(items, own, *earlier, attended, lse, weight, *pieces)
    return out[0], out[1], out[2:]


def embed_kernel(
    width, rows, micro, forward, ids_ref, items_ref, table_ref, w_ref, gain_ref,
    start_ref, hidden_ref, proj_ref, kv_ref, previous_ref,
):
    begin = pl.multiple_of(chunk_begin(forward, rows), 128)
    edge = pl.multiple_of(jnp.maximum(begin - 128, 0), 128)

    def delayed(ref):
        own, before = ref[micro, :, pl.ds(begin, rows)], ref[micro, :, pl.ds(edge, 128)]
        place = lax.broadcasted_iota(jnp.int32, own.shape, 1)
        return own, jnp.where(place == 0, before[:, 127:128], pltpu.roll(own, 1, axis=1))

    own_items, earlier_items = delayed(items_ref)
    place = lax.broadcasted_iota(jnp.int32, own_items.shape, 1)
    keep = (own_items == earlier_items) & ((place > 0) | (begin > 0))
    ids = jnp.where(keep, delayed(ids_ref)[1], -1).astype(F32)
    ids = jnp.transpose(ids)
    previous_ref[...] = ids.astype(jnp.int32)
    low = lax.broadcasted_iota(jnp.int32, (rows, 128), 1).astype(F32)
    squares = jnp.zeros((rows, 1), F32)
    parts = []
    for j in range(SLOTS):
        own = jnp.broadcast_to(ids[:, j : j + 1], (rows, 128))
        hot = jnp.concatenate(
            [jnp.where(own == low, 1.0, 0.0), jnp.where(own == low + 128.0, 1.0, 0.0)], axis=1
        ).astype(BF16)
        part = mm(hot, table_ref[j * VOCAB : (j + 1) * VOCAB, :])
        parts.append(part)
        squares = squares + jnp.sum(part * part, axis=-1, keepdims=True)
    factor = lax.rsqrt(squares * (1.0 / D) + epsilon)
    for j in range(SLOTS):
        cs = slice(j * GSLOT, (j + 1) * GSLOT)
        start_ref[:, cs] = parts[j].astype(BF16)
        hidden_ref[:, cs] = (parts[j] * factor * gain_ref[:, cs]).astype(BF16)
    hidden = hidden_ref[...]
    for c in range(3):
        cs = slice(c * width, (c + 1) * width)
        part = mm(hidden, w_ref[:, cs]).astype(BF16)
        proj_ref[:, cs] = part
        if c:
            kv_ref[:, (c - 1) * width : c * width] = part


def embed_rows(ids, items, micro, forward, rows, table, weight, gain):
    width = weight.shape[1] // 3
    vm = pl.BlockSpec(memory_space=pltpu.VMEM)
    return pl.pallas_call(
        functools.partial(embed_kernel, width, rows, micro, forward),
        out_shape=[
            jax.ShapeDtypeStruct((rows, D), BF16),
            jax.ShapeDtypeStruct((rows, D), BF16),
            jax.ShapeDtypeStruct((rows, 3 * width), BF16),
            jax.ShapeDtypeStruct((rows, 2 * width), BF16),
            jax.ShapeDtypeStruct((rows, SLOTS), jnp.int32),
        ],
        in_specs=[vm] * 5,
        out_specs=[vm] * 5,
        cost_estimate=pl.CostEstimate(flops=2 * 10**9, bytes_accessed=6 * 10**6, transcendentals=1000),
        compiler_params=pltpu.CompilerParams(vmem_limit_bytes=32 * 2**20),
        name="embed_rows",
    )(ids, items, table, weight, gain)


def up_kernel(count, *refs):
    hidden, weight, outs = refs[:count], refs[count], refs[count + 1 :]
    for i in range(count):
        for c in range(0, weight.shape[1], 256):
            value, slope = gelu_pair(mm(hidden[i][...], weight[:, c : c + 256]))
            outs[2 * i][:, c : c + 256] = value.astype(BF16)
            outs[2 * i + 1][:, c : c + 256] = slope.astype(BF16)


def up_rows(hidden, weight):
    count = len(hidden)
    vm = pl.BlockSpec(memory_space=pltpu.VMEM)
    shape = jax.ShapeDtypeStruct((hidden[0].shape[0], weight.shape[1]), BF16)
    out = pl.pallas_call(
        functools.partial(up_kernel, count),
        out_shape=[shape] * (2 * count),
        in_specs=[vm] * (count + 1),
        out_specs=[vm] * (2 * count),
        cost_estimate=pl.CostEstimate(flops=4 * 10**9, bytes_accessed=10**7, transcendentals=10**6),
        compiler_params=pltpu.CompilerParams(vmem_limit_bytes=32 * 2**20),
        name="up_rows",
    )(*hidden, weight)
    return [(out[2 * i], out[2 * i + 1]) for i in range(count)]


def gelu_pair(x):
    c = 0.7978845608028654
    x2 = x * x
    t = jnp.tanh(c * (x + 0.044715 * (x2 * x)))
    half = 0.5 * (1.0 + t)
    slope = half + (0.5 * c) * x * (1.0 - t * t) * (1.0 + (3 * 0.044715) * x2)
    return x * half, slope


def byte_kernel(
    rows, tile, with_base,
    pieces, micro, forward, slot_rows, start_ref, own_ref, *rest
):
    piece_refs, rest = rest[:pieces], rest[pieces:]
    ids_ref, mask_ref, count_ref, w_in, w_up, w_out, w_down, w_head, w_embed, w_bridge, gains_ref = rest[:11]
    rest = rest[11:]
    if with_base:
        base, rest = rest[:9], rest[9:]
    else:
        base = None
    (g_in, g_up, g_out, g_down, g_head, g_embed, g_bridge, g_gain, loss_ref, inputg_ref,
     hid, proj, probs, att, act, slope, fin, lgrad, bgrad, egrad, attg, projg, sgrad, startv, att_t, projg_t,
     wide_rows, own_ids, prev_ids, weights, inputs_ref) = rest
    steps = rows // tile
    blocks = tile // 128
    g_gain_local = gains_ref[0:1, :]
    g_gain_final = gains_ref[1:2, :]
    first = lax.broadcasted_iota(jnp.int32, (128, 128), 1) < 64
    lane = lax.broadcasted_iota(jnp.int32, (SLOTS, 256), 1) % 128
    patch = lane // SLOTS
    causal = lax.broadcasted_iota(jnp.int32, (SLOTS, 256), 0) <= lane % SLOTS
    none = jnp.zeros((SLOTS, 256), F32)
    patches = rows // SLOTS
    begin = chunk_begin(forward, slot_rows) + lax.axis_index(STACK) * patches
    here = pl.ds(pl.multiple_of(begin, 128), patches)
    ids = jnp.transpose(ids_ref[micro, :, here].astype(F32))
    counts = jnp.transpose(mask_ref[micro, :, here].astype(F32))
    for j in range(SLOTS):
        cs = slice(j * GSLOT, (j + 1) * GSLOT)
        at = pl.ds(j, patches, stride=SLOTS)
        total = own_ref[:, cs] + start_ref[:, cs].astype(F32)
        for piece in piece_refs:
            total = total + piece[:, cs].astype(F32)
        wide_rows[at, :] = total
        spread = functools.partial(jnp.broadcast_to, shape=(patches, 128))
        own_ids[at, :] = spread(ids[:, j : j + 1])
        prev_ids[at, :] = spread(ids[:, j - 1 : j]) if j else jnp.full((patches, 128), -1.0, F32)
        weights[at, :] = spread(counts[:, j : j + 1] / count_ref[0, 0])
    inputs_ref[...] = wide_rows[...].astype(BF16)

    def one_hot(ids):
        low = lax.broadcasted_iota(jnp.int32, ids.shape, 1).astype(F32)
        return jnp.concatenate(
            [jnp.where(ids == low, 1.0, 0.0), jnp.where(ids == low + 128.0, 1.0, 0.0)], axis=1
        )

    zero_low = jnp.zeros((128, 128), BF16)

    def stack(x):
        return jnp.concatenate([jnp.where(first, x, zero_low), jnp.where(first, zero_low, x)], axis=0)

    def narrow(x):
        out = x[:SLOTS]
        for j in range(1, 16):
            out = jnp.where(patch == j, x[j * SLOTS : (j + 1) * SLOTS], out)
        return out

    def widen(x):
        return jnp.concatenate([jnp.where(patch == j, x, none) for j in range(16)], axis=0)

    def norm(v):
        factor = lax.rsqrt(jnp.mean(v * v, axis=-1, keepdims=True) + epsilon)
        return v * factor, factor

    def step(t, carry):
        loss, gl, gf = carry
        at = pl.ds(pl.multiple_of(t * tile, tile), tile)
        inputs = inputs_ref[at, :]
        weighting = weights[at, :]
        lookup = one_hot(prev_ids[at, :]).astype(BF16)
        start = mm(inputs, w_bridge[...]) + mm(lookup, w_embed[...])
        startv[...] = start
        scaled, factor = norm(start)
        hidden = (scaled * g_gain_local).astype(BF16)
        hid[at, :] = hidden
        for c in range(3):
            proj[:, c * LD : (c + 1) * LD] = mm(hidden, w_in[:, c * LD : (c + 1) * LD]).astype(BF16)

        def attend(b, _):
            ra = pl.ds(b * 128 if isinstance(b, int) else pl.multiple_of(b * 128, 128), 128)
            for pair in range(4):
                cs = slice(pair * 128, pair * 128 + 128)
                qs = stack(proj[ra, cs] * jnp.asarray(0.125, BF16))
                kp = proj[ra, LD + pair * 128 : LD + pair * 128 + 128]
                vp = proj[ra, 2 * LD + pair * 128 : 2 * LD + pair * 128 + 128]
                s = jnp.where(causal, narrow(mm_nt(kp, qs)), masked_score)
                e = jnp.exp(s - jnp.max(s, axis=0, keepdims=True))
                p = e * (1.0 / jnp.sum(e, axis=0, keepdims=True))
                probs[b * 4 + pair] = p
                flipped = jnp.transpose(widen(p).astype(BF16))
                wide = jnp.concatenate([flipped[:128], flipped[128:]], axis=1)
                att_t[ra, cs] = mm(wide, stack(vp)).astype(BF16)
            return 0

        def two(i, _):
            attend(2 * i, 0)
            return attend(2 * i + 1, 0)

        lax.fori_loop(0, blocks // 2, two, 0)
        attended = att_t[...]
        att[at, :] = attended
        after = start + mm(attended, w_out[...])
        for c in range(4):
            cs = slice(c * 512, c * 512 + 512)
            a, s = gelu_pair(mm(hidden, w_up[:, cs]))
            a = a.astype(BF16)
            act[at, cs] = a
            slope[:, cs] = s.astype(BF16)
            after = after + mm(a, w_down[cs, :])
        scaled_f, factor_f = norm(after)
        final = (scaled_f * g_gain_final).astype(BF16)
        fin[at, :] = final
        logits = mm(final, w_head[...])
        hot = one_hot(own_ids[at, :])
        top = jnp.max(logits, axis=-1, keepdims=True)
        log_total = top + jnp.log(jnp.sum(jnp.exp(logits - top), axis=-1, keepdims=True))
        loss = loss + jnp.sum(
            weighting[:, :1] * (log_total - jnp.sum(logits * hot, axis=-1, keepdims=True)), axis=0, keepdims=True
        )
        lg = ((jnp.exp(logits - log_total) - hot) * jnp.concatenate([weighting, weighting], axis=1)).astype(BF16)
        lgrad[at, :] = lg
        fg = mm_nt(lg, w_head[...])
        gf = gf + jnp.sum(fg * scaled_f, axis=0, keepdims=True)
        inner = fg * g_gain_final
        after_grad = factor_f * (inner - scaled_f * jnp.mean(inner * scaled_f, axis=-1, keepdims=True))
        bg = after_grad.astype(BF16)
        bgrad[at, :] = bg
        attg[...] = mm_nt(bg, w_out[...]).astype(BF16)
        hg = None
        for c in range(4):
            cs = slice(c * 512, c * 512 + 512)
            eg = (slope[:, cs] * mm_nt(bg, w_down[cs, :])).astype(BF16)
            egrad[at, cs] = eg
            term = mm_nt(eg, w_up[:, cs])
            hg = term if hg is None else hg + term

        def attend_back(b, _):
            ra = pl.ds(b * 128 if isinstance(b, int) else pl.multiple_of(b * 128, 128), 128)
            for pair in range(4):
                cs = slice(pair * 128, pair * 128 + 128)
                qs = stack(proj[ra, cs] * jnp.asarray(0.125, BF16))
                kp = proj[ra, LD + pair * 128 : LD + pair * 128 + 128]
                vp = proj[ra, 2 * LD + pair * 128 : 2 * LD + pair * 128 + 128]
                das = stack(attg[ra, cs])
                p = probs[b * 4 + pair]
                dp = narrow(mm_nt(vp, das))
                ds = widen(p * (dp - jnp.sum(p * dp, axis=0, keepdims=True)))
                flipped = jnp.transpose(ds.astype(BF16))
                wide = jnp.concatenate([flipped[:128], flipped[128:]], axis=1)
                projg_t[ra, cs] = (mm(wide, stack(kp)) * 0.125).astype(BF16)
                projg_t[ra, LD + pair * 128 : LD + pair * 128 + 128] = mm(ds.astype(BF16), qs).astype(BF16)
                projg_t[ra, 2 * LD + pair * 128 : 2 * LD + pair * 128 + 128] = mm(widen(p).astype(BF16), das).astype(BF16)
            return 0

        for b in range(blocks):
            attend_back(b, 0)
        for c in range(3):
            own = projg_t[:, c * LD : (c + 1) * LD]
            projg[at, c * LD : (c + 1) * LD] = own
            hg = hg + mm_nt(own, w_in[:, c * LD : (c + 1) * LD])
        start = startv[...]
        scaled, factor = norm(start)
        gl = gl + jnp.sum(hg * scaled, axis=0, keepdims=True)
        inner = hg * g_gain_local
        sg = (after_grad + factor * (inner - scaled * jnp.mean(inner * scaled, axis=-1, keepdims=True))).astype(BF16)
        sgrad[at, :] = sg
        wide_rows[at, :] = mm_nt(sg, w_bridge[...])
        return loss, gl, gf

    init = (jnp.zeros((1, 1), F32), jnp.zeros((1, LD), F32), jnp.zeros((1, LD), F32))
    loss, gl, gf = lax.fori_loop(0, steps, step, init)

    for j in range(SLOTS):
        inputg_ref[:, j * GSLOT : (j + 1) * GSLOT] = wide_rows[pl.ds(j, patches, stride=SLOTS), :].astype(BF16)

    def put(ref, index, value, which):
        if base is not None:
            value = value + base[which][index].astype(F32)
        ref[index] = value.astype(ref.dtype)

    every = slice(None)
    if base is not None:
        loss = loss + base[8][...]
        gl = gl + base[7][0:1, :]
        gf = gf + base[7][1:2, :]
    loss_ref[...] = loss
    g_gain[0:1, :] = gl
    g_gain[1:2, :] = gf
    hidden_t = jnp.transpose(hid[...])
    for c in range(3):
        cs = slice(c * 512, c * 512 + 512)
        put(g_in, (every, cs), mm(hidden_t, projg[:, cs]), 0)
    for c in range(4):
        cs = slice(c * 512, c * 512 + 512)
        put(g_up, (every, cs), mm(hidden_t, egrad[:, cs]), 1)
    put(g_out, (every, every), mm_tn(att[...], bgrad[...]), 2)
    for c in range(4):
        cs = slice(c * 512, c * 512 + 512)
        put(g_down, (cs, every), mm_tn(act[:, cs], bgrad[...]), 3)
    put(g_head, (every, every), mm_tn(fin[...], lgrad[...]), 4)
    lookup_all = one_hot(prev_ids[...]).astype(BF16)
    put(g_embed, (every, every), mm_tn(lookup_all, sgrad[...]), 5)
    put(g_bridge, (every, every), mm_tn(inputs_ref[...], sgrad[...]), 6)


def byte_layer(start, own, pieces, ids, mask, micro, forward, slot_rows, count, weights, gains, base=None, tile=512):
    rows = start.shape[0] * SLOTS
    shapes = [(LD, 3 * LD), (LD, LFF), (LD, LD), (LFF, LD), (LD, VOCAB), (VOCAB, LD), (GSLOT, LD)]
    out_shape = [jax.ShapeDtypeStruct(s, BF16) for s in shapes] + [
        jax.ShapeDtypeStruct((2, LD), F32), jax.ShapeDtypeStruct((1, 1), F32),
        jax.ShapeDtypeStruct(start.shape, BF16)]
    args = [start, own, *pieces, ids, mask, count, *weights, gains] + (list(base) if base is not None else [])
    vm = pl.BlockSpec(memory_space=pltpu.VMEM)
    in_specs = [vm] * len(args)
    in_specs[4 + len(pieces)] = pl.BlockSpec(memory_space=pltpu.SMEM)
    return pl.pallas_call(
        functools.partial(byte_kernel, rows, tile, base is not None, len(pieces), micro, forward, slot_rows),
        out_shape=out_shape,
        in_specs=in_specs,
        out_specs=[vm] * len(out_shape),
        cost_estimate=pl.CostEstimate(flops=43 * 10**9, bytes_accessed=150 * 10**6, transcendentals=10**6),
        scratch_shapes=[
            pltpu.VMEM((rows, LD), BF16),
            pltpu.VMEM((tile, 3 * LD), BF16),
            pltpu.VMEM((tile // 128 * 4, SLOTS, 256), F32),
            pltpu.VMEM((rows, LD), BF16),
            pltpu.VMEM((rows, LFF), BF16),
            pltpu.VMEM((tile, LFF), BF16),
            pltpu.VMEM((rows, LD), BF16),
            pltpu.VMEM((rows, VOCAB), BF16),
            pltpu.VMEM((rows, LD), BF16),
            pltpu.VMEM((rows, LFF), BF16),
            pltpu.VMEM((tile, LD), BF16),
            pltpu.VMEM((rows, 3 * LD), BF16),
            pltpu.VMEM((rows, LD), BF16),
            pltpu.VMEM((tile, LD), F32),
            pltpu.VMEM((tile, LD), BF16),
            pltpu.VMEM((tile, 3 * LD), BF16),
            pltpu.VMEM((rows, GSLOT), F32),
            pltpu.VMEM((rows, GSLOT), F32),
            pltpu.VMEM((rows, GSLOT), F32),
            pltpu.VMEM((rows, GSLOT), F32),
            pltpu.VMEM((rows, GSLOT), BF16),
        ],
        compiler_params=pltpu.CompilerParams(vmem_limit_bytes=61 * 2**20),
        name="byte_layer",
    )(*args)


def other(index, offset, size):
    return index ^ offset if size & (size - 1) == 0 else lax.rem(index + offset, size)


def origin(index, offset, size):
    return index ^ offset if size & (size - 1) == 0 else lax.rem(index + size - offset, size)


def place_of(ref, by_column, extent, index):
    at = pl.ds(pl.multiple_of(index * extent, extent), extent)
    return ref.at[:, at] if by_column else ref.at[at, :]


def remote(src, dst, send, recv, device):
    return pltpu.make_async_remote_copy(
        src_ref=src, dst_ref=dst, send_sem=send, recv_sem=recv, device_id=device, device_id_type=MESH
    )


def greet(devices):
    barrier = pltpu.get_barrier_semaphore()
    for device in devices:
        pl.semaphore_signal(barrier, inc=1, device_id=device, device_id_type=MESH)
    pl.semaphore_wait(barrier, len(devices))


def group_peers(slots, groups):
    s, m, d = lax.axis_index(SLOT), lax.axis_index(STACK), lax.axis_index(CORE)
    across = [(other(s, j, slots), m, d) for j in range(1, slots)]
    beside = [(s, m, other(d, k, groups)) for k in range(1, groups)]
    return across, beside


def stack_peers(stacks):
    s, m, d = lax.axis_index(SLOT), lax.axis_index(STACK), lax.axis_index(CORE)
    return [(s, other(m, j, stacks), d) for j in range(1, stacks)]


def gather_kernel(sizes, columns, forwarded, *refs):
    slots, stacks, groups = sizes
    count = len(columns)
    wide, tail, counted = refs[:count], refs[count], refs[count + 1]
    outs, gain_out, count_out = refs[count + 2 : 2 * count + 2], refs[2 * count + 2], refs[2 * count + 3]
    shards, rest = refs[2 * count + 4 : 3 * count + 4], refs[3 * count + 4 :]
    (tail_z, tail_s, tail_d, held_count, own_sem, xs, xr, cs, cr, zs, zr, ts, tr, ds, dr, ns, nr) = rest
    s, m, d = lax.axis_index(SLOT), lax.axis_index(STACK), lax.axis_index(CORE)
    across, beside = group_peers(slots, groups)
    above = stack_peers(stacks)
    for w in range(count):
        if len(wide[w].shape) == 3:
            breadth = wide[w].shape[2]
            for i in range(wide[w].shape[0]):
                shards[w][:, i * breadth : (i + 1) * breadth] = wide[w][i].astype(BF16)
        else:
            shards[w][...] = wide[w][...].astype(BF16)
    tail_z[m] = tail[...].astype(BF16)
    held_count[d] = counted[...]
    greet(across + beside + above)

    def place(w, slot, group, half=None):
        rows, breadth = shards[w].shape
        index = slot * groups + group
        if half is None:
            return place_of(outs[w], columns[w], breadth if columns[w] else rows, index)
        size = rows // 2
        if columns[w]:
            return outs[w].at[pl.ds(half * size, size), pl.ds(pl.multiple_of(index * breadth, breadth), breadth)]
        return outs[w].at[pl.ds(pl.multiple_of(index * rows + half * size, size), size), :]

    tail_copies = [remote(tail_z.at[m], tail_z.at[m], zs.at[j], zr.at[j], above[j - 1]) for j in range(1, stacks)]
    tail_copies += [
        remote(held_count.at[d], held_count.at[d], ns.at[k], nr.at[k], beside[k - 1]) for k in range(1, groups)
    ]
    for copy in tail_copies:
        copy.start()
    sends, pending = [], []
    direct = (1, 2) if forwarded else tuple(range(1, slots))
    for w in range(count):
        for j in direct:
            copy = remote(shards[w], place(w, s, d), xs.at[w, j], xr.at[w, j], across[j - 1])
            copy.start()
            sends.append(copy)
    for w in range(count):
        for k in range(1, groups):
            copy = remote(shards[w], place(w, s, d), cs.at[w, 0, k], cr.at[w, 0, k], beside[k - 1])
            copy.start()
            pending.append(copy)
        copy = pltpu.make_async_copy(shards[w], place(w, s, d), own_sem.at[w])
        copy.start()
        pending.append(copy)

    for copy in tail_copies:
        copy.wait()
    total = held_count[0]
    for k in range(1, groups):
        total = total + held_count[k]
    count_out[...] = total
    tail_s[s] = tail_z[stacks - 1]
    step = [remote(tail_s.at[s], tail_s.at[s], ts.at[j], tr.at[j], across[j - 1]) for j in range(1, slots)]
    for copy in step:
        copy.start()
    for copy in step:
        copy.wait()
    tail_d[d] = tail_s[slots - 1]
    step = [remote(tail_d.at[d], tail_d.at[d], ds.at[k], dr.at[k], beside[k - 1]) for k in range(1, groups)]
    for copy in step:
        copy.start()
    for copy in step:
        copy.wait()
    gain_out[...] = tail_d[groups - 1].astype(F32)

    def spread(w, j, slot):
        here = place(w, slot, d)
        for k in range(1, groups):
            copy = remote(here, here, cs.at[w, j, k], cr.at[w, j, k], beside[k - 1])
            copy.start()
            pending.append(copy)

    for w in range(count):
        for j in direct:
            slot = origin(s, j, slots)
            here = place(w, slot, d)
            remote(here, here, xs.at[w, j], xr.at[w, j], across[j - 1]).wait_recv()
            if forwarded:
                half = 0 if j == 1 else 1
                part, index = place(w, slot, d, half), 3 if j == 1 else 0
                copy = remote(part, part, xs.at[w, index], xr.at[w, index], across[2 - j])
                copy.start()
                sends.append(copy)
            spread(w, j, slot)
    if forwarded:
        for w in range(count):
            slot = s ^ 3
            for half, index in ((0, 3), (1, 0)):
                part = place(w, slot, d, half)
                remote(part, part, xs.at[w, index], xr.at[w, index], across[1 - half]).wait_recv()
            spread(w, 3, slot)
    for copy in sends:
        copy.wait_send()
    for copy in pending:
        copy.wait()


def gather_weights(shards, columns, tail, counted):
    sizes = tuple(lax.axis_size(axis) for axis in (SLOT, STACK, CORE))
    slots, stacks, groups = sizes
    count = len(shards)
    parts = slots * groups
    flats = [(v.shape[1], v.shape[0] * v.shape[2]) if v.ndim == 3 else v.shape for v in shards]
    shapes = [
        (v[0], v[1] * parts) if c else (v[0] * parts, v[1]) for v, c in zip(flats, columns)
    ]
    forwarded = slots == 4 and all(v[0] % 32 == 0 for v in flats)
    anywhere = pl.BlockSpec(memory_space=pl.ANY)
    vm = pl.BlockSpec(memory_space=pltpu.VMEM)
    dma = pltpu.SemaphoreType.DMA
    return pl.pallas_call(
        functools.partial(gather_kernel, sizes, columns, forwarded),
        out_shape=[jax.ShapeDtypeStruct(shape, BF16) for shape in shapes]
        + [jax.ShapeDtypeStruct(tail.shape, F32), jax.ShapeDtypeStruct(counted.shape, F32)],
        in_specs=[vm] * (count + 2),
        out_specs=[anywhere] * count + [vm] * 2,
        scratch_shapes=[pltpu.VMEM(v, BF16) for v in flats]
        + [
            pltpu.VMEM((stacks,) + tail.shape, BF16),
            pltpu.VMEM((slots,) + tail.shape, BF16),
            pltpu.VMEM((groups,) + tail.shape, BF16),
            pltpu.VMEM((groups,) + counted.shape, F32),
            dma((count,)),
            dma((count, slots)), dma((count, slots)),
            dma((count, slots, groups)), dma((count, slots, groups)),
            dma((stacks,)), dma((stacks,)),
            dma((slots,)), dma((slots,)),
            dma((groups,)), dma((groups,)),
            dma((groups,)), dma((groups,)),
        ],
        compiler_params=pltpu.CompilerParams(
            collective_id=1, has_side_effects=True, vmem_limit_bytes=24 * 2**20
        ),
        cost_estimate=pl.CostEstimate(flops=10**6, bytes_accessed=120 * 10**6, transcendentals=0),
        name="gather_weights",
    )(*shards, tail, counted)


def scatter_kernel(sizes, columns, extents, shared, *refs):
    slots, stacks, groups = sizes
    count = len(columns)
    partials, outs = refs[:count], refs[count : 2 * count]
    rest = refs[2 * count :]
    from_core, stage, from_slot = rest[:count], rest[count : 2 * count], rest[2 * count : 3 * count]
    cs, cr, xs, xr = rest[3 * count : 3 * count + 4]
    if shared:
        from_z, own_c, from_c, zs, zr, ts, tr = rest[3 * count + 4 :]
    s, m, d = lax.axis_index(SLOT), lax.axis_index(STACK), lax.axis_index(CORE)
    across, beside = group_peers(slots, groups)
    above = stack_peers(stacks)
    greet(across + beside + above if shared else across + beside)
    order = tuple(range(count))

    def part(w, slot, group):
        return place_of(partials[w], columns[w], extents[w], slot * groups + group)

    first = {}
    for w in order:
        for j in tuple(range(1, slots)) + (0,):
            t = other(s, j, slots)
            for k in range(1, groups):
                copy = remote(
                    part(w, t, other(d, k, groups)), from_core[w].at[j, k - 1],
                    cs.at[w, j, k], cr.at[w, j, k], beside[k - 1],
                )
                copy.start()
                first[w, j, k] = copy
    second = {}
    for w in order:
        for j in tuple(range(1, slots)) + (0,):
            t = other(s, j, slots)
            for k in range(1, groups):
                first[w, j, k].wait_recv()
            total = part(w, t, d)[...].astype(F32)
            for k in range(1, groups):
                total = total + from_core[w][j, k - 1].astype(F32)
            if j:
                stage[w][j] = total.astype(BF16)
                copy = remote(stage[w].at[j], from_slot[w].at[j], xs.at[w, j], xr.at[w, j], across[j - 1])
                copy.start()
                second[w, j] = copy
            else:
                outs[w][: total.shape[0]] = total
    for w in order:
        for j in range(1, slots):
            second[w, j].wait_recv()
        total = outs[w][: from_slot[w].shape[1]]
        for j in range(1, slots):
            total = total + from_slot[w][j].astype(F32)
        outs[w][: total.shape[0]] = total
        if shared:
            from_z[m] = total.astype(BF16)
            third = [
                remote(from_z.at[m], from_z.at[m], zs.at[j], zr.at[j], above[j - 1])
                for j in range(1, stacks)
            ]
            for copy in third:
                copy.start()
    if shared:
        w = 0
        size = from_slot[w].shape[1]
        for copy in third:
            copy.wait()
        total = from_z[0].astype(F32)
        for j in range(1, stacks):
            total = total + from_z[j].astype(F32)
        own_c[...] = total.astype(BF16)
        fourth = [remote(own_c, from_c.at[k], ts.at[k], tr.at[k], beside[k - 1]) for k in range(1, groups)]
        for copy in fourth:
            copy.start()
        outs[w][pl.ds(pl.multiple_of(d * size, size), size), :] = own_c[...].astype(F32)
        for k in range(1, groups):
            fourth[k - 1].wait()
            outs[w][pl.ds(pl.multiple_of(origin(d, k, groups) * size, size), size), :] = from_c[k].astype(F32)
    for copy in first.values():
        copy.wait_send()
    for copy in second.values():
        copy.wait_send()


def scatter_grads(partials, columns, shared=False):
    sizes = tuple(lax.axis_size(axis) for axis in (SLOT, STACK, CORE))
    slots, stacks, groups = sizes
    count = len(partials)
    parts = slots * groups
    blocks = [
        (v.shape[0], v.shape[1] // parts) if c else (v.shape[0] // parts, v.shape[1])
        for v, c in zip(partials, columns)
    ]
    extents = tuple(b[1] if c else b[0] for b, c in zip(blocks, columns))
    shapes = [(b[0] * groups, b[1]) for b in blocks] if shared else blocks
    vm = pl.BlockSpec(memory_space=pltpu.VMEM)
    dma = pltpu.SemaphoreType.DMA
    last = blocks[-1]
    return pl.pallas_call(
        functools.partial(scatter_kernel, sizes, columns, extents, shared),
        out_shape=[jax.ShapeDtypeStruct(shape, F32) for shape in shapes],
        in_specs=[vm] * count,
        out_specs=[vm] * count,
        scratch_shapes=[pltpu.VMEM((slots, groups - 1) + b, BF16) for b in blocks]
        + [pltpu.VMEM((slots,) + b, BF16) for b in blocks]
        + [pltpu.VMEM((slots,) + b, BF16) for b in blocks]
        + [dma((count, slots, groups))] * 2
        + [dma((count, slots))] * 2
        + (
            [
                pltpu.VMEM((stacks,) + last, BF16),
                pltpu.VMEM(last, BF16), pltpu.VMEM((groups,) + last, BF16),
                dma((stacks,)), dma((stacks,)), dma((groups,)), dma((groups,)),
            ]
            if shared
            else []
        ),
        compiler_params=pltpu.CompilerParams(
            collective_id=4 if shared else 2, has_side_effects=True, vmem_limit_bytes=48 * 2**20
        ),
        cost_estimate=pl.CostEstimate(
            flops=10**6, bytes_accessed=(10 if shared else 120) * 10**6, transcendentals=0
        ),
        name="scatter_small" if shared else "scatter_grads",
    )(*partials)


def total_kernel(sizes, value, out, held_z, held_s, held_d, zs, zr, xs, xr, cs, cr):
    slots, stacks, groups = sizes
    across, beside = group_peers(slots, groups)
    above = stack_peers(stacks)
    greet(across + beside + above)
    total = value[...]
    for axis, peers, held, send, recv in (
        (STACK, above, held_z, zs, zr), (SLOT, across, held_s, xs, xr), (CORE, beside, held_d, cs, cr)
    ):
        index = lax.axis_index(axis)
        held[index] = total
        copies = [
            remote(held.at[index], held.at[index], send.at[j], recv.at[j], peer)
            for j, peer in enumerate(peers)
        ]
        for copy in copies:
            copy.start()
        for copy in copies:
            copy.wait()
        total = held[0]
        for j in range(1, len(peers) + 1):
            total = total + held[j]
    out[...] = total


def total_of(value):
    sizes = tuple(lax.axis_size(axis) for axis in (SLOT, STACK, CORE))
    slots, stacks, groups = sizes
    vm = pl.BlockSpec(memory_space=pltpu.VMEM)
    dma = pltpu.SemaphoreType.DMA
    return pl.pallas_call(
        functools.partial(total_kernel, sizes),
        out_shape=jax.ShapeDtypeStruct(value.shape, F32),
        in_specs=[vm],
        out_specs=vm,
        scratch_shapes=[pltpu.VMEM((size,) + value.shape, F32) for size in (stacks, slots, groups)]
        + [dma((size,)) for size in (stacks, stacks, slots, slots, groups, groups)],
        compiler_params=pltpu.CompilerParams(collective_id=3, has_side_effects=True),
        name="total_of",
    )(value)


def pieces_of(size):
    return max(step for step in range(16, 129, 16) if size % step == 0)


def pack_layout():
    layout = []
    offset = 0
    for height, breadth in (
        (LD, 3 * LD), (LD, LFF), (LD, LD), (LFF, LD), (LD, VOCAB), (VOCAB, LD), (GSLOT, LD)
    ):
        layout.append((offset, height, breadth // 128))
        offset += height * breadth // 128
    return layout, offset


def unpack_kernel(share, rows, count, blocks_ref, *refs):
    outs, flat = refs[:-1], refs[-1]
    chunk = pieces_of(rows)
    flat[0:8, :] = jnp.zeros((8, 128), F32)

    def block(b, _):
        top = lax.div(b * share, 128)
        held = flat[pl.ds(top, 1), :]
        for i in range(0, rows, chunk):
            source = pl.ds(pl.multiple_of(b * rows, 16) + i, chunk)
            flat[pl.ds(top + i, chunk), :] = blocks_ref[source, :].astype(F32)
        flat[pl.ds(top, 1), :] = flat[pl.ds(top, 1), :] + held
        return 0

    lax.fori_loop(0, count, block, 0)
    layout, _ = pack_layout()
    for out, (offset, height, breadth) in zip(outs, layout):
        def part(i, _, out=out, offset=offset, breadth=breadth):
            for c in range(breadth):
                values = flat[pl.ds(offset + i * (128 * breadth) + c, 128, stride=breadth), :]
                out[pl.ds(pl.multiple_of(i * 128, 128), 128), c * 128 : (c + 1) * 128] = values.astype(BF16)
            return 0
        lax.fori_loop(0, height // 128, part, 0)


def unpack(blocks, share):
    rows = block_rows(share)
    count = blocks.shape[0] // rows
    layout, used = pack_layout()
    vm = pl.BlockSpec(memory_space=pltpu.VMEM)
    return pl.pallas_call(
        functools.partial(unpack_kernel, share, rows, count),
        out_shape=[jax.ShapeDtypeStruct((h, b * 128), BF16) for _, h, b in layout],
        in_specs=[vm],
        out_specs=[vm] * len(layout),
        scratch_shapes=[pltpu.VMEM((share * count // 128 + rows + 8, 128), F32)],
        compiler_params=pltpu.CompilerParams(vmem_limit_bytes=48 * 2**20),
        name="unpack",
    )(blocks)


def pack_kernel(share, rows, count, *refs):
    matrices, out, flat = refs[:-2], refs[-2], refs[-1]
    chunk = pieces_of(rows)
    layout, used = pack_layout()
    for matrix, (offset, height, breadth) in zip(matrices, layout):
        def part(i, _, matrix=matrix, offset=offset, breadth=breadth):
            for c in range(breadth):
                values = matrix[pl.ds(pl.multiple_of(i * 128, 128), 128), c * 128 : (c + 1) * 128]
                flat[pl.ds(offset + i * (128 * breadth) + c, 128, stride=breadth), :] = values.astype(F32)
            return 0
        lax.fori_loop(0, height // 128, part, 0)
    spare = flat.shape[0] - used
    flat[used:, :] = jnp.zeros((spare, 128), F32)

    def block(b, _):
        top = lax.div(b * share, 128)
        for i in range(0, rows, chunk):
            target = pl.ds(pl.multiple_of(b * rows, 16) + i, chunk)
            out[target, :] = flat[pl.ds(top + i, chunk), :].astype(BF16)
        return 0

    lax.fori_loop(0, count, block, 0)


def pack(matrices, share):
    rows = block_rows(share)
    layout, used = pack_layout()
    total = used + (D + 2 * LD) // 128
    count = total * 128 // share
    vm = pl.BlockSpec(memory_space=pltpu.VMEM)
    return pl.pallas_call(
        functools.partial(pack_kernel, share, rows, count),
        out_shape=jax.ShapeDtypeStruct((count * rows, 128), BF16),
        in_specs=[vm] * len(layout),
        out_specs=vm,
        scratch_shapes=[pltpu.VMEM((total + rows + 8, 128), F32)],
        compiler_params=pltpu.CompilerParams(vmem_limit_bytes=48 * 2**20),
        name="pack",
    )(*matrices)


def partner(index, offset, size):
    return index ^ offset if size & (size - 1) == 0 else (index + offset) % size


def swap(value, axis, offset):
    size = lax.axis_size(axis)
    if size & (size - 1) == 0:
        pairs = [(i, i ^ offset) for i in range(size)]
    else:
        pairs = [(i, (i + offset) % size) for i in range(size)]
    return lax.ppermute(value, axis, pairs)


def source(index, offset, size):
    return index ^ offset if size & (size - 1) == 0 else (index + size - offset) % size


def trade_rows(partial, axis):
    size = lax.axis_size(axis)
    index = lax.axis_index(axis)
    share = partial.shape[0] // size
    pieces = []
    for offset in range(1, size):
        block = lax.dynamic_slice_in_dim(partial, partner(index, offset, size) * share, share, 0)
        pieces.append(swap(block.astype(BF16), axis, offset))
    return lax.dynamic_slice_in_dim(partial, index * share, share, 0), pieces


def share_rows(block, axis):
    return [block] + [swap(block, axis, offset) for offset in range(1, lax.axis_size(axis))]


def shift_chunks(value, distance, forward):
    size = lax.axis_size(SLOT)
    if forward:
        pairs = [(i, i + distance) for i in range(size - distance)]
    else:
        pairs = [(i + distance, i) for i in range(size - distance)]
    return lax.ppermute(value, SLOT, pairs)


def update(weight, moment, average, gradient, factor, rate):
    step_grad = factor * gradient
    moment_next = momentum_keep * moment + step_grad
    weight_next = weight - rate * (step_grad + momentum_keep * moment_next)
    average_next = average_keep * average + (1.0 - average_keep) * weight_next
    return (weight_next, moment_next, average_next)


def block_rows(share):
    return -(-(-(-share // 128) + 1) // 16) * 16


def gather_pack(local_pack):
    share = local_pack.shape[0]
    index = lax.axis_index((SLOT, STACK, CORE))
    offset = lax.rem(index * share, 128)
    rows = block_rows(share)
    block = lax.dynamic_update_slice_in_dim(
        jnp.zeros((rows * 128,), BF16), local_pack.astype(BF16), offset, 0
    )
    return lax.all_gather(block.reshape(rows, 128), (SLOT, STACK, CORE), axis=0, tiled=True)


def local(
    byte_ids, item_ids, loss_mask,
    attend_in, expand_in, attend_out, expand_out, slot_table, local_pack,
    moment_attend_in, moment_expand_in, moment_attend_out, moment_expand_out,
    moment_slot_table, moment_local_pack,
    average_attend_in, average_expand_in, average_attend_out, average_expand_out,
    average_slot_table, average_local_pack,
):
    slot_size, mp_size = lax.axis_size(SLOT), lax.axis_size(STACK)
    slot_index, mp_index, dp_index = (
        lax.axis_index(SLOT), lax.axis_index(STACK), lax.axis_index(CORE),
    )
    counted = jnp.full((8, 128), jnp.sum(loss_mask.astype(F32)))
    width = attend_in.shape[2]
    piece = slot_table.shape[0] * VOCAB // lax.axis_size(CORE)
    table_shard = lax.dynamic_slice_in_dim(
        slot_table.reshape(-1, GSLOT), dp_index * piece, piece, 0
    )
    tail = local_pack[-(D + 2 * LD) :].reshape(-1, 128)
    shards = [table_shard, jnp.transpose(attend_in, (1, 0, 2)), expand_in]
    late = [attend_out, expand_out]
    wide = attend_out.shape[1] % 128 == 0
    if wide:
        table, full_in_flat, full_expand, full_out, full_shrink, gains, counted = gather_weights(
            shards + late, (False, False, False, True, True), tail, counted
        )
    else:
        table, full_in_flat, full_expand, gains, counted = gather_weights(
            shards, (False, False, False), tail, counted
        )
        full_out, full_shrink = (
            lax.all_gather(v.astype(BF16), (SLOT, CORE), axis=1, tiled=True) for v in late
        )
    pack_whole = gather_pack(local_pack)
    gains = gains.reshape(-1)
    mask_count = counted[0, 0]
    gain_global = gains[:D]
    local_gains = gains[D:].reshape(2, LD)
    unpacked = unpack(pack_whole, local_pack.shape[0])
    group_rows = byte_ids.shape[1]
    rows = group_rows // slot_size
    local_rows = rows // mp_size
    vocab_ids = jnp.arange(VOCAB)
    reach = min(slot_size - 1, -(-(longest_item - 1) // rows))
    ids_t, mask_t = jnp.transpose(byte_ids, (0, 2, 1)), jnp.transpose(loss_mask, (0, 2, 1))
    micros = []
    for micro in range(byte_ids.shape[0]):
        forward = micro % 2 == 0
        start_rows, hidden, projected, own_kv, own_previous = embed_rows(
            ids_t, item_ids, micro, forward, rows, table, full_in_flat, gain_global[None]
        )
        earlier = [shift_chunks(own_kv, d, forward) for d in range(1, reach + 1)]
        micros.append(types.SimpleNamespace(
            forward=forward, micro=micro, start_rows=start_rows, hidden=hidden, projected=projected,
            earlier=earlier, own_previous=own_previous,
        ))
    for m, pair in zip(micros, up_rows([m.hidden for m in micros], full_expand)):
        m.active, m.slope = pair
    for m in micros:
        m.attended, m.lse = attention_fwd(
            item_ids, m.micro, m.forward, m.projected, m.earlier
        )
        m.own, m.pieces = trade_rows(
            product(m.attended, full_out) + product(m.active, full_shrink), STACK
        )
        m.own_start = lax.dynamic_slice_in_dim(
            m.start_rows, mp_index * local_rows, local_rows, 0
        )
    base = None
    for m in micros:
        out = byte_layer(
            m.own_start, m.own, m.pieces, ids_t, mask_t, m.micro, m.forward, rows,
            mask_count.reshape(1, 1), unpacked[:7], local_gains, base,
        )
        base = out[:9]
        m.own_back = out[9]
        m.branch_pieces = share_rows(out[9], STACK)
    matrices, local_gain_grads, loss_sum = base[:7], base[7], base[8][0, 0]
    local_blocks = pack(matrices, local_pack.shape[0])
    sums = None
    table_grad = None
    gain_global_grad = None
    for m in micros:
        branch_grad, m.query_grad, m.kv_grads = attention_bwd(
            item_ids, m.micro, m.forward, m.projected, m.earlier, m.attended, m.lse,
            full_out, m.branch_pieces,
        )
        m.branch_grad = branch_grad
        m.returned = [
            shift_chunks(m.kv_grads[d], d, not m.forward) for d in range(1, reach + 1)
        ]
        m.expanded_grad = (
            m.slope.astype(F32) * back_product(branch_grad, full_shrink)
        ).astype(BF16)
    for m in micros:
        kv_total = m.kv_grads[0].astype(F32)
        for value in m.returned:
            kv_total = kv_total + value.astype(F32)
        m.projected_grad = jnp.concatenate([m.query_grad, kv_total.astype(BF16)], axis=1)
        m.partial = back_product(m.projected_grad, full_in_flat) + back_product(
            m.expanded_grad, full_expand
        )
        m.back = trade_rows(m.partial, STACK)
    sums = None
    for m in micros:
        terms = (
            gram_product(m.hidden, m.projected_grad),
            gram_product(m.hidden, m.expanded_grad),
            gram_product(m.attended, m.branch_grad),
            gram_product(m.active, m.branch_grad),
        )
        sums = terms if sums is None else tuple(a + b for a, b in zip(sums, terms))
    sums = tuple(s.astype(BF16) for s in sums)
    if wide:
        sums, _ = lax.optimization_barrier((sums, [m.back[0] for m in micros]))
        own_in, own_expand, own_out, own_shrink = scatter_grads(sums, (False, False, True, True))
    else:
        own_in, own_expand = scatter_grads(sums[:2], (False, False))
        own_out, own_shrink = (
            lax.psum_scatter(v, (SLOT, CORE), scatter_dimension=1, tiled=True).astype(F32)
            for v in sums[2:]
        )
    begun, own_in = lax.optimization_barrier(([m.own_start for m in micros], own_in))
    norms = [norm_forward(v.astype(F32), gain_global) for v in begun]
    backs, own_in = lax.optimization_barrier(([m.back for m in micros], own_in))
    table_grad = None
    for m, (hidden_grad, pieces), (_, scaled, factor) in zip(micros, backs, norms):
        for value in pieces:
            hidden_grad = hidden_grad + value.astype(F32)
        gain_term = jnp.sum(hidden_grad * scaled, axis=0)
        start_grad = (
            m.own_back.astype(F32) + norm_backward(scaled, factor, gain_global, hidden_grad)
        ).astype(BF16)
        own_lookup = lax.dynamic_slice_in_dim(m.own_previous, mp_index * local_rows, local_rows, 0)
        own_lookup = (own_lookup[:, :, None] == vocab_ids).astype(BF16)
        table_term = jnp.einsum(
            "pjv,pjg->jvg", own_lookup, start_grad.reshape(local_rows, SLOTS, GSLOT),
            preferred_element_type=F32,
        )
        if table_grad is None:
            table_grad, gain_global_grad = table_term, gain_term
        else:
            table_grad = table_grad + table_term
            gain_global_grad = gain_global_grad + gain_term
    gain_grads = jnp.concatenate([gain_global_grad, local_gain_grads.reshape(-1)])
    parts = slot_size * lax.axis_size(CORE)
    small = jnp.concatenate(
        [
            table_grad.astype(BF16).reshape(parts, -1, GSLOT),
            jnp.broadcast_to(gain_grads.astype(BF16).reshape(1, -1, GSLOT), (parts, 16, GSLOT)),
        ],
        axis=1,
    ).reshape(-1, GSLOT)
    squares = jnp.float32(0.0)
    for gradient in (own_in, own_expand, own_out, own_shrink):
        squares = squares + jnp.sum(gradient * gradient)
    small, squares = lax.optimization_barrier((small, squares))
    own_small = scatter_grads([small], (False,), True)[0]
    own_small = own_small.reshape(lax.axis_size(CORE), piece + 16, GSLOT)
    own_table = own_small[:, :piece].reshape(slot_table.shape)
    gain_total = own_small[0, piece:].reshape(-1)
    last = (slot_index == slot_size - 1) & (mp_index == mp_size - 1)
    last = last & (dp_index == lax.axis_size(CORE) - 1)
    owner = ((mp_index == 0) & (dp_index == 0)).astype(F32)
    squares = squares + owner * jnp.sum(own_table * own_table)
    squares = squares + jnp.where(last, jnp.sum(gain_total * gain_total), 0.0)
    own_in = jnp.stack([own_in[:, i * width : (i + 1) * width] for i in range(3)])
    own_block = lax.psum_scatter(local_blocks, (SLOT, STACK, CORE), scatter_dimension=0, tiled=True)
    pack_share, tail_size = local_pack.shape[0], D + 2 * LD
    offset = lax.rem(lax.axis_index((SLOT, STACK, CORE)) * pack_share, 128)
    index = jnp.arange(own_block.shape[0])[:, None] * 128 + jnp.arange(128)[None, :] - offset
    inside = (index >= 0) & (index < jnp.where(last, pack_share - tail_size, pack_share))
    squares = squares + jnp.sum(jnp.where(inside, own_block.astype(F32) ** 2, 0.0))
    own_pack = lax.dynamic_slice_in_dim(own_block.reshape(-1), offset, pack_share, 0).astype(F32)
    own_pack = jnp.concatenate(
        [own_pack[:-tail_size], jnp.where(last, gain_total, own_pack[-tail_size:])]
    )
    both = total_of(jnp.stack([jnp.full((8, 128), squares), jnp.full((8, 128), loss_sum)]))
    total_squares, loss_value = both[0, 0, 0], both[1, 0, 0]
    clip_norm = jnp.sqrt(total_squares)
    factor = clip_max / jnp.maximum(clip_norm, clip_max)
    results = [loss_value * mask_count, mask_count, clip_norm]
    for weight, moment, average, gradient, rate in (
        (attend_in, moment_attend_in, average_attend_in, own_in, rate_dense),
        (expand_in, moment_expand_in, average_expand_in, own_expand, rate_dense),
        (attend_out, moment_attend_out, average_attend_out, own_out, rate_project),
        (expand_out, moment_expand_out, average_expand_out, own_shrink, rate_dense),
        (slot_table, moment_slot_table, average_slot_table, own_table, rate_table),
        (local_pack, moment_local_pack, average_local_pack, own_pack, rate_dense),
    ):
        if gradient is own_in:
            weight, moment, average = (jnp.transpose(v, (1, 0, 2)) for v in (weight, moment, average))
        changed = update(weight, moment, average, gradient, factor, rate)
        if gradient is own_in:
            changed = tuple(jnp.transpose(v, (1, 0, 2)) for v in changed)
        results.extend(changed)
    return tuple(results)


def solution(mesh):
    placed = (
        P(None, CORE, None),
        P(None, CORE, None),
        P(None, CORE, None),
        P((SLOT, CORE), None, STACK),
        P((SLOT, CORE), STACK),
        P(STACK, (SLOT, CORE)),
        P(STACK, (SLOT, CORE)),
        P(SLOT, None, None),
        P((SLOT, STACK, CORE)),
        P((SLOT, CORE), None, STACK),
        P((SLOT, CORE), STACK),
        P(STACK, (SLOT, CORE)),
        P(STACK, (SLOT, CORE)),
        P(SLOT, None, None),
        P((SLOT, STACK, CORE)),
        P((SLOT, CORE), None, STACK),
        P((SLOT, CORE), STACK),
        P(STACK, (SLOT, CORE)),
        P(STACK, (SLOT, CORE)),
        P(SLOT, None, None),
        P((SLOT, STACK, CORE)),
    )
    return jax.shard_map(
        local,
        mesh=mesh,
        in_specs=placed,
        out_specs=(
            P(),
            P(),
            P(),
            P((SLOT, CORE), None, STACK),
            P((SLOT, CORE), None, STACK),
            P((SLOT, CORE), None, STACK),
            P((SLOT, CORE), STACK),
            P((SLOT, CORE), STACK),
            P((SLOT, CORE), STACK),
            P(STACK, (SLOT, CORE)),
            P(STACK, (SLOT, CORE)),
            P(STACK, (SLOT, CORE)),
            P(STACK, (SLOT, CORE)),
            P(STACK, (SLOT, CORE)),
            P(STACK, (SLOT, CORE)),
            P(SLOT, None, None),
            P(SLOT, None, None),
            P(SLOT, None, None),
            P((SLOT, STACK, CORE)),
            P((SLOT, STACK, CORE)),
            P((SLOT, STACK, CORE)),
        ),
        check_vma=False,
    )
```
